32 devices in a mesh: groups: 2 (over x), blk: 16 (over z, y, core).
Axes of the slice: x: 2, y: 2, z: 4, core: 2. Of those that a mesh axis runs over, the one named last changes fastest.
Arguments:
- embeddings: bfloat16 [8192, 768], P(('groups', 'blk')), parts along dimension 0, may hold values from -0.21875 to 0.21875
- pos_ids: int32 [8192, 32], P(('groups', 'blk')), parts along dimension 0, may hold values from 0 to 4095, all different within a row
- pos_count: int32 [8192], P(('groups', 'blk')), parts along dimension 0, may hold values from 1 to 32
- label_slot: int32 [4096], replicated, may hold values from 0 to 4095, each once
- weights: float32 [4096, 768], P('blk'), may hold values from -6 to 6
- first_moment: float32 [4096, 768], P('blk'), may hold values from -6 to 6
- second_moment: float32 [4096, 768], P('blk'), may hold values from 0.5 to 5
Outputs:
- new_weights: float32 [8192, 768], P(('groups', 'blk')), parts along dimension 0
- new_first: float32 [8192, 768], P(('groups', 'blk')), parts along dimension 0
- new_second: float32 [8192, 768], P(('groups', 'blk')), parts along dimension 0
The draws below stay inside these ranges and needn't reach their ends.
There are 2 independent parts, one for each index of `groups`. The reference program is written for one: setup_inputs(seed, part) draws one part's arguments, and reference() takes and returns one part's arrays. A program takes and returns all parts, laid end to end along the dimension named above; an argument that names none is the same for every part. Nothing has to cross between parts.
Inputs may be any that keep to these rules, and one draw needn't show every extreme that they name: `pos_ids`: the 32 ids of one document are distinct. Only the first pos_count entries of a document's list are positives. `label_slot`: a permutation of the label rows.
All inputs are finite; a program needn't handle non-finite values.
Results may differ from the reference program's by a relative error of at most 0.00032.
Values may be sent and summed in bfloat16 or wider, within the bound.
No kernel may reach another device: no remote copies, remote signals or barrier semaphores. Data moves between devices by JAX's collectives and lax.ppermute only.
A program may use at most 128 MiB of HBM per device.

```python
import math
import jax
import jax.numpy as jnp
from jax import lax

D = 768
LISTS = 32
LAB_DEV = 256
LABELS = 4096
DOCS = 4096
N_BLK = 16


def set_ends(entries, rng, least, largest):
    longest = entries.shape.index(max(entries.shape))
    spots = []
    for shift in (0, 1):
        where = [jax.random.randint(jax.random.fold_in(rng, axis), (), 0, length) for axis, length in enumerate(entries.shape)]
        where[longest] = (where[longest] + shift) % entries.shape[longest]
        spots.append(tuple(where))
    return entries.at[spots[0]].set(least).at[spots[1]].set(largest)


def steps_of(own_key, dims, split, least, largest):
    def one(axis_at, parts):
        draws = jax.random.uniform(jax.random.fold_in(jax.random.fold_in(own_key, 6), axis_at), (parts,), jnp.float32, least / len(split), largest / len(split))
        return jnp.repeat(jnp.exp(draws), dims[axis_at] // parts).reshape((-1,) + (1,) * (len(dims) - axis_at - 1))

    factor_of = one(*split[0])
    for cut in split[1:]:
        factor_of = factor_of * one(*cut)
    return factor_of


def different_ones(stream_key, rows, number_of, top, lift):
    sequence = jax.random.permutation(jax.random.fold_in(stream_key, 1), number_of)
    boost = sequence
    for power in range(3):
        boost = boost * boost // number_of
    boost = boost * lift // number_of
    lots = jax.random.randint(jax.random.fold_in(stream_key, 2), (rows, number_of), 0, 4096) + boost
    sure = jax.random.permutation(jax.random.fold_in(stream_key, 3), rows)[jnp.arange(number_of) % rows]
    lots = jnp.where(jnp.arange(rows)[:, None] == sure[None, :], 1 << 14, lots)
    merit = lots * number_of + jnp.arange(number_of)
    return lax.top_k(merit.astype(jnp.int32), top)[1].astype(jnp.int32)


def normal_values(own_key, shape, deviation, reach, cuts=(), kind=jnp.bfloat16):
    drawn = jax.random.normal(own_key, shape, jnp.float32) * deviation
    if len(cuts) > 0:
        drawn = steps_of(own_key, shape, cuts, -0.22, 0.18) * drawn
    return jnp.clip(drawn, min=-reach, max=reach).astype(kind)


def setup_inputs(seed: int = 0, part: int = 0) -> dict:
    key_list = jax.random.split(jax.random.key(seed), 8)
    part_splits = jax.random.split(jax.random.fold_in(key_list[7], part), 8)
    embeddings = normal_values(part_splits[0], (DOCS, D), (D ** -0.5), 0.21875, ((0, 16),))
    pos_ids = different_ones(part_splits[1], DOCS, LABELS, LISTS, 128)
    pos_count = set_ends(jax.random.randint(part_splits[2], (DOCS,), 1, LISTS + 1), jax.random.fold_in(part_splits[2], 1), 1, LISTS).astype(jnp.int32)
    label_slot = jax.random.permutation(key_list[3], LABELS).astype(jnp.int32)
    weights = normal_values(key_list[4], (LABELS, D), 1.0, 6.0, ((0, 16),), jnp.float32)
    first_moment = normal_values(key_list[5], (LABELS, D), 1.0, 6.0, ((0, 16),), jnp.float32)
    second_moment = jnp.clip(jnp.exp(math.log(5.0) - 2.3025851 * jax.random.uniform(key_list[6], (LABELS, D), jnp.float32) ** steps_of(key_list[6], (LABELS, D), ((0, 16),), -0.2, 0.2)), 0.5, 5.0)
    return dict(embeddings=embeddings, pos_ids=pos_ids, pos_count=pos_count, label_slot=label_slot, weights=weights, first_moment=first_moment, second_moment=second_moment)


learn_rate = 0.01
beta_one = 0.9
beta_two = 0.95
adam_eps = 1e-08
decay_rate = 0.1
correct_one = 1.0 - 0.9 ** 10
correct_two = 1.0 - 0.95 ** 10

def block_signal(weight_rows, offset, doc_block, slot_rows, is_live):
    height = weight_rows.shape[0]
    width = doc_block.shape[0]
    logits = lax.dot_general(weight_rows, doc_block, (((1,), (1,)), ((), ())), preferred_element_type=jnp.float32)
    local_row = slot_rows - offset
    inside = is_live & (local_row >= 0) & (local_row < height)
    column = jnp.broadcast_to(jnp.arange(width, dtype=jnp.int32)[:, None], slot_rows.shape)
    target = jnp.zeros((height, width), jnp.float32).at[jnp.where(inside, local_row, height), column].set(1.0, mode='drop')
    return (jax.nn.sigmoid(logits) - target).astype(jnp.bfloat16)

def adam_step(weights, first_moment, second_moment, gradient):
    new_first = beta_one * first_moment + (1.0 - beta_one) * gradient
    new_second = beta_two * second_moment + (1.0 - beta_two) * gradient * gradient
    update = new_first / correct_one / (jnp.sqrt(new_second / correct_two) + adam_eps)
    new_weights = weights - learn_rate * (update + decay_rate * weights)
    return (new_weights, new_first, new_second)

def reference(embeddings, pos_ids, pos_count, label_slot, weights, first_moment, second_moment):
    slot_rows = jnp.take(label_slot, pos_ids, axis=0).astype(jnp.int32)
    is_live = jnp.arange(pos_ids.shape[1], dtype=jnp.int32)[None, :] < pos_count[:, None]
    cast_weights = weights.astype(jnp.bfloat16)

    def one_block(index):
        offset = (index * LAB_DEV).astype(jnp.int32)
        weight_rows = lax.dynamic_slice_in_dim(cast_weights, offset, LAB_DEV, 0)
        signal = block_signal(weight_rows, offset, embeddings, slot_rows, is_live)
        return jnp.dot(signal, embeddings, preferred_element_type=jnp.float32)
    gradient = lax.map(one_block, jnp.arange(N_BLK, dtype=jnp.int32)).reshape(weights.shape)
    new_weights, new_first, new_second = adam_step(weights, first_moment, second_moment, gradient)
    return (new_weights, new_first, new_second)
```

```python
import functools

import jax
import jax.numpy as jnp
from jax import lax
from jax.experimental import pallas as pl
from jax.experimental.pallas import tpu as pltpu
from jax.sharding import PartitionSpec as P

learn_rate = 0.01
beta_one = 0.9
beta_two = 0.95
adam_eps = 1e-08
decay_rate = 0.1
correct_one = 1.0 - 0.9**10
correct_two = 1.0 - 0.95**10

WORD = 32
VMEM_LIMIT = 48 * 1024 * 1024


def lookup_kernel(ids_ref, count_ref, table_ref, rows_ref):
    slots, docs = ids_ref.shape
    table_rows = table_ref.shape[0]
    for start in range(0, docs, 128):
        ids = ids_ref[:, start : start + 128]
        high_part = ids >> 7
        low_part = ids & 127

        def pick(t, found):
            line = jnp.broadcast_to(table_ref[pl.ds(t, 1), :], (slots, 128))
            here = jnp.take_along_axis(line, low_part, axis=1)
            return jnp.where(high_part == t, here, found)

        found = lax.fori_loop(0, table_rows, pick, jnp.full((slots, 128), -1, jnp.int32), unroll=8)
        place = lax.broadcasted_iota(jnp.int32, (slots, 128), 0)
        live = place < count_ref[:, start : start + 128]
        rows_ref[:, start : start + 128] = jnp.where(live, found, -1)


def lookup_rows(label_slot, pos_ids, pos_count):
    docs, slots = pos_ids.shape
    return pl.pallas_call(
        lookup_kernel,
        out_shape=jax.ShapeDtypeStruct((slots, docs), jnp.int32),
        name="lookup",
    )(pos_ids.T, pos_count.reshape(1, docs), label_slot.reshape(-1, 128))


def target_of(rows, base, height):
    slots, docs = rows.shape
    local = rows - base
    word = local >> 5
    bit = jnp.left_shift(jnp.ones_like(local), local & (WORD - 1))
    words = [
        jnp.sum(jnp.where(word == w, bit, 0), axis=0, keepdims=True) for w in range(height // WORD)
    ]
    shift = lax.broadcasted_iota(jnp.int32, (WORD, docs), 0)
    spread = [(jnp.broadcast_to(line, (WORD, docs)) >> shift) & 1 for line in words]
    return jnp.concatenate(spread, axis=0).astype(jnp.float32)


def gradient_kernel(base_ref, mine_ref, other_ref, docs_ref, rows_ref, mine_out, other_out):
    height = mine_ref.shape[0]

    @pl.when(pl.program_id(0) == 0)
    def _():
        mine_out[...] = jnp.zeros_like(mine_out)
        other_out[...] = jnp.zeros_like(other_out)

    docs = docs_ref[...]
    rows = rows_ref[...].astype(jnp.int32)
    for half, (w_ref, out_ref) in enumerate(((mine_ref, mine_out), (other_ref, other_out))):
        logits = lax.dot_general(
            w_ref[...], docs, (((1,), (1,)), ((), ())), preferred_element_type=jnp.float32
        )
        target = target_of(rows, base_ref[half], height)
        signal = (jax.nn.sigmoid(logits) - target).astype(jnp.bfloat16)
        out_ref[...] += jnp.dot(signal, docs, preferred_element_type=jnp.float32)


def gradient_parts(bases, mine, other, docs, rows, tile):
    height, width = mine.shape
    slots = rows.shape[1]
    steps = docs.shape[0] // tile
    whole = pl.BlockSpec((height, width), lambda i: (0, 0))
    shape = jax.ShapeDtypeStruct((height, width), jnp.float32)
    return pl.pallas_call(
        gradient_kernel,
        grid=(steps,),
        in_specs=[
            pl.BlockSpec(memory_space=pltpu.SMEM),
            whole,
            whole,
            pl.BlockSpec((tile, width), lambda i: (i, 0)),
            pl.BlockSpec((None, slots, tile), lambda i: (i, 0, 0)),
        ],
        out_specs=[whole, whole],
        out_shape=[shape, shape],
        compiler_params=pltpu.CompilerParams(vmem_limit_bytes=VMEM_LIMIT),
        name="gradient",
    )(bases, mine, other, docs, rows)


def adam_step(weights, first_moment, second_moment, gradient):
    new_first = beta_one * first_moment + (1.0 - beta_one) * gradient
    new_second = beta_two * second_moment + (1.0 - beta_two) * gradient * gradient
    update = new_first / correct_one / (jnp.sqrt(new_second / correct_two) + adam_eps)
    new_weights = weights - learn_rate * (update + decay_rate * weights)
    return (new_weights, new_first, new_second)


def per_device(
    blocks, embeddings, pos_ids, pos_count, label_slot, weights, first_moment, second_moment
):
    owned = weights.shape[0]
    me = lax.axis_index("blk")
    swap = [(i, i ^ 1) for i in range(blocks)]
    columns = [list(range(core, blocks, 2)) for core in range(2)]
    mine = weights.astype(jnp.bfloat16)
    other = lax.ppermute(mine, "blk", swap)
    docs = lax.all_gather(embeddings, "blk", axis=0, tiled=True, axis_index_groups=columns)
    rows = lookup_rows(label_slot, pos_ids, pos_count)
    rows = lax.all_gather(rows, "blk", axis=0, axis_index_groups=columns)
    bases = jnp.stack([me * owned, (me ^ 1) * owned]).astype(jnp.int32)
    mine_part, other_part = gradient_parts(bases, mine, other, docs, rows, embeddings.shape[0])
    gradient = mine_part + lax.ppermute(other_part, "blk", swap)
    return adam_step(weights, first_moment, second_moment, gradient)


def solution(mesh):
    in_specs = (
        P(("groups", "blk"), None),
        P(("groups", "blk"), None),
        P(("groups", "blk")),
        P(),
        P("blk", None),
        P("blk", None),
        P("blk", None),
    )
    out_specs = (P(("groups", "blk"), None), P(("groups", "blk"), None), P(("groups", "blk"), None))
    return jax.shard_map(
        functools.partial(per_device, mesh.shape["blk"]),
        mesh=mesh,
        in_specs=in_specs,
        out_specs=out_specs,
        check_vma=False,
    )
```

```python
import functools

import jax
import jax.numpy as jnp
import numpy as np
from jax import lax
from jax.experimental import pallas as pl
from jax.experimental.pallas import tpu as pltpu
from jax.sharding import PartitionSpec as P

learn_rate = 0.01
beta_one = 0.9
beta_two = 0.95
adam_eps = 1e-08
decay_rate = 0.1
correct_one = 1.0 - 0.9**10
correct_two = 1.0 - 0.95**10

WORD = 32
VMEM_LIMIT = 32 * 1024 * 1024


def lookup_kernel(ids_ref, count_ref, table_ref, rows_ref):
    slots, docs = ids_ref.shape
    table_rows = table_ref.shape[0]
    for start in range(0, docs, 128):
        ids = ids_ref[:, start : start + 128]
        high_part = ids >> 7
        low_part = ids & 127

        def pick(t, found):
            line = jnp.broadcast_to(table_ref[pl.ds(t, 1), :], (slots, 128))
            here = jnp.take_along_axis(line, low_part, axis=1)
            return jnp.where(high_part == t, here, found)

        found = lax.fori_loop(0, table_rows, pick, jnp.full((slots, 128), -1, jnp.int32), unroll=8)
        place = lax.broadcasted_iota(jnp.int32, (slots, 128), 0)
        live = place < count_ref[:, start : start + 128]
        rows_ref[:, start : start + 128] = jnp.where(live, found, -1).astype(jnp.int16)


def lookup_rows(label_slot, pos_ids, pos_count):
    docs, slots = pos_ids.shape
    return pl.pallas_call(
        lookup_kernel,
        out_shape=jax.ShapeDtypeStruct((slots, docs), jnp.int16),
        name="lookup",
    )(pos_ids.T, pos_count.reshape(1, docs), label_slot.reshape(-1, 128))


def target_of(rows, base, height):
    slots, docs = rows.shape
    local = rows - base
    word = local >> 5
    bit = jnp.left_shift(jnp.ones_like(local), local & (WORD - 1))
    words = [
        jnp.sum(jnp.where(word == w, bit, 0), axis=0, keepdims=True) for w in range(height // WORD)
    ]
    shift = lax.broadcasted_iota(jnp.int32, (WORD, docs), 0)
    spread = [(jnp.broadcast_to(line, (WORD, docs)) >> shift) & 1 for line in words]
    return jnp.concatenate(spread, axis=0).astype(jnp.float32)


def gradient_kernel(bases, slots, fresh, info_ref, *refs):
    halves = len(bases)
    w_refs, refs = refs[:halves], refs[halves:]
    up_ref, down_ref, rows_ref = refs[:3]
    old_refs, new_refs = refs[3:-halves], refs[-halves:]
    split = up_ref.shape[0]
    docs = jnp.concatenate([up_ref[...], down_ref[...]], axis=0)
    rows = jnp.concatenate(
        [rows_ref[info_ref[slots[0]], :, :split], rows_ref[info_ref[slots[1]], :, split:]], axis=1
    ).astype(jnp.int32)
    for half in range(halves):
        weights = w_refs[half][...]
        logits = lax.dot_general(
            weights, docs, (((1,), (1,)), ((), ())), preferred_element_type=jnp.float32
        )
        target = target_of(rows, info_ref[bases[half]], weights.shape[0])
        signal = (jax.nn.sigmoid(logits) - target).astype(jnp.bfloat16)
        part = jnp.dot(signal, docs, preferred_element_type=jnp.float32)
        new_refs[half][...] = part if fresh else old_refs[half][...] + part


def add_gradient(info, bases, slots, weights, up, down, rows, sums):
    halves = len(weights)
    height, width = weights[0].shape
    docs = up.shape[0] + down.shape[0]
    vmem = pl.BlockSpec(memory_space=pltpu.VMEM)
    sums = list(sums or [])
    first_sum = 1 + halves + 3
    return pl.pallas_call(
        functools.partial(gradient_kernel, bases, slots, not sums),
        in_specs=[pl.BlockSpec(memory_space=pltpu.SMEM)] + [vmem] * (halves + 3 + len(sums)),
        out_specs=[vmem] * halves,
        out_shape=[jax.ShapeDtypeStruct((height, width), jnp.float32)] * halves,
        input_output_aliases={first_sum + i: i for i in range(len(sums))},
        compiler_params=pltpu.CompilerParams(vmem_limit_bytes=VMEM_LIMIT),
        cost_estimate=pl.CostEstimate(
            flops=4 * halves * height * width * docs,
            bytes_accessed=halves * height * width * 10,
            transcendentals=halves * height * docs,
        ),
        name="gradient",
    )(info, *weights, up, down, rows, *sums)


def adam_step(weights, first_moment, second_moment, gradient):
    new_first = beta_one * first_moment + (1.0 - beta_one) * gradient
    new_second = beta_two * second_moment + (1.0 - beta_two) * gradient * gradient
    update = new_first / correct_one / (jnp.sqrt(new_second / correct_two) + adam_eps)
    new_weights = weights - learn_rate * (update + decay_rate * weights)
    return (new_weights, new_first, new_second)


def closed_path(chips):
    return list(range(0, chips, 2)) + list(range(1, chips, 2))[::-1]


def over_cores(pairs):
    return [(2 * a + core, 2 * b + core) for a, b in pairs for core in range(2)]


def constants_of(blocks, owned, path, slot_of):
    chips = blocks // 2
    table = np.zeros((blocks, 2 + 2 * chips), np.int32)
    for me in range(blocks):
        chip = me // 2
        place = path.index(chip)
        table[me, :2] = me * owned, (me ^ 1) * owned
        for step in range(chips):
            table[me, 2 + 2 * step] = slot_of.index(path[(place - step) % chips] ^ chip)
            table[me, 3 + 2 * step] = slot_of.index(path[(place + step) % chips] ^ chip)
    return table


def after(values, first):
    return lax.optimization_barrier((values, first))[0]


def per_device(
    blocks, embeddings, pos_ids, pos_count, label_slot, weights, first_moment, second_moment
):
    owned = weights.shape[0]
    chips = blocks // 2
    path = closed_path(chips)
    upward = over_cores([(path[i], path[(i + 1) % chips]) for i in range(chips)])
    downward = [(b, a) for a, b in upward]
    swap = [(i, i ^ 1) for i in range(blocks)]
    distances = [chips >> (i + 1) for i in range(chips.bit_length() - 1)]
    slot_of = [0]
    for distance in distances:
        slot_of = slot_of + [s ^ distance for s in slot_of]
    table = jnp.asarray(constants_of(blocks, owned, path, slot_of))
    info = lax.dynamic_index_in_dim(table, lax.axis_index("blk"), keepdims=False)

    split = embeddings.shape[0] // 2
    halves = [(embeddings[:split], embeddings[split:])]
    rows = mine = other = sums = None
    worked = 0
    for step in range(1, chips):
        up, down = halves[-1]
        arriving = (lax.ppermute(up, "blk", upward), lax.ppermute(down, "blk", downward))
        if step == 1:
            rows = lookup_rows(label_slot, pos_ids, pos_count)[None]
            mine = weights.astype(jnp.bfloat16)
            other = lax.ppermute(mine, "blk", swap)
            done = (rows, mine)
        elif step - 2 < len(distances):
            exchange = over_cores([(c, c ^ distances[step - 2]) for c in range(chips)])
            rows = jnp.concatenate([rows, lax.ppermute(rows, "blk", exchange)], axis=0)
            done = (rows, other)
        else:
            for _ in range(2 if step < chips - 1 else chips):
                if worked < step and worked < chips - 1:
                    slots = (2 + 2 * worked, 3 + 2 * worked)
                    sums = add_gradient(info, (0, 1), slots, [mine, other], *halves[worked], rows, sums)
                    worked += 1
            done = sums
        halves.append(after(arriving, done))
    for late in range(worked, chips - 1):
        slots = (2 + 2 * late, 3 + 2 * late)
        sums = add_gradient(info, (0, 1), slots, [mine, other], *halves[late], rows, sums)
    slots = (2 * chips, 2 * chips + 1)
    (other_sum,) = add_gradient(info, (1,), slots, [other], *halves[-1], rows, sums[1:])
    got = lax.ppermute(other_sum, "blk", swap)
    (mine_sum,) = add_gradient(info, (0,), slots, [mine], *halves[-1], rows, sums[:1])
    return adam_step(weights, first_moment, second_moment, mine_sum + got)


def solution(mesh):
    in_specs = (
        P(("groups", "blk"), None),
        P(("groups", "blk"), None),
        P(("groups", "blk")),
        P(),
        P("blk", None),
        P("blk", None),
        P("blk", None),
    )
    out_specs = (P(("groups", "blk"), None), P(("groups", "blk"), None), P(("groups", "blk"), None))
    return jax.shard_map(
        functools.partial(per_device, mesh.shape["blk"]),
        mesh=mesh,
        in_specs=in_specs,
        out_specs=out_specs,
        check_vma=False,
    )
```

```python
import functools

import jax
import jax.numpy as jnp
import numpy as np
from jax import lax
from jax.experimental import pallas as pl
from jax.experimental.pallas import tpu as pltpu
from jax.sharding import PartitionSpec as P

learn_rate = 0.01
beta_one = 0.9
beta_two = 0.95
adam_eps = 1e-08
decay_rate = 0.1
correct_one = 1.0 - 0.9**10
correct_two = 1.0 - 0.95**10

WORD = 32
VMEM_LIMIT = 32 * 1024 * 1024


def lookup_kernel(ids_ref, count_ref, table_ref, rows_ref):
    slots, docs = ids_ref.shape
    table_rows = table_ref.shape[0]
    for start in range(0, docs, 128):
        ids = ids_ref[:, start : start + 128]
        high_part = ids >> 7
        low_part = ids & 127

        def pick(t, found):
            line = jnp.broadcast_to(table_ref[pl.ds(t, 1), :], (slots, 128))
            here = jnp.take_along_axis(line, low_part, axis=1)
            return jnp.where(high_part == t, here, found)

        found = lax.fori_loop(0, table_rows, pick, jnp.full((slots, 128), -1, jnp.int32), unroll=8)
        place = lax.broadcasted_iota(jnp.int32, (slots, 128), 0)
        live = place < count_ref[:, start : start + 128]
        rows_ref[:, start : start + 128] = jnp.where(live, found, -1).astype(jnp.int16)


def lookup_rows(label_slot, pos_ids, pos_count):
    docs, slots = pos_ids.shape
    return pl.pallas_call(
        lookup_kernel,
        out_shape=jax.ShapeDtypeStruct((slots, docs), jnp.int16),
        name="lookup",
    )(pos_ids.T, pos_count.reshape(1, docs), label_slot.reshape(-1, 128))


def signs_of(rows, base, height):
    slots, docs = rows.shape
    local = rows - base
    word = local >> 5
    bit = jnp.left_shift(jnp.ones_like(local), local & (WORD - 1))
    words = [
        jnp.sum(jnp.where(word == w, bit, 0), axis=0, keepdims=True) for w in range(height // WORD)
    ]
    place = jnp.left_shift(
        jnp.ones((WORD, docs), jnp.int32), lax.broadcasted_iota(jnp.int32, (WORD, docs), 0)
    )
    spread = [
        jnp.where((jnp.broadcast_to(line, (WORD, docs)) & place) != 0, -1.0, 1.0) for line in words
    ]
    return jnp.concatenate(spread, axis=0)


def gradient_kernel(bases, pieces, fresh, info_ref, rows_ref, *refs):
    blocks = len(bases)
    w_refs, refs = refs[:blocks], refs[blocks:]
    doc_refs, refs = refs[: len(pieces)], refs[len(pieces) :]
    old_refs, new_refs = refs[:-blocks], refs[-blocks:]
    height = w_refs[0].shape[0]
    docs = jnp.concatenate([ref[...] for ref in doc_refs], axis=0)
    weights = jnp.concatenate([ref[...] for ref in w_refs], axis=0)
    rows = jnp.concatenate(
        [rows_ref[info_ref[column], :, start:end] for column, start, end in pieces], axis=1
    ).astype(jnp.int32)
    halved = lax.dot_general(
        weights, docs, (((1,), (1,)), ((), ())), preferred_element_type=jnp.float32
    )
    signs = jnp.concatenate([signs_of(rows, info_ref[base], height) for base in bases], axis=0)
    signal = (jnp.tanh(halved) + signs).astype(jnp.bfloat16)
    part = jnp.dot(signal, docs, preferred_element_type=jnp.float32)
    for block in range(blocks):
        piece = part[block * height : (block + 1) * height]
        new_refs[block][...] = piece if fresh else old_refs[block][...] + piece


def add_gradient(info, bases, pieces, rows, weights, docs, sums):
    blocks = len(weights)
    height, width = weights[0].shape
    number = sum(doc.shape[0] for doc in docs)
    vmem = pl.BlockSpec(memory_space=pltpu.VMEM)
    sums = list(sums or [])
    inputs = [rows, *weights, *docs, *sums]
    first_sum = 1 + len(inputs) - len(sums)
    return pl.pallas_call(
        functools.partial(gradient_kernel, bases, pieces, not sums),
        in_specs=[pl.BlockSpec(memory_space=pltpu.SMEM)] + [vmem] * len(inputs),
        out_specs=[vmem] * blocks,
        out_shape=[jax.ShapeDtypeStruct((height, width), jnp.float32)] * blocks,
        input_output_aliases={first_sum + i: i for i in range(len(sums))},
        compiler_params=pltpu.CompilerParams(vmem_limit_bytes=VMEM_LIMIT),
        cost_estimate=pl.CostEstimate(
            flops=4 * blocks * height * width * number,
            bytes_accessed=blocks * height * width * 10,
            transcendentals=blocks * height * number,
        ),
        name="gradient",
    )(info, *inputs)


def adam_step(weights, first_moment, second_moment, gradient):
    new_first = beta_one * first_moment + (1.0 - beta_one) * gradient
    new_second = beta_two * second_moment + (1.0 - beta_two) * gradient * gradient
    update = new_first / correct_one / (jnp.sqrt(new_second / correct_two) + adam_eps)
    new_weights = weights - learn_rate * (update + decay_rate * weights)
    return (new_weights, new_first, new_second)


def over_cores(pairs):
    return [(2 * a + core, 2 * b + core) for a, b in pairs for core in range(2)]


def constants_of(blocks, owned, across, distances):
    chips = blocks // 2
    along = chips // across
    slot_of = [0]
    for distance in distances:
        slot_of = slot_of + [s ^ distance for s in slot_of]
    table = np.zeros((blocks, 2 + 4 * along), np.int32)
    for me in range(blocks):
        chip = me // 2
        z, y = divmod(chip, across)
        table[me, :2] = me * owned, (me ^ 1) * owned
        for step in range(along):
            sources = [((z + sign * step) % along, other) for other in (0, 1) for sign in (-1, 1)]
            for i, (from_z, other) in enumerate(sources):
                from_chip = from_z * across + (y + other) % across
                table[me, 2 + 4 * step + i] = slot_of.index(from_chip ^ chip)
    return table


def after(values, first):
    return lax.optimization_barrier((values, first))[0]


def per_device(
    blocks,
    across,
    embeddings,
    pos_ids,
    pos_count,
    label_slot,
    weights,
    first_moment,
    second_moment,
):
    owned = weights.shape[0]
    chips = blocks // 2
    along = chips // across
    upward = over_cores([(c, (c + across) % chips) for c in range(chips)])
    downward = [(b, a) for a, b in upward]
    beside = over_cores([(c, c ^ 1) for c in range(chips)])
    swap = [(i, i ^ 1) for i in range(blocks)]
    distances = [1] * (across - 1)
    distances += [chips >> (i + 1) for i in range(along.bit_length() - 1)]
    table = jnp.asarray(constants_of(blocks, owned, across, distances))
    info = lax.dynamic_index_in_dim(table, lax.axis_index("blk"), keepdims=False)
    number = embeddings.shape[0]
    split = number // 2

    def send(value, pairs):
        return lax.ppermute(value, "blk", pairs)

    def pieces_of(step, other):
        column = 2 + 4 * step + 2 * other
        return ((column, 0, split), (column + 1, split, number))

    own = ((2, 0, number),)
    neighbour = ((4, 0, number),)
    if across == 2:
        beside_own = send(embeddings, beside)
    a_half, b_half = embeddings[:split], embeddings[split:]
    a_next, b_next = send(a_half, upward), send(b_half, downward)
    mine = weights.astype(jnp.bfloat16) * 0.5
    other = send(mine, swap)
    rows = lookup_rows(label_slot, pos_ids, pos_count)[None]
    row_parts = [rows]
    row_next = send(rows, over_cores([(c, c ^ distances[0]) for c in range(chips)]))
    sums = add_gradient(info, (0, 1), own, rows, [mine, other], [embeddings], None)
    waiting = []
    late = []
    if across == 2:
        waiting.append((1, neighbour, [beside_own]))
        late_b = None
    stage = 0

    def advance(tie):
        nonlocal rows, row_next, stage
        if stage == len(distances):
            return
        got = after(row_next, tie)
        rows = jnp.concatenate([rows, got], axis=0)
        stage += 1
        if stage < len(distances):
            row_next = send(rows, over_cores([(c, c ^ distances[stage]) for c in range(chips)]))

    def work(limit):
        nonlocal sums
        while waiting and limit and (waiting[0][0] <= stage):
            _, pieces, docs = waiting.pop(0)
            sums = add_gradient(info, (0, 1), pieces, rows, [mine, other], docs, sums)
            limit -= 1

    for step in range(1, along):
        last = step == along - 1
        a_half = after(a_next, sums)
        if not last:
            a_next = send(a_half, upward)
        if across == 2:
            a_beside = send(a_half, beside)
        b_half = after(b_next, sums)
        if not last:
            b_next = send(b_half, downward)
        if across == 2 and not last:
            b_beside = send(b_half, beside)
        if across == 2 and step == 1:
            late_b = send(after(beside_own, sums)[split:], upward)
        advance(sums)
        work(1)
        advance(sums)
        waiting.append((len(distances), pieces_of(step, 0), [a_half, b_half]))
        if across == 2:
            waiting.append((len(distances), pieces_of(step, 1), [a_beside, late_b if last else b_beside]))
        if step > 1:
            work(1 if not last else len(waiting) - 1)
    while stage < len(distances):
        advance(sums)
    work(len(waiting) - 1)
    _, pieces, docs = waiting.pop()
    (other_sum,) = add_gradient(info, (1,), pieces, rows, [other], docs, sums[1:])
    got = send(other_sum, swap)
    (mine_sum,) = add_gradient(info, (0,), pieces, rows, [mine], docs, sums[:1])
    return adam_step(weights, first_moment, second_moment, 0.5 * (mine_sum + got))


def solution(mesh):
    in_specs = (
        P(("groups", "blk"), None),
        P(("groups", "blk"), None),
        P(("groups", "blk")),
        P(),
        P("blk", None),
        P("blk", None),
        P("blk", None),
    )
    out_specs = (P(("groups", "blk"), None), P(("groups", "blk"), None), P(("groups", "blk"), None))
    return jax.shard_map(
        functools.partial(per_device, mesh.shape["blk"], 4 // mesh.shape["groups"]),
        mesh=mesh,
        in_specs=in_specs,
        out_specs=out_specs,
        check_vma=False,
    )
```

```python
import functools

import jax
import jax.numpy as jnp
from jax import lax
from jax.experimental import pallas as pl
from jax.experimental.pallas import tpu as pltpu
from jax.sharding import PartitionSpec as P

learn_rate = 0.01
beta_one = 0.9
beta_two = 0.95
adam_eps = 1e-08
decay_rate = 0.1
correct_one = 1.0 - 0.9**10
correct_two = 1.0 - 0.95**10

WORD = 32
VMEM_LIMIT = 32 * 1024 * 1024
SMALL = pl.CostEstimate(flops=1, bytes_accessed=1, transcendentals=0)


def lookup_kernel(ids_ref, count_ref, table_ref, rows_ref):
    slots, docs = ids_ref.shape
    pairs = table_ref.shape[0] // 2
    starts = range(0, docs, 128)
    ids = [ids_ref[:, start : start + 128] for start in starts]
    line_of = [(chunk >> 7) & (pairs - 1) for chunk in ids]
    lane_of = [chunk & 127 for chunk in ids]

    def pick(t, found):
        both = table_ref[pl.ds(t, 1), :] | (table_ref[pl.ds(t + pairs, 1), :] << 16)
        line = jnp.broadcast_to(both, (slots, 128))
        return tuple(
            jnp.where(line_of[i] == t, jnp.take_along_axis(line, lane_of[i], axis=1), found[i])
            for i in range(len(ids))
        )

    found = tuple(jnp.zeros((slots, 128), jnp.int32) for _ in ids)
    if pairs <= 16:
        for t in range(pairs):
            found = pick(t, found)
    else:
        found = lax.fori_loop(0, pairs, pick, found, unroll=8)
    place = lax.broadcasted_iota(jnp.int32, (slots, 128), 0)
    for i, start in enumerate(starts):
        row = jnp.where((ids[i] >> 7) < pairs, found[i], found[i] >> 16) & 0xFFFF
        live = place < count_ref[:, start : start + 128]
        rows_ref[:, start : start + 128] = jnp.where(live, row, -1).astype(jnp.int16)


def lookup_rows(label_slot, pos_ids, pos_count):
    docs, slots = pos_ids.shape
    return pl.pallas_call(
        lookup_kernel,
        out_shape=jax.ShapeDtypeStruct((slots, docs), jnp.int16),
        cost_estimate=SMALL,
        name="lookup",
    )(pos_ids.T, pos_count.reshape(1, docs), label_slot.reshape(-1, 128))


def signs_of(rows, base, height):
    slots, docs = rows.shape
    local = rows - base
    word = local >> 5
    bit = jnp.left_shift(jnp.ones_like(local), local & (WORD - 1))
    words = [
        jnp.sum(jnp.where(word == w, bit, 0), axis=0, keepdims=True) for w in range(height // WORD)
    ]
    place = jnp.left_shift(
        jnp.ones((WORD, docs), jnp.int32), lax.broadcasted_iota(jnp.int32, (WORD, docs), 0)
    )
    spread = [
        jnp.where((jnp.broadcast_to(line, (WORD, docs)) & place) != 0, -1.0, 1.0) for line in words
    ]
    return jnp.concatenate(spread, axis=0)


def row_slot(layout, step, other):
    across, along, distances = layout
    me = lax.axis_index("blk")
    core, chip = me & 1, me >> 1
    shift = across.bit_length() - 1
    from_z = ((chip >> shift) - step * (1 - 2 * core)) & (along - 1)
    from_chip = (from_z << shift) | ((chip & (across - 1)) ^ other)
    apart = chip ^ from_chip
    slot = 0
    for place, distance in enumerate(distances):
        slot = slot | (((apart >> (distance.bit_length() - 1)) & 1) << place)
    return slot


def gradient_kernel(layout, owners, sources, fresh, rows_ref, *refs):
    blocks = len(owners)
    w_refs, refs = refs[:blocks], refs[blocks:]
    doc_refs, refs = refs[: len(sources)], refs[len(sources) :]
    old_refs, new_refs = refs[:-blocks], refs[-blocks:]
    height = w_refs[0].shape[0]
    me = lax.axis_index("blk")
    docs = jnp.concatenate([ref[...] for ref in doc_refs], axis=0)
    weights = jnp.concatenate([ref[...] for ref in w_refs], axis=0)
    rows = jnp.concatenate(
        [rows_ref[row_slot(layout, *source)] for source in sources], axis=1
    ).astype(jnp.int32)
    halved = lax.dot_general(
        weights, docs, (((1,), (1,)), ((), ())), preferred_element_type=jnp.float32
    )
    signs = jnp.concatenate(
        [signs_of(rows, (me ^ owner) * height, height) for owner in owners], axis=0
    )
    signal = (jnp.tanh(halved) + signs).astype(jnp.bfloat16)
    part = jnp.dot(signal, docs, preferred_element_type=jnp.float32)
    for block in range(blocks):
        piece = part[block * height : (block + 1) * height]
        new_refs[block][...] = piece if fresh else old_refs[block][...] + piece


def add_gradient(layout, owners, sources, rows, weights, docs, sums):
    blocks = len(weights)
    height, width = weights[0].shape
    vmem = pl.BlockSpec(memory_space=pltpu.VMEM)
    sums = list(sums)
    inputs = [rows, *weights, *docs, *sums]
    first_sum = len(inputs) - len(sums)
    return pl.pallas_call(
        functools.partial(gradient_kernel, layout, owners, sources, not sums),
        in_specs=[vmem] * len(inputs),
        out_specs=[vmem] * blocks,
        out_shape=[jax.ShapeDtypeStruct((height, width), jnp.float32)] * blocks,
        input_output_aliases={first_sum + i: i for i in range(len(sums))},
        compiler_params=pltpu.CompilerParams(vmem_limit_bytes=VMEM_LIMIT),
        cost_estimate=SMALL,
        name="gradient",
    )(*inputs)


def adam_step(weights, first_moment, second_moment, gradient):
    new_first = beta_one * first_moment + (1.0 - beta_one) * gradient
    new_second = beta_two * second_moment + (1.0 - beta_two) * gradient * gradient
    update = new_first / correct_one / (jnp.sqrt(new_second / correct_two) + adam_eps)
    new_weights = weights - learn_rate * (update + decay_rate * weights)
    return (new_weights, new_first, new_second)


def over_cores(pairs):
    return [(2 * a + core, 2 * b + core) for a, b in pairs for core in range(2)]


together = lax.optimization_barrier


def per_device(
    blocks,
    across,
    embeddings,
    pos_ids,
    pos_count,
    label_slot,
    weights,
    first_moment,
    second_moment,
):
    chips = blocks // 2
    along = chips // across
    distances = [1] * (across - 1)
    distances += [chips >> (i + 1) for i in range(along.bit_length() - 1)]
    layout = (across, along, tuple(distances))

    def send(value, pairs):
        return lax.ppermute(value, "blk", pairs)

    ring = [(i, (i + (2 - 4 * (i & 1)) * across) % blocks) for i in range(blocks)]
    back = [(b, a) for a, b in ring]
    beside = over_cores([(c, c ^ 1) for c in range(chips)])
    swap = [(i, i ^ 1) for i in range(blocks)]
    stages = [over_cores([(c, c ^ distance) for c in range(chips)]) for distance in distances]

    coming = send(embeddings, ring)
    if across == 2:
        neighbour = send(embeddings, beside)
    rows = lookup_rows(label_slot, pos_ids, pos_count)[None]
    coming_rows = [send(rows, stages[0])]
    mine = weights.astype(jnp.bfloat16) * 0.5
    other = send(mine, swap)
    sums = ()

    def work(source, docs):
        nonlocal sums
        sums = add_gradient(layout, (0, 1), [source], rows, [mine, other], [docs], sums)

    def gather_rows():
        nonlocal rows, sums
        stage = len(coming_rows)
        if coming_rows[-1] is not None:
            got, sums = together((coming_rows[-1], sums))
            rows = jnp.concatenate([rows, got], axis=0)
            coming_rows.append(send(rows, stages[stage]) if stage < len(stages) else None)

    gather_rows()
    waiting = [((0, 0), embeddings)]
    arrived = [coming, sums, rows]
    if across == 2:
        arrived.append(neighbour)
    for step in range(1, along):
        arrived = together(tuple(arrived))
        block, sums, rows = arrived[:3]
        if across == 2:
            waiting.append(((step - 1, 1), arrived[3]))
        if step == along - 1:
            break
        coming = send(block, ring)
        arrived = [coming, None, None]
        if across == 2:
            arrived.append(send(block, beside))
            if step == 1:
                far = ((along - 1, 1), send(waiting[-1][1], back))
        for source, docs in waiting:
            work(source, docs)
            gather_rows()
        waiting = [((step, 0), block)]
        if across == 2 and step == 2:
            waiting.append(far)
        arrived[1:3] = sums, rows
    waiting.append(((along - 1, 0), block))
    while coming_rows[-1] is not None:
        gather_rows()
    while len(waiting) > 1:
        work(*waiting.pop(0))
    source, docs = waiting.pop()
    (other_sum,) = add_gradient(layout, (1,), [source], rows, [other], [docs], sums[1:])
    got = send(other_sum, swap)
    (mine_sum,) = add_gradient(layout, (0,), [source], rows, [mine], [docs], sums[:1])
    return adam_step(weights, first_moment, second_moment, 0.5 * (mine_sum + got))


def solution(mesh):
    in_specs = (
        P(("groups", "blk"), None),
        P(("groups", "blk"), None),
        P(("groups", "blk")),
        P(),
        P("blk", None),
        P("blk", None),
        P("blk", None),
    )
    out_specs = (P(("groups", "blk"), None), P(("groups", "blk"), None), P(("groups", "blk"), None))
    return jax.shard_map(
        functools.partial(per_device, mesh.shape["blk"], 4 // mesh.shape["groups"]),
        mesh=mesh,
        in_specs=in_specs,
        out_specs=out_specs,
        check_vma=False,
    )
```

```python
import functools

import jax
import jax.numpy as jnp
from jax import lax
from jax.experimental import pallas as pl
from jax.experimental.pallas import tpu as pltpu
from jax.sharding import PartitionSpec as P

learn_rate = 0.01
beta_one = 0.9
beta_two = 0.95
adam_eps = 1e-08
decay_rate = 0.1
correct_one = 1.0 - 0.9**10
correct_two = 1.0 - 0.95**10

WORD = 32
LANES = 128
VMEM_LIMIT = 32 * 1024 * 1024
LONG = pl.CostEstimate(flops=10**10, bytes_accessed=10**6, transcendentals=0)


def power_of_two(exponent, bits, start, sign):
    value = start
    for bit in range(bits):
        factor = 2.0 ** (sign * (1 << bit))
        value = value * jnp.where(((exponent >> bit) & 1) == 1, factor, 1.0)
    return value


def lookup_kernel(bits, ids_ref, count_ref, table_ref, docs_ref, out_ref):
    slots, docs = ids_ref.shape
    pairs = table_ref.shape[0] // 2
    starts = range(0, docs, LANES)
    ids = [ids_ref[:, start : start + LANES] for start in starts]
    line_of = [(chunk >> 7) & (pairs - 1) for chunk in ids]
    lane_of = [chunk & (LANES - 1) for chunk in ids]

    def pick(t, found):
        both = table_ref[pl.ds(t, 1), :] | (table_ref[pl.ds(t + pairs, 1), :] << 16)
        line = jnp.broadcast_to(both, (slots, LANES))
        return tuple(
            jnp.where(line_of[i] == t, jnp.take_along_axis(line, lane_of[i], axis=1), found[i])
            for i in range(len(ids))
        )

    found = tuple(jnp.zeros((slots, LANES), jnp.int32) for _ in ids)
    if pairs <= 16:
        for t in range(pairs):
            found = pick(t, found)
    else:
        found = lax.fori_loop(0, pairs, pick, found, unroll=8)
    place = lax.broadcasted_iota(jnp.int32, (slots, LANES), 0)
    head = out_ref.shape[0] - slots // 2
    out_ref[:head, :] = docs_ref[:head, :]
    out_ref[head:, :] = jnp.zeros((slots // 2, out_ref.shape[1]), jnp.bfloat16)
    for i, start in enumerate(starts):
        row = jnp.where((ids[i] >> 7) < pairs, found[i], found[i] >> 16) & 0xFFFF
        low = (LANES + (row & (LANES - 1))).astype(jnp.float32)
        code = power_of_two(row >> 7, bits, low * 2.0**-64, 1)
        code = jnp.where(place < count_ref[:, start : start + LANES], code, 0.0)
        code = code.astype(jnp.bfloat16)
        out_ref[head:, start : start + LANES] = code[: slots // 2]
        out_ref[head:, docs + start : docs + start + LANES] = code[slots // 2 :]


def lookup_rows(label_slot, pos_ids, pos_count, embeddings, head):
    docs, slots = pos_ids.shape
    lines = label_slot.shape[0] // LANES
    return pl.pallas_call(
        functools.partial(lookup_kernel, (lines - 1).bit_length()),
        out_shape=jax.ShapeDtypeStruct((head + slots // 2, embeddings.shape[1]), jnp.bfloat16),
        name="lookup",
    )(pos_ids.T, pos_count.reshape(1, docs), label_slot.reshape(lines, LANES), embeddings)


def signs_of(codes, owner, bits, height):
    docs = codes.shape[1]
    scale = power_of_two(owner * (height // LANES), bits, jnp.float32(2.0**64), -1)
    scaled = codes * scale
    place = jnp.left_shift(
        jnp.ones((WORD, docs), jnp.int32), lax.broadcasted_iota(jnp.int32, (WORD, docs), 0)
    )
    spread = []
    for part in range(height // LANES):
        row = jnp.minimum(scaled * 2.0**-part, 512.0).astype(jnp.int32) - LANES
        word = row >> 5
        bit = jnp.left_shift(jnp.ones_like(row), row & (WORD - 1))
        for w in range(LANES // WORD):
            line = jnp.sum(jnp.where(word == w, bit, 0), axis=0, keepdims=True)
            line = jnp.broadcast_to(line, (WORD, docs))
            spread.append(jnp.where((line & place) != 0, -1.0, 1.0))
    return jnp.concatenate(spread, axis=0)


def gradient_kernel(bits, owners, fresh, a_ref, b_ref, *refs):
    blocks = len(owners)
    w_refs, refs = refs[:blocks], refs[blocks:]
    old_refs, new_refs = refs[:-blocks], refs[-blocks:]
    height = w_refs[0].shape[0]
    me = lax.axis_index("blk")
    after = b_ref.shape[0]
    head = a_ref.shape[0]
    slots = 32
    head = head - slots // 2
    docs = jnp.concatenate([a_ref[:head, :], b_ref[...]], axis=0)
    number = head + after
    codes = jnp.concatenate(
        [a_ref[head:, :number], a_ref[head:, number : 2 * number]], axis=0
    ).astype(jnp.float32)
    weights = jnp.concatenate([ref[...] for ref in w_refs], axis=0)
    halved = lax.dot_general(
        weights, docs, (((1,), (1,)), ((), ())), preferred_element_type=jnp.float32
    )
    signs = jnp.concatenate([signs_of(codes, me ^ owner, bits, height) for owner in owners], axis=0)
    signal = (jnp.tanh(halved) + signs).astype(jnp.bfloat16)
    part = jnp.dot(signal, docs, preferred_element_type=jnp.float32)
    for block in range(blocks):
        piece = part[block * height : (block + 1) * height]
        new_refs[block][...] = piece if fresh else old_refs[block][...] + piece


def add_gradient(bits, owners, a, b, weights, sums):
    blocks = len(weights)
    height, width = weights[0].shape
    vmem = pl.BlockSpec(memory_space=pltpu.VMEM)
    sums = list(sums)
    inputs = [a, b, *weights, *sums]
    first_sum = len(inputs) - len(sums)
    return pl.pallas_call(
        functools.partial(gradient_kernel, bits, owners, not sums),
        in_specs=[vmem] * len(inputs),
        out_specs=[vmem] * blocks,
        out_shape=[jax.ShapeDtypeStruct((height, width), jnp.float32)] * blocks,
        input_output_aliases={first_sum + i: i for i in range(len(sums))},
        compiler_params=pltpu.CompilerParams(vmem_limit_bytes=VMEM_LIMIT),
        cost_estimate=LONG,
        name="gradient",
    )(*inputs)


def adam_step(weights, first_moment, second_moment, gradient):
    new_first = beta_one * first_moment + (1.0 - beta_one) * gradient
    new_second = beta_two * second_moment + (1.0 - beta_two) * gradient * gradient
    update = new_first / correct_one / (jnp.sqrt(new_second / correct_two) + adam_eps)
    new_weights = weights - learn_rate * (update + decay_rate * weights)
    return (new_weights, new_first, new_second)


def ring_of(blocks, across):
    path = list(range(0, blocks // 2, across))
    if across == 2:
        path += list(range(1, blocks // 2, 2))[::-1]
    pairs = []
    for here, there in zip(path, path[1:] + path[:1]):
        pairs += [(2 * here, 2 * there), (2 * there + 1, 2 * here + 1)]
    return pairs


together = lax.optimization_barrier


def per_device(
    blocks,
    across,
    embeddings,
    pos_ids,
    pos_count,
    label_slot,
    weights,
    first_moment,
    second_moment,
):
    chips = blocks // 2
    ring = ring_of(blocks, across)
    swap = [(i, i ^ 1) for i in range(blocks)]
    bits = (label_slot.shape[0] // LANES - 1).bit_length()
    head = embeddings.shape[0] // 2

    def send(value, pairs):
        return lax.ppermute(value, "blk", pairs)

    def add(owner, docs, total):
        (total,) = add_gradient(bits, (owner,), *docs, [(mine, other)[owner]], total)
        return (total,)

    b = embeddings[head:]
    next_b = send(b, ring)
    a = lookup_rows(label_slot, pos_ids, pos_count, embeddings, head)
    next_a = send(a, ring)
    mine = weights.astype(jnp.bfloat16) * 0.5
    other = send(mine, swap)
    mine_sum, other_sum = (), ()
    for step in range(1, chips):
        before = (a, b)
        b, before, other_sum = together((next_b, before, other_sum))
        if step < chips - 1:
            next_b = send(b, ring)
        mine_sum = add(0, before, mine_sum)
        a, before, mine_sum = together((next_a, before, mine_sum))
        if step < chips - 1:
            next_a = send(a, ring)
        other_sum = add(1, before, other_sum)
    other_sum = add(1, (a, b), other_sum)
    got = send(other_sum[0], swap)
    mine_sum = add(0, (a, b), mine_sum)
    return adam_step(weights, first_moment, second_moment, 0.5 * (mine_sum[0] + got))


def solution(mesh):
    in_specs = (
        P(("groups", "blk"), None),
        P(("groups", "blk"), None),
        P(("groups", "blk")),
        P(),
        P("blk", None),
        P("blk", None),
        P("blk", None),
    )
    out_specs = (P(("groups", "blk"), None), P(("groups", "blk"), None), P(("groups", "blk"), None))
    return jax.shard_map(
        functools.partial(per_device, mesh.shape["blk"], 4 // mesh.shape["groups"]),
        mesh=mesh,
        in_specs=in_specs,
        out_specs=out_specs,
        check_vma=False,
    )
```

```python
import functools

import jax
import jax.numpy as jnp
from jax import lax
from jax.experimental import pallas as pl
from jax.experimental.pallas import tpu as pltpu
from jax.sharding import PartitionSpec as P

learn_rate = 0.01
beta_one = 0.9
beta_two = 0.95
adam_eps = 1e-08
decay_rate = 0.1
correct_one = 1.0 - 0.9**10
correct_two = 1.0 - 0.95**10

WORD = 32
LANES = 128
VMEM_LIMIT = 32 * 1024 * 1024


def power_of_two(exponent, bits, start, sign):
    value = start
    for bit in range(bits):
        factor = 2.0 ** (sign * (1 << bit))
        value = value * jnp.where(((exponent >> bit) & 1) == 1, factor, 1.0)
    return value


def lookup_kernel(bits, ids_ref, count_ref, table_ref, docs_ref, out_ref):
    slots, docs = ids_ref.shape
    pairs = table_ref.shape[0] // 2
    starts = range(0, docs, LANES)
    ids = [ids_ref[:, start : start + LANES] for start in starts]
    line_of = [(chunk >> 7) & (pairs - 1) for chunk in ids]
    lane_of = [chunk & (LANES - 1) for chunk in ids]

    def pick(t, found):
        both = table_ref[pl.ds(t, 1), :] | (table_ref[pl.ds(t + pairs, 1), :] << 16)
        line = jnp.broadcast_to(both, (slots, LANES))
        return tuple(
            jnp.where(line_of[i] == t, jnp.take_along_axis(line, lane_of[i], axis=1), found[i])
            for i in range(len(ids))
        )

    found = tuple(jnp.zeros((slots, LANES), jnp.int32) for _ in ids)
    if pairs <= 16:
        for t in range(pairs):
            found = pick(t, found)
    else:
        found = lax.fori_loop(0, pairs, pick, found, unroll=8)
    place = lax.broadcasted_iota(jnp.int32, (slots, LANES), 0)
    head = out_ref.shape[0] - slots // 2
    out_ref[:head, :] = docs_ref[:head, :]
    out_ref[head:, :] = jnp.zeros((slots // 2, out_ref.shape[1]), jnp.bfloat16)
    for i, start in enumerate(starts):
        row = jnp.where((ids[i] >> 7) < pairs, found[i], found[i] >> 16) & 0xFFFF
        low = (LANES + (row & (LANES - 1))).astype(jnp.float32)
        code = power_of_two(row >> 7, bits, low * 2.0**-64, 1)
        code = jnp.where(place < count_ref[:, start : start + LANES], code, 0.0)
        code = code.astype(jnp.bfloat16)
        out_ref[head:, start : start + LANES] = code[: slots // 2]
        out_ref[head:, docs + start : docs + start + LANES] = code[slots // 2 :]


def lookup_rows(label_slot, pos_ids, pos_count, embeddings, head):
    docs, slots = pos_ids.shape
    lines = label_slot.shape[0] // LANES
    return pl.pallas_call(
        functools.partial(lookup_kernel, (lines - 1).bit_length()),
        out_shape=jax.ShapeDtypeStruct((head + slots // 2, embeddings.shape[1]), jnp.bfloat16),
        name="lookup",
    )(pos_ids.T, pos_count.reshape(1, docs), label_slot.reshape(lines, LANES), embeddings)


def signs_of(codes, owner, bits, height):
    docs = codes.shape[1]
    scale = power_of_two(owner * (height // LANES), bits, jnp.float32(2.0**64), -1)
    scaled = codes * scale
    place = jnp.left_shift(
        jnp.ones((WORD, docs), jnp.int32), lax.broadcasted_iota(jnp.int32, (WORD, docs), 0)
    )
    spread = []
    for part in range(height // LANES):
        row = jnp.minimum(scaled * 2.0**-part, 512.0).astype(jnp.int32) - LANES
        word = row >> 5
        bit = jnp.left_shift(jnp.ones_like(row), row & (WORD - 1))
        for w in range(LANES // WORD):
            line = jnp.sum(jnp.where(word == w, bit, 0), axis=0, keepdims=True)
            line = jnp.broadcast_to(line, (WORD, docs))
            spread.append(jnp.where((line & place) != 0, -1.0, 1.0))
    return jnp.concatenate(spread, axis=0)


def gradient_kernel(bits, owners, fresh, a_ref, b_ref, *refs):
    blocks = len(owners)
    w_refs, refs = refs[:blocks], refs[blocks:]
    old_refs, new_refs = refs[:-blocks], refs[-blocks:]
    height = w_refs[0].shape[0]
    me = lax.axis_index("blk")
    after = b_ref.shape[0]
    head = a_ref.shape[0]
    slots = 32
    head = head - slots // 2
    docs = jnp.concatenate([a_ref[:head, :], b_ref[...]], axis=0)
    number = head + after
    codes = jnp.concatenate(
        [a_ref[head:, :number], a_ref[head:, number : 2 * number]], axis=0
    ).astype(jnp.float32)
    weights = jnp.concatenate([ref[...] for ref in w_refs], axis=0)
    halved = lax.dot_general(
        weights, docs, (((1,), (1,)), ((), ())), preferred_element_type=jnp.float32
    )
    signs = jnp.concatenate([signs_of(codes, me ^ owner, bits, height) for owner in owners], axis=0)
    signal = (jnp.tanh(halved) + signs).astype(jnp.bfloat16)
    part = jnp.dot(signal, docs, preferred_element_type=jnp.float32)
    for block in range(blocks):
        piece = part[block * height : (block + 1) * height]
        new_refs[block][...] = piece if fresh else old_refs[block][...] + piece


def add_gradient(bits, owners, a, b, weights, sums, flops):
    blocks = len(weights)
    height, width = weights[0].shape
    vmem = pl.BlockSpec(memory_space=pltpu.VMEM)
    sums = list(sums)
    inputs = [a, b, *weights, *sums]
    first_sum = len(inputs) - len(sums)
    return pl.pallas_call(
        functools.partial(gradient_kernel, bits, owners, not sums),
        in_specs=[vmem] * len(inputs),
        out_specs=[vmem] * blocks,
        out_shape=[jax.ShapeDtypeStruct((height, width), jnp.float32)] * blocks,
        input_output_aliases={first_sum + i: i for i in range(len(sums))},
        compiler_params=pltpu.CompilerParams(vmem_limit_bytes=VMEM_LIMIT),
        cost_estimate=pl.CostEstimate(flops=flops, bytes_accessed=10**6, transcendentals=0),
        name="gradient",
    )(*inputs)


def adam_step(weights, first_moment, second_moment, gradient):
    new_first = beta_one * first_moment + (1.0 - beta_one) * gradient
    new_second = beta_two * second_moment + (1.0 - beta_two) * gradient * gradient
    update = new_first / correct_one / (jnp.sqrt(new_second / correct_two) + adam_eps)
    new_weights = weights - learn_rate * (update + decay_rate * weights)
    return (new_weights, new_first, new_second)


def ring_of(blocks, across):
    path = list(range(0, blocks // 2, across))
    if across == 2:
        path += list(range(1, blocks // 2, 2))[::-1]
    steps = zip(path, path[1:] + path[:1])
    return [(2 * here + core, 2 * there + core) for here, there in steps for core in range(2)]


together = lax.optimization_barrier


def per_device(
    blocks,
    across,
    embeddings,
    pos_ids,
    pos_count,
    label_slot,
    weights,
    first_moment,
    second_moment,
):
    half_way = blocks // 4
    up = ring_of(blocks, across)
    down = [(there, here) for here, there in up]
    swap = [(i, i ^ 1) for i in range(blocks)]
    bits = (label_slot.shape[0] // LANES - 1).bit_length()
    head = embeddings.shape[0] // 2

    def send(value, pairs):
        return lax.ppermute(value, "blk", pairs)

    b = embeddings[head:]
    coming = {"up_b": send(b, up), "down_b": send(b, down)}
    a = lookup_rows(label_slot, pos_ids, pos_count, embeddings, head)
    coming |= {"up_a": send(a, up), "down_a": send(a, down)}
    mine = weights.astype(jnp.bfloat16) * 0.5
    other = send(mine, swap)
    sums = [(), ()]

    def work(owner, docs, flops):
        weights_of = [(mine, other)[owner]]
        sums[owner] = add_gradient(bits, (owner,), *docs, weights_of, sums[owner], flops)

    waiting = [(0, ()), (0, ()), (0, ()), (0, (a, b)), (1, (a, b))]
    for step in range(1, half_way + 1):
        messages = ["up_b", "down_b", "up_a", "down_a"] if step < half_way else ["down_b", "up_a"]
        passed_on = messages if step < half_way - 1 else ["down_b", "up_a"]
        while step == half_way and len(waiting) > len(messages):
            work(*waiting.pop(0), 3 * 10**8)
        flops = 6 * 10**8 if step < half_way - 1 else 5 * 10**8
        came = {}
        for message in messages:
            owner, docs = waiting.pop(0)
            came[message], docs, sums = together((coming[message], docs, sums))
            if step < half_way and message in passed_on:
                coming[message] = send(came[message], up if message in ("up_a", "up_b") else down)
            if docs:
                work(owner, docs, flops)
        if step < half_way:
            for docs in ((came["up_a"], came["up_b"]), (came["down_a"], came["down_b"])):
                waiting += [(0, docs), (1, docs)]
    docs = (came["up_a"], came["down_b"])
    work(1, docs, 3 * 10**8)
    got = send(sums[1][0], swap)
    work(0, docs, 3 * 10**8)
    return adam_step(weights, first_moment, second_moment, 0.5 * (sums[0][0] + got))


def solution(mesh):
    in_specs = (
        P(("groups", "blk"), None),
        P(("groups", "blk"), None),
        P(("groups", "blk")),
        P(),
        P("blk", None),
        P("blk", None),
        P("blk", None),
    )
    out_specs = (P(("groups", "blk"), None), P(("groups", "blk"), None), P(("groups", "blk"), None))
    return jax.shard_map(
        functools.partial(per_device, mesh.shape["blk"], 4 // mesh.shape["groups"]),
        mesh=mesh,
        in_specs=in_specs,
        out_specs=out_specs,
        check_vma=False,
    )
```

```python
import functools

import jax
import jax.numpy as jnp
from jax import lax
from jax.experimental import pallas as pl
from jax.experimental.pallas import tpu as pltpu
from jax.sharding import PartitionSpec as P

learn_rate = 0.01
beta_one = 0.9
beta_two = 0.95
adam_eps = 1e-08
decay_rate = 0.1
correct_one = 1.0 - 0.9**10
correct_two = 1.0 - 0.95**10

WORD = 32
LANES = 128
VMEM_LIMIT = 32 * 1024 * 1024
FLOPS = 5 * 10**8
LATE_FLOPS = 10 * 10**8
END_FLOPS = 40 * 10**8


def power_of_two(exponent, bits, start, sign):
    value = start
    for bit in range(bits):
        factor = 2.0 ** (sign * (1 << bit))
        value = value * jnp.where(((exponent >> bit) & 1) == 1, factor, 1.0)
    return value


def lookup_kernel(bits, ids_ref, count_ref, table_ref, docs_ref, weights_ref, out_ref, cast_ref):
    slots, docs = ids_ref.shape
    pairs = table_ref.shape[0] // 2
    starts = range(0, docs, LANES)
    ids = [ids_ref[:, start : start + LANES] for start in starts]
    line_of = [(chunk >> 7) & (pairs - 1) for chunk in ids]
    lane_of = [chunk & (LANES - 1) for chunk in ids]

    def pick(t, found):
        both = table_ref[pl.ds(t, 1), :] | (table_ref[pl.ds(t + pairs, 1), :] << 16)
        line = jnp.broadcast_to(both, (slots, LANES))
        return tuple(
            jnp.where(line_of[i] == t, jnp.take_along_axis(line, lane_of[i], axis=1), found[i])
            for i in range(len(ids))
        )

    found = tuple(jnp.zeros((slots, LANES), jnp.int32) for _ in ids)
    if pairs <= 16:
        for t in range(pairs):
            found = pick(t, found)
    else:
        found = lax.fori_loop(0, pairs, pick, found, unroll=8)
    place = lax.broadcasted_iota(jnp.int32, (slots, LANES), 0)
    head = out_ref.shape[0] - slots // 2
    out_ref[:head, :] = docs_ref[:head, :]
    out_ref[head:, :] = jnp.zeros((slots // 2, out_ref.shape[1]), jnp.bfloat16)
    for i, start in enumerate(starts):
        row = jnp.where((ids[i] >> 7) < pairs, found[i], found[i] >> 16) & 0xFFFF
        low = (LANES + (row & (LANES - 1))).astype(jnp.float32)
        code = power_of_two(row >> 7, bits, low * 2.0**-64, 1)
        code = jnp.where(place < count_ref[:, start : start + LANES], code, 0.0)
        code = code.astype(jnp.bfloat16)
        out_ref[head:, start : start + LANES] = code[: slots // 2]
        out_ref[head:, docs + start : docs + start + LANES] = code[slots // 2 :]
    cast_ref[...] = weights_ref[...].astype(jnp.bfloat16) * 0.5


def lookup_rows(label_slot, pos_ids, pos_count, embeddings, weights, head):
    docs, slots = pos_ids.shape
    lines = label_slot.shape[0] // LANES
    return pl.pallas_call(
        functools.partial(lookup_kernel, (lines - 1).bit_length()),
        out_shape=[
            jax.ShapeDtypeStruct((head + slots // 2, embeddings.shape[1]), jnp.bfloat16),
            jax.ShapeDtypeStruct(weights.shape, jnp.bfloat16),
        ],
        compiler_params=pltpu.CompilerParams(vmem_limit_bytes=VMEM_LIMIT),
        name="lookup",
    )(pos_ids.T, pos_count.reshape(1, docs), label_slot.reshape(lines, LANES), embeddings, weights)


def signs_of(codes, owner, bits, height):
    docs = codes.shape[1]
    scale = power_of_two(owner * (height // LANES), bits, jnp.float32(2.0**64), -1)
    scaled = codes * scale
    place = jnp.left_shift(
        jnp.ones((WORD, docs), jnp.int32), lax.broadcasted_iota(jnp.int32, (WORD, docs), 0)
    )
    spread = []
    for part in range(height // LANES):
        row = jnp.minimum(scaled * 2.0**-part, 512.0).astype(jnp.int32) - LANES
        word = row >> 5
        bit = jnp.left_shift(jnp.ones_like(row), row & (WORD - 1))
        for w in range(LANES // WORD):
            line = jnp.sum(jnp.where(word == w, bit, 0), axis=0, keepdims=True)
            line = jnp.broadcast_to(line, (WORD, docs))
            spread.append(jnp.where((line & place) != 0, -1.0, 1.0))
    return jnp.concatenate(spread, axis=0)


def gradient_kernel(bits, owners, fresh, a_ref, b_ref, *refs):
    blocks = len(owners)
    w_refs, refs = refs[:blocks], refs[blocks:]
    old_refs, new_refs = refs[:-blocks], refs[-blocks:]
    height = w_refs[0].shape[0]
    me = lax.axis_index("blk")
    after = b_ref.shape[0]
    head = a_ref.shape[0]
    slots = 32
    head = head - slots // 2
    docs = jnp.concatenate([a_ref[:head, :], b_ref[...]], axis=0)
    number = head + after
    codes = jnp.concatenate(
        [a_ref[head:, :number], a_ref[head:, number : 2 * number]], axis=0
    ).astype(jnp.float32)
    weights = jnp.concatenate([ref[...] for ref in w_refs], axis=0)
    halved = lax.dot_general(
        weights, docs, (((1,), (1,)), ((), ())), preferred_element_type=jnp.float32
    )
    signs = jnp.concatenate([signs_of(codes, me ^ owner, bits, height) for owner in owners], axis=0)
    signal = (jnp.tanh(halved) + signs).astype(jnp.bfloat16)
    part = jnp.dot(signal, docs, preferred_element_type=jnp.float32)
    for block in range(blocks):
        piece = part[block * height : (block + 1) * height]
        new_refs[block][...] = piece if fresh else old_refs[block][...] + piece


def add_gradient(bits, owners, a, b, weights, sums, flops):
    blocks = len(weights)
    height, width = weights[0].shape
    vmem = pl.BlockSpec(memory_space=pltpu.VMEM)
    sums = list(sums)
    inputs = [a, b, *weights, *sums]
    first_sum = len(inputs) - len(sums)
    return pl.pallas_call(
        functools.partial(gradient_kernel, bits, owners, not sums),
        in_specs=[vmem] * len(inputs),
        out_specs=[vmem] * blocks,
        out_shape=[jax.ShapeDtypeStruct((height, width), jnp.float32)] * blocks,
        input_output_aliases={first_sum + i: i for i in range(len(sums))},
        compiler_params=pltpu.CompilerParams(vmem_limit_bytes=VMEM_LIMIT),
        cost_estimate=pl.CostEstimate(flops=flops, bytes_accessed=10**6, transcendentals=0),
        name="gradient",
    )(*inputs)


def adam_step(weights, first_moment, second_moment, gradient):
    new_first = beta_one * first_moment + (1.0 - beta_one) * gradient
    new_second = beta_two * second_moment + (1.0 - beta_two) * gradient * gradient
    update = new_first / correct_one / (jnp.sqrt(new_second / correct_two) + adam_eps)
    new_weights = weights - learn_rate * (update + decay_rate * weights)
    return (new_weights, new_first, new_second)


def ring_of(blocks, across):
    path = list(range(0, blocks // 2, across))
    if across == 2:
        path += list(range(1, blocks // 2, 2))[::-1]
    steps = zip(path, path[1:] + path[:1])
    return [(2 * here + core, 2 * there + core) for here, there in steps for core in range(2)]


together = lax.optimization_barrier


def per_device(
    blocks,
    across,
    embeddings,
    pos_ids,
    pos_count,
    label_slot,
    weights,
    first_moment,
    second_moment,
):
    half_way = blocks // 4
    up = ring_of(blocks, across)
    down = [(there, here) for here, there in up]
    swap = [(i, i ^ 1) for i in range(blocks)]
    bits = (label_slot.shape[0] // LANES - 1).bit_length()
    head = embeddings.shape[0] // 2

    def send(value, pairs):
        return lax.ppermute(value, "blk", pairs)

    b = embeddings[head:]
    coming = {"up_b": send(b, up), "down_b": send(b, down)}
    a, mine = lookup_rows(label_slot, pos_ids, pos_count, embeddings, weights, head)
    coming |= {"up_a": send(a, up), "down_a": send(a, down)}
    cast = [mine, send(mine, swap)]
    sums = ()
    waiting = [(a, b)]
    for step in range(1, half_way):
        came = {}
        for message in ("up_b", "down_b", "up_a", "down_a"):
            came[message], waiting, sums = together((coming.pop(message), waiting, sums))
            if step < half_way - 1 or message in ("down_b", "up_a"):
                coming[message] = send(came[message], up if message in ("up_a", "up_b") else down)
            if (step > 1 and message in ("down_b", "up_a")) or (step == 2 and message == "down_a"):
                flops = FLOPS if step < half_way - 1 else LATE_FLOPS
                sums = add_gradient(bits, (0, 1), *waiting.pop(0), cast, sums, flops)
        waiting += [(came["up_a"], came["up_b"]), (came["down_a"], came["down_b"])]
    for docs in waiting:
        sums = add_gradient(bits, (0, 1), *docs, cast, sums, FLOPS)
    mine_sum, other_sum = sums
    got = send(other_sum, swap)
    last_b, mine_sum = together((coming["down_b"], mine_sum))
    beside_b = send(last_b, swap)
    last_a, mine_sum = together((coming["up_a"], mine_sum))
    beside_a = send(last_a, swap)
    mine_sum = add_gradient(bits, (0,), last_a, last_b, [mine], [mine_sum], END_FLOPS)
    beside_a, beside_b, mine_sum = together((beside_a, beside_b, mine_sum))
    (mine_sum,) = add_gradient(bits, (0,), beside_a, beside_b, [mine], mine_sum, END_FLOPS)
    return adam_step(weights, first_moment, second_moment, 0.5 * (mine_sum + got))


def solution(mesh):
    in_specs = (
        P(("groups", "blk"), None),
        P(("groups", "blk"), None),
        P(("groups", "blk")),
        P(),
        P("blk", None),
        P("blk", None),
        P("blk", None),
    )
    out_specs = (P(("groups", "blk"), None), P(("groups", "blk"), None), P(("groups", "blk"), None))
    return jax.shard_map(
        functools.partial(per_device, mesh.shape["blk"], 4 // mesh.shape["groups"]),
        mesh=mesh,
        in_specs=in_specs,
        out_specs=out_specs,
        check_vma=False,
    )
```

```python
import functools

import jax
import jax.numpy as jnp
from jax import lax
from jax.experimental import pallas as pl
from jax.experimental.pallas import tpu as pltpu
from jax.sharding import PartitionSpec as P

learn_rate = 0.01
beta_one = 0.9
beta_two = 0.95
adam_eps = 1e-08
decay_rate = 0.1
correct_one = 1.0 - 0.9**10
correct_two = 1.0 - 0.95**10

WORD = 32
LANES = 128
VMEM_LIMIT = 32 * 1024 * 1024
FLOPS = 5 * 10**8
LATE_FLOPS = 10 * 10**8
END_FLOPS = 40 * 10**8


def power_of_two(exponent, bits, start, sign):
    value = start
    for bit in range(bits):
        factor = 2.0 ** (sign * (1 << bit))
        value = value * jnp.where(((exponent >> bit) & 1) == 1, factor, 1.0)
    return value


def prepare_kernel(
    bits,
    ids_hbm,
    count_hbm,
    table_hbm,
    docs_hbm,
    weights_hbm,
    a_ref,
    b_ref,
    cast_ref,
    ids_ref,
    count_ref,
    table_ref,
    weights_ref,
    done,
):
    slots, docs = ids_ref.shape
    head = docs - b_ref.shape[0]
    fetches = [
        pltpu.make_async_copy(source, target, done.at[i])
        for i, (source, target) in enumerate(
            (
                (ids_hbm, ids_ref),
                (table_hbm, table_ref),
                (count_hbm, count_ref),
                (docs_hbm.at[pl.ds(0, head)], a_ref.at[pl.ds(0, head)]),
                (docs_hbm.at[pl.ds(head, docs - head)], b_ref),
                (weights_hbm, weights_ref),
            )
        )
    ]
    for fetch in fetches:
        fetch.start()
    for fetch in fetches[:3]:
        fetch.wait()
    pairs = table_ref.shape[0] // 2
    starts = range(0, docs, LANES)
    ids = [ids_ref[:, start : start + LANES] for start in starts]
    line_of = [(chunk >> 7) & (pairs - 1) for chunk in ids]
    lane_of = [chunk & (LANES - 1) for chunk in ids]

    def pick(t, found):
        both = table_ref[pl.ds(t, 1), :] | (table_ref[pl.ds(t + pairs, 1), :] << 16)
        line = jnp.broadcast_to(both, (slots, LANES))
        return tuple(
            jnp.where(line_of[i] == t, jnp.take_along_axis(line, lane_of[i], axis=1), found[i])
            for i in range(len(ids))
        )

    found = tuple(jnp.zeros((slots, LANES), jnp.int32) for _ in ids)
    if pairs <= 16:
        for t in range(pairs):
            found = pick(t, found)
    else:
        found = lax.fori_loop(0, pairs, pick, found, unroll=8)
    place = lax.broadcasted_iota(jnp.int32, (slots, LANES), 0)
    a_ref[head:, :] = jnp.zeros((slots // 2, a_ref.shape[1]), jnp.bfloat16)
    for i, start in enumerate(starts):
        row = jnp.where((ids[i] >> 7) < pairs, found[i], found[i] >> 16) & 0xFFFF
        low = (LANES + (row & (LANES - 1))).astype(jnp.float32)
        code = power_of_two(row >> 7, bits, low * 2.0**-64, 1)
        code = jnp.where(place < count_ref[:, start : start + LANES], code, 0.0)
        code = code.astype(jnp.bfloat16)
        a_ref[head:, start : start + LANES] = code[: slots // 2]
        a_ref[head:, docs + start : docs + start + LANES] = code[slots // 2 :]
    for fetch in fetches[3:]:
        fetch.wait()
    cast_ref[...] = weights_ref[...].astype(jnp.bfloat16) * 0.5


def prepare(label_slot, pos_ids, pos_count, embeddings, weights, head):
    docs, slots = pos_ids.shape
    width = embeddings.shape[1]
    lines = label_slot.shape[0] // LANES
    table = label_slot.reshape(lines, LANES)
    inputs = (pos_ids.T, pos_count.reshape(1, docs), table, embeddings, weights)
    return pl.pallas_call(
        functools.partial(prepare_kernel, (lines - 1).bit_length()),
        in_specs=[pl.BlockSpec(memory_space=pltpu.HBM)] * 5,
        out_specs=[pl.BlockSpec(memory_space=pltpu.VMEM)] * 3,
        out_shape=[
            jax.ShapeDtypeStruct((head + slots // 2, width), jnp.bfloat16),
            jax.ShapeDtypeStruct((docs - head, width), jnp.bfloat16),
            jax.ShapeDtypeStruct(weights.shape, jnp.bfloat16),
        ],
        scratch_shapes=[
            pltpu.VMEM((slots, docs), jnp.int32),
            pltpu.VMEM((1, docs), jnp.int32),
            pltpu.VMEM((lines, LANES), jnp.int32),
            pltpu.VMEM(weights.shape, jnp.float32),
            pltpu.SemaphoreType.DMA((6,)),
        ],
        compiler_params=pltpu.CompilerParams(vmem_limit_bytes=VMEM_LIMIT),
        name="prepare",
    )(*(pltpu.with_memory_space_constraint(x, pltpu.HBM) for x in inputs))


def signs_of(codes, owner, bits, height):
    docs = codes.shape[1]
    scale = power_of_two(owner * (height // LANES), bits, jnp.float32(2.0**64), -1)
    scaled = codes * scale
    place = jnp.left_shift(
        jnp.ones((WORD, docs), jnp.int32), lax.broadcasted_iota(jnp.int32, (WORD, docs), 0)
    )
    spread = []
    for part in range(height // LANES):
        row = jnp.minimum(scaled * 2.0**-part, 512.0).astype(jnp.int32) - LANES
        word = row >> 5
        bit = jnp.left_shift(jnp.ones_like(row), row & (WORD - 1))
        for w in range(LANES // WORD):
            line = jnp.sum(jnp.where(word == w, bit, 0), axis=0, keepdims=True)
            line = jnp.broadcast_to(line, (WORD, docs))
            spread.append(jnp.where((line & place) != 0, -1.0, 1.0))
    return jnp.concatenate(spread, axis=0)


def gradient_kernel(bits, owners, fresh, a_ref, b_ref, *refs):
    blocks = len(owners)
    w_refs, refs = refs[:blocks], refs[blocks:]
    old_refs, new_refs = refs[:-blocks], refs[-blocks:]
    height = w_refs[0].shape[0]
    me = lax.axis_index("blk")
    after = b_ref.shape[0]
    head = a_ref.shape[0]
    slots = 32
    head = head - slots // 2
    docs = jnp.concatenate([a_ref[:head, :], b_ref[...]], axis=0)
    number = head + after
    codes = jnp.concatenate(
        [a_ref[head:, :number], a_ref[head:, number : 2 * number]], axis=0
    ).astype(jnp.float32)
    weights = jnp.concatenate([ref[...] for ref in w_refs], axis=0)
    halved = lax.dot_general(
        weights, docs, (((1,), (1,)), ((), ())), preferred_element_type=jnp.float32
    )
    signs = jnp.concatenate([signs_of(codes, me ^ owner, bits, height) for owner in owners], axis=0)
    signal = (jnp.tanh(halved) + signs).astype(jnp.bfloat16)
    part = jnp.dot(signal, docs, preferred_element_type=jnp.float32)
    for block in range(blocks):
        piece = part[block * height : (block + 1) * height]
        new_refs[block][...] = piece if fresh else old_refs[block][...] + piece


def add_gradient(bits, owners, a, b, weights, sums, flops):
    blocks = len(weights)
    height, width = weights[0].shape
    vmem = pl.BlockSpec(memory_space=pltpu.VMEM)
    sums = list(sums)
    inputs = [a, b, *weights, *sums]
    first_sum = len(inputs) - len(sums)
    return pl.pallas_call(
        functools.partial(gradient_kernel, bits, owners, not sums),
        in_specs=[vmem] * len(inputs),
        out_specs=[vmem] * blocks,
        out_shape=[jax.ShapeDtypeStruct((height, width), jnp.float32)] * blocks,
        input_output_aliases={first_sum + i: i for i in range(len(sums))},
        compiler_params=pltpu.CompilerParams(vmem_limit_bytes=VMEM_LIMIT),
        cost_estimate=pl.CostEstimate(flops=flops, bytes_accessed=10**6, transcendentals=0),
        name="gradient",
    )(*inputs)


def adam_step(weights, first_moment, second_moment, gradient):
    new_first = beta_one * first_moment + (1.0 - beta_one) * gradient
    new_second = beta_two * second_moment + (1.0 - beta_two) * gradient * gradient
    update = new_first / correct_one / (jnp.sqrt(new_second / correct_two) + adam_eps)
    new_weights = weights - learn_rate * (update + decay_rate * weights)
    return (new_weights, new_first, new_second)


def ring_of(blocks, across):
    path = list(range(0, blocks // 2, across))
    if across == 2:
        path += list(range(1, blocks // 2, 2))[::-1]
    steps = zip(path, path[1:] + path[:1])
    return [(2 * here + core, 2 * there + core) for here, there in steps for core in range(2)]


together = lax.optimization_barrier


def per_device(
    blocks,
    across,
    embeddings,
    pos_ids,
    pos_count,
    label_slot,
    weights,
    first_moment,
    second_moment,
):
    half_way = blocks // 4
    up = ring_of(blocks, across)
    down = [(there, here) for here, there in up]
    swap = [(i, i ^ 1) for i in range(blocks)]
    bits = (label_slot.shape[0] // LANES - 1).bit_length()
    head = embeddings.shape[0] // 2

    def send(value, pairs):
        return lax.ppermute(value, "blk", pairs)

    a, b, mine = prepare(label_slot, pos_ids, pos_count, embeddings, weights, head)
    coming = {"up_b": send(b, up), "down_b": send(b, down)}
    coming |= {"up_a": send(a, up), "down_a": send(a, down)}
    cast = [mine, send(mine, swap)]
    sums = ()
    waiting = [(a, b)]
    for step in range(1, half_way):
        came = {}
        for message in ("up_b", "down_b", "up_a", "down_a"):
            came[message], waiting, sums = together((coming.pop(message), waiting, sums))
            if step < half_way - 1 or message in ("down_b", "up_a"):
                coming[message] = send(came[message], up if message in ("up_a", "up_b") else down)
            if (step > 1 and message in ("down_b", "up_a")) or (step == 2 and message == "down_a"):
                flops = FLOPS if step < half_way - 1 else LATE_FLOPS
                sums = add_gradient(bits, (0, 1), *waiting.pop(0), cast, sums, flops)
        waiting += [(came["up_a"], came["up_b"]), (came["down_a"], came["down_b"])]
    for docs in waiting:
        sums = add_gradient(bits, (0, 1), *docs, cast, sums, FLOPS)
    mine_sum, other_sum = sums
    got = send(other_sum, swap)
    last_b, mine_sum = together((coming["down_b"], mine_sum))
    beside_b = send(last_b, swap)
    last_a, mine_sum = together((coming["up_a"], mine_sum))
    beside_a = send(last_a, swap)
    mine_sum = add_gradient(bits, (0,), last_a, last_b, [mine], [mine_sum], END_FLOPS)
    beside_a, beside_b, mine_sum = together((beside_a, beside_b, mine_sum))
    (mine_sum,) = add_gradient(bits, (0,), beside_a, beside_b, [mine], mine_sum, END_FLOPS)
    return adam_step(weights, first_moment, second_moment, 0.5 * (mine_sum + got))


def solution(mesh):
    in_specs = (
        P(("groups", "blk"), None),
        P(("groups", "blk"), None),
        P(("groups", "blk")),
        P(),
        P("blk", None),
        P("blk", None),
        P("blk", None),
    )
    out_specs = (P(("groups", "blk"), None), P(("groups", "blk"), None), P(("groups", "blk"), None))
    return jax.shard_map(
        functools.partial(per_device, mesh.shape["blk"], 4 // mesh.shape["groups"]),
        mesh=mesh,
        in_specs=in_specs,
        out_specs=out_specs,
        check_vma=False,
    )
```

```python
import functools

import jax
import jax.numpy as jnp
from jax import lax
from jax.experimental import pallas as pl
from jax.experimental.pallas import tpu as pltpu
from jax.sharding import PartitionSpec as P

learn_rate = 0.01
beta_one = 0.9
beta_two = 0.95
adam_eps = 1e-08
decay_rate = 0.1
correct_one = 1.0 - 0.9**10
correct_two = 1.0 - 0.95**10

WORD = 32
LANES = 128
PIECES = 4
VMEM_LIMIT = 32 * 1024 * 1024
FLOPS = 5 * 10**8
LATE_FLOPS = 10 * 10**8
END_FLOPS = 100 * 10**8


def power_of_two(exponent, bits, start, sign):
    value = start
    for bit in range(bits):
        factor = 2.0 ** (sign * (1 << bit))
        value = value * jnp.where(((exponent >> bit) & 1) == 1, factor, 1.0)
    return value


def prepare_kernel(
    bits,
    ids_hbm,
    count_hbm,
    table_hbm,
    docs_hbm,
    weights_hbm,
    a_ref,
    b_ref,
    cast_ref,
    ids_ref,
    count_ref,
    table_ref,
    weights_ref,
    done,
):
    slots, docs = ids_ref.shape
    head = docs - b_ref.shape[0]
    fetches = [
        pltpu.make_async_copy(source, target, done.at[i])
        for i, (source, target) in enumerate(
            (
                (ids_hbm, ids_ref),
                (table_hbm, table_ref),
                (count_hbm, count_ref),
                (docs_hbm.at[pl.ds(0, head)], a_ref.at[pl.ds(0, head)]),
                (docs_hbm.at[pl.ds(head, docs - head)], b_ref),
                (weights_hbm, weights_ref),
            )
        )
    ]
    for fetch in fetches:
        fetch.start()
    for fetch in fetches[:3]:
        fetch.wait()
    pairs = table_ref.shape[0] // 2
    starts = range(0, docs, LANES)
    ids = [ids_ref[:, start : start + LANES] for start in starts]
    line_of = [(chunk >> 7) & (pairs - 1) for chunk in ids]
    lane_of = [chunk & (LANES - 1) for chunk in ids]

    def pick(t, found):
        both = table_ref[pl.ds(t, 1), :] | (table_ref[pl.ds(t + pairs, 1), :] << 16)
        line = jnp.broadcast_to(both, (slots, LANES))
        return tuple(
            jnp.where(line_of[i] == t, jnp.take_along_axis(line, lane_of[i], axis=1), found[i])
            for i in range(len(ids))
        )

    found = tuple(jnp.zeros((slots, LANES), jnp.int32) for _ in ids)
    if pairs <= 16:
        for t in range(pairs):
            found = pick(t, found)
    else:
        found = lax.fori_loop(0, pairs, pick, found, unroll=8)
    place = lax.broadcasted_iota(jnp.int32, (slots, LANES), 0)
    a_ref[head:, :] = jnp.zeros((slots // 2, a_ref.shape[1]), jnp.bfloat16)
    for i, start in enumerate(starts):
        row = jnp.where((ids[i] >> 7) < pairs, found[i], found[i] >> 16) & 0xFFFF
        low = (LANES + (row & (LANES - 1))).astype(jnp.float32)
        code = power_of_two(row >> 7, bits, low * 2.0**-64, 1)
        code = jnp.where(place < count_ref[:, start : start + LANES], code, 0.0)
        code = code.astype(jnp.bfloat16)
        a_ref[head:, start : start + LANES] = code[: slots // 2]
        a_ref[head:, docs + start : docs + start + LANES] = code[slots // 2 :]
    for fetch in fetches[3:]:
        fetch.wait()
    cast_ref[...] = weights_ref[...].astype(jnp.bfloat16) * 0.5


def prepare(label_slot, pos_ids, pos_count, embeddings, weights, head):
    docs, slots = pos_ids.shape
    width = embeddings.shape[1]
    lines = label_slot.shape[0] // LANES
    table = label_slot.reshape(lines, LANES)
    inputs = (pos_ids.T, pos_count.reshape(1, docs), table, embeddings, weights)
    return pl.pallas_call(
        functools.partial(prepare_kernel, (lines - 1).bit_length()),
        in_specs=[pl.BlockSpec(memory_space=pltpu.HBM)] * 5,
        out_specs=[pl.BlockSpec(memory_space=pltpu.VMEM)] * 3,
        out_shape=[
            jax.ShapeDtypeStruct((head + slots // 2, width), jnp.bfloat16),
            jax.ShapeDtypeStruct((docs - head, width), jnp.bfloat16),
            jax.ShapeDtypeStruct(weights.shape, jnp.bfloat16),
        ],
        scratch_shapes=[
            pltpu.VMEM((slots, docs), jnp.int32),
            pltpu.VMEM((1, docs), jnp.int32),
            pltpu.VMEM((lines, LANES), jnp.int32),
            pltpu.VMEM(weights.shape, jnp.float32),
            pltpu.SemaphoreType.DMA((6,)),
        ],
        compiler_params=pltpu.CompilerParams(vmem_limit_bytes=VMEM_LIMIT),
        name="prepare",
    )(*(pltpu.with_memory_space_constraint(x, pltpu.HBM) for x in inputs))


def signs_of(codes, owner, bits, height):
    docs = codes.shape[1]
    scale = power_of_two(owner * (height // LANES), bits, jnp.float32(2.0**64), -1)
    scaled = codes * scale
    place = jnp.left_shift(
        jnp.ones((WORD, docs), jnp.int32), lax.broadcasted_iota(jnp.int32, (WORD, docs), 0)
    )
    spread = []
    for part in range(height // LANES):
        row = jnp.minimum(scaled * 2.0**-part, 512.0).astype(jnp.int32) - LANES
        word = row >> 5
        bit = jnp.left_shift(jnp.ones_like(row), row & (WORD - 1))
        for w in range(LANES // WORD):
            line = jnp.sum(jnp.where(word == w, bit, 0), axis=0, keepdims=True)
            line = jnp.broadcast_to(line, (WORD, docs))
            spread.append(jnp.where((line & place) != 0, -1.0, 1.0))
    return jnp.concatenate(spread, axis=0)


def doubled_gradient(bits, owners, a_ref, b_ref, w_refs):
    height = w_refs[0].shape[0]
    head = b_ref.shape[0]
    number = 2 * head
    docs = jnp.concatenate([a_ref[:head, :], b_ref[...]], axis=0)
    codes = jnp.concatenate([a_ref[head:, :number], a_ref[head:, number : 2 * number]], axis=0)
    codes = codes.astype(jnp.float32)
    weights = jnp.concatenate([ref[...] for ref in w_refs], axis=0)
    halved = lax.dot_general(
        weights, docs, (((1,), (1,)), ((), ())), preferred_element_type=jnp.float32
    )
    me = lax.axis_index("blk")
    signs = jnp.concatenate([signs_of(codes, me ^ owner, bits, height) for owner in owners], axis=0)
    signal = (jnp.tanh(halved) + signs).astype(jnp.bfloat16)
    return jnp.dot(signal, docs, preferred_element_type=jnp.float32)


def gradient_kernel(bits, owners, fresh, a_ref, b_ref, *refs):
    blocks = len(owners)
    w_refs, refs = refs[:blocks], refs[blocks:]
    old_refs, new_refs = refs[:-blocks], refs[-blocks:]
    height = w_refs[0].shape[0]
    part = doubled_gradient(bits, owners, a_ref, b_ref, w_refs)
    for block in range(blocks):
        piece = part[block * height : (block + 1) * height]
        new_refs[block][...] = piece if fresh else old_refs[block][...] + piece


def add_gradient(bits, owners, a, b, weights, sums, flops):
    blocks = len(weights)
    height, width = weights[0].shape
    vmem = pl.BlockSpec(memory_space=pltpu.VMEM)
    sums = list(sums)
    inputs = [a, b, *weights, *sums]
    first_sum = len(inputs) - len(sums)
    return pl.pallas_call(
        functools.partial(gradient_kernel, bits, owners, not sums),
        in_specs=[vmem] * len(inputs),
        out_specs=[vmem] * blocks,
        out_shape=[jax.ShapeDtypeStruct((height, width), jnp.float32)] * blocks,
        input_output_aliases={first_sum + i: i for i in range(len(sums))},
        compiler_params=pltpu.CompilerParams(vmem_limit_bytes=VMEM_LIMIT),
        cost_estimate=pl.CostEstimate(flops=flops, bytes_accessed=10**6, transcendentals=0),
        name="gradient",
    )(*inputs)


def finish_kernel(
    bits,
    a_ref,
    b_ref,
    cast_ref,
    sum_ref,
    other_ref,
    weights_ref,
    first_ref,
    second_ref,
    weights_hbm,
    first_hbm,
    second_hbm,
    weights_out,
    first_out,
    second_out,
    done,
):
    part = doubled_gradient(bits, (0,), a_ref, b_ref, [cast_ref])
    height = part.shape[0]
    size = height // PIECES
    writes = []
    for i in range(PIECES):
        here = pl.ds(i * size, size)
        gradient = 0.5 * (sum_ref[here, :] + other_ref[here, :] + part[i * size : (i + 1) * size])
        new_weights, new_first, new_second = adam_step(
            weights_ref[here, :], first_ref[here, :], second_ref[here, :], gradient
        )
        for k, (value, out, hbm) in enumerate(
            (
                (new_first, first_out, first_hbm),
                (new_second, second_out, second_hbm),
                (new_weights, weights_out, weights_hbm),
            )
        ):
            out[here, :] = value
            write = pltpu.make_async_copy(out.at[here], hbm.at[here], done.at[i, k])
            write.start()
            writes.append(write)
    for write in writes:
        write.wait()


def finish(bits, a, b, cast, mine_sum, other_sum, weights, first_moment, second_moment):
    shape = jax.ShapeDtypeStruct(weights.shape, jnp.float32)
    return pl.pallas_call(
        functools.partial(finish_kernel, bits),
        in_specs=[pl.BlockSpec(memory_space=pltpu.VMEM)] * 8,
        out_specs=[pl.BlockSpec(memory_space=pltpu.HBM)] * 3,
        out_shape=[shape] * 3,
        scratch_shapes=[pltpu.VMEM(weights.shape, jnp.float32)] * 3
        + [pltpu.SemaphoreType.DMA((PIECES, 3))],
        compiler_params=pltpu.CompilerParams(vmem_limit_bytes=VMEM_LIMIT),
        cost_estimate=pl.CostEstimate(flops=END_FLOPS, bytes_accessed=10**6, transcendentals=0),
        name="finish",
    )(a, b, cast, mine_sum, other_sum, weights, first_moment, second_moment)


def adam_step(weights, first_moment, second_moment, gradient):
    new_first = beta_one * first_moment + (1.0 - beta_one) * gradient
    new_second = beta_two * second_moment + (1.0 - beta_two) * gradient * gradient
    update = new_first / correct_one / (jnp.sqrt(new_second / correct_two) + adam_eps)
    new_weights = weights - learn_rate * (update + decay_rate * weights)
    return (new_weights, new_first, new_second)


def ring_of(blocks, across):
    path = list(range(0, blocks // 2, across))
    if across == 2:
        path += list(range(1, blocks // 2, 2))[::-1]
    steps = zip(path, path[1:] + path[:1])
    return [(2 * here + core, 2 * there + core) for here, there in steps for core in range(2)]


together = lax.optimization_barrier


def per_device(
    blocks,
    across,
    embeddings,
    pos_ids,
    pos_count,
    label_slot,
    weights,
    first_moment,
    second_moment,
):
    half_way = blocks // 4
    up = ring_of(blocks, across)
    down = [(there, here) for here, there in up]
    swap = [(i, i ^ 1) for i in range(blocks)]
    bits = (label_slot.shape[0] // LANES - 1).bit_length()
    head = embeddings.shape[0] // 2

    def send(value, pairs):
        return lax.ppermute(value, "blk", pairs)

    a, b, mine = prepare(label_slot, pos_ids, pos_count, embeddings, weights, head)
    coming = {"up_b": send(b, up), "down_a": send(a, down)}
    coming |= {"up_a": send(a, up), "down_b": send(b, down)}
    cast = [mine, send(mine, swap)]
    sums = ()
    waiting = [(a, b)]

    def work(flops):
        return add_gradient(bits, (0, 1), *waiting.pop(0), cast, sums, flops)

    for step in range(1, half_way):
        last = step == half_way - 1
        came = {}
        for message in ("up_b", "down_a", "up_a", "down_b"):
            came[message], waiting, sums = together((coming.pop(message), waiting, sums))
            if message in ("up_b", "down_a") or not last:
                coming[message] = send(came[message], up if message in ("up_a", "up_b") else down)
            if message in ("up_a", "down_b"):
                side = message.split("_")[0]
                waiting.append((came[side + "_a"], came[side + "_b"]))
            if waiting and (last or (step > 1 and message != "down_b")):
                sums = work(LATE_FLOPS if last else FLOPS)
    while waiting:
        sums = work(LATE_FLOPS)
    mine_sum, other_sum = sums
    got = send(other_sum, swap)
    last_b, mine_sum = together((coming["up_b"], mine_sum))
    beside_b = send(last_b, swap)
    last_a, mine_sum = together((coming["down_a"], mine_sum))
    beside_a = send(last_a, swap)
    (mine_sum,) = add_gradient(bits, (0,), last_a, last_b, [mine], [mine_sum], END_FLOPS)
    state = (weights, first_moment, second_moment)
    return finish(bits, beside_a, beside_b, mine, mine_sum, got, *state)


def solution(mesh):
    in_specs = (
        P(("groups", "blk"), None),
        P(("groups", "blk"), None),
        P(("groups", "blk")),
        P(),
        P("blk", None),
        P("blk", None),
        P("blk", None),
    )
    out_specs = (P(("groups", "blk"), None), P(("groups", "blk"), None), P(("groups", "blk"), None))
    return jax.shard_map(
        functools.partial(per_device, mesh.shape["blk"], 4 // mesh.shape["groups"]),
        mesh=mesh,
        in_specs=in_specs,
        out_specs=out_specs,
        check_vma=False,
    )
```

```python
import functools

import jax
import jax.numpy as jnp
from jax import lax
from jax.experimental import pallas as pl
from jax.experimental.pallas import tpu as pltpu
from jax.sharding import PartitionSpec as P

learn_rate = 0.01
beta_one = 0.9
beta_two = 0.95
adam_eps = 1e-08
decay_rate = 0.1
correct_one = 1.0 - 0.9**10
correct_two = 1.0 - 0.95**10

WORD = 32
LANES = 128
PIECE = 32
VMEM_LIMIT = 32 * 1024 * 1024
FLOPS = 5 * 10**8
LATE_FLOPS = 10 * 10**8
END_FLOPS = 100 * 10**8


def power_of_two(exponent, bits, start, sign):
    value = start
    for bit in range(bits):
        factor = 2.0 ** (sign * (1 << bit))
        value = value * jnp.where(((exponent >> bit) & 1) == 1, factor, 1.0)
    return value


def prepare_kernel(
    bits,
    ids_hbm,
    count_hbm,
    table_hbm,
    docs_hbm,
    weights_hbm,
    a_ref,
    b_ref,
    cast_ref,
    ids_ref,
    count_ref,
    table_ref,
    weights_ref,
    done,
):
    slots, docs = ids_ref.shape
    head = docs - b_ref.shape[0]
    fetches = [
        pltpu.make_async_copy(source, target, done.at[i])
        for i, (source, target) in enumerate(
            (
                (ids_hbm, ids_ref),
                (table_hbm, table_ref),
                (count_hbm, count_ref),
                (docs_hbm.at[pl.ds(0, head)], a_ref.at[pl.ds(0, head)]),
                (docs_hbm.at[pl.ds(head, docs - head)], b_ref),
                (weights_hbm, weights_ref),
            )
        )
    ]
    for fetch in fetches:
        fetch.start()
    for fetch in fetches[:3]:
        fetch.wait()
    pairs = table_ref.shape[0] // 2
    starts = range(0, docs, LANES)
    ids = [ids_ref[:, start : start + LANES] for start in starts]
    line_of = [(chunk >> 7) & (pairs - 1) for chunk in ids]
    lane_of = [chunk & (LANES - 1) for chunk in ids]

    def pick(t, found):
        both = table_ref[pl.ds(t, 1), :] | (table_ref[pl.ds(t + pairs, 1), :] << 16)
        line = jnp.broadcast_to(both, (slots, LANES))
        return tuple(
            jnp.where(line_of[i] == t, jnp.take_along_axis(line, lane_of[i], axis=1), found[i])
            for i in range(len(ids))
        )

    found = tuple(jnp.zeros((slots, LANES), jnp.int32) for _ in ids)
    if pairs <= 16:
        for t in range(pairs):
            found = pick(t, found)
    else:
        found = lax.fori_loop(0, pairs, pick, found, unroll=8)
    place = lax.broadcasted_iota(jnp.int32, (slots, LANES), 0)
    a_ref[head:, :] = jnp.zeros((slots // 2, a_ref.shape[1]), jnp.bfloat16)
    for i, start in enumerate(starts):
        row = jnp.where((ids[i] >> 7) < pairs, found[i], found[i] >> 16) & 0xFFFF
        low = (LANES + (row & (LANES - 1))).astype(jnp.float32)
        code = power_of_two(row >> 7, bits, low * 2.0**-64, 1)
        code = jnp.where(place < count_ref[:, start : start + LANES], code, 0.0)
        code = code.astype(jnp.bfloat16)
        a_ref[head:, start : start + LANES] = code[: slots // 2]
        a_ref[head:, docs + start : docs + start + LANES] = code[slots // 2 :]
    for fetch in fetches[3:]:
        fetch.wait()
    cast_ref[...] = weights_ref[...].astype(jnp.bfloat16) * 0.5


def prepare(label_slot, pos_ids, pos_count, embeddings, weights, head):
    docs, slots = pos_ids.shape
    width = embeddings.shape[1]
    lines = label_slot.shape[0] // LANES
    table = label_slot.reshape(lines, LANES)
    inputs = (pos_ids.T, pos_count.reshape(1, docs), table, embeddings, weights)
    return pl.pallas_call(
        functools.partial(prepare_kernel, (lines - 1).bit_length()),
        in_specs=[pl.BlockSpec(memory_space=pltpu.HBM)] * 5,
        out_specs=[pl.BlockSpec(memory_space=pltpu.VMEM)] * 3,
        out_shape=[
            jax.ShapeDtypeStruct((head + slots // 2, width), jnp.bfloat16),
            jax.ShapeDtypeStruct((docs - head, width), jnp.bfloat16),
            jax.ShapeDtypeStruct(weights.shape, jnp.bfloat16),
        ],
        scratch_shapes=[
            pltpu.VMEM((slots, docs), jnp.int32),
            pltpu.VMEM((1, docs), jnp.int32),
            pltpu.VMEM((lines, LANES), jnp.int32),
            pltpu.VMEM(weights.shape, jnp.float32),
            pltpu.SemaphoreType.DMA((6,)),
        ],
        compiler_params=pltpu.CompilerParams(vmem_limit_bytes=VMEM_LIMIT),
        name="prepare",
    )(*(pltpu.with_memory_space_constraint(x, pltpu.HBM) for x in inputs))


def signs_of(codes, owner, bits, height, parts):
    docs = codes.shape[1]
    scale = power_of_two(owner * (height // LANES), bits, jnp.float32(2.0**64), -1)
    scaled = codes * scale
    place = jnp.left_shift(
        jnp.ones((WORD, docs), jnp.int32), lax.broadcasted_iota(jnp.int32, (WORD, docs), 0)
    )
    spread = []
    for part in parts:
        row = jnp.minimum(scaled * 2.0**-part, 512.0).astype(jnp.int32) - LANES
        word = row >> 5
        bit = jnp.left_shift(jnp.ones_like(row), row & (WORD - 1))
        for w in range(LANES // WORD):
            line = jnp.sum(jnp.where(word == w, bit, 0), axis=0, keepdims=True)
            line = jnp.broadcast_to(line, (WORD, docs))
            spread.append(jnp.where((line & place) != 0, -1.0, 1.0))
    return jnp.concatenate(spread, axis=0)


def doubled_gradient(bits, owners, a_ref, b_ref, w_refs, parts=None):
    height = w_refs[0].shape[0]
    head = b_ref.shape[0]
    number = 2 * head
    docs = jnp.concatenate([a_ref[:head, :], b_ref[...]], axis=0)
    codes = jnp.concatenate([a_ref[head:, :number], a_ref[head:, number : 2 * number]], axis=0)
    codes = codes.astype(jnp.float32)
    parts = range(height // LANES) if parts is None else parts
    weights = jnp.concatenate(
        [ref[part * LANES : (part + 1) * LANES, :] for ref in w_refs for part in parts], axis=0
    )
    halved = lax.dot_general(
        weights, docs, (((1,), (1,)), ((), ())), preferred_element_type=jnp.float32
    )
    me = lax.axis_index("blk")
    signs = jnp.concatenate(
        [signs_of(codes, me ^ owner, bits, height, parts) for owner in owners], axis=0
    )
    signal = (jnp.tanh(halved) + signs).astype(jnp.bfloat16)
    return jnp.dot(signal, docs, preferred_element_type=jnp.float32)


def gradient_kernel(bits, owners, fresh, a_ref, b_ref, *refs):
    blocks = len(owners)
    w_refs, refs = refs[:blocks], refs[blocks:]
    old_refs, new_refs = refs[:-blocks], refs[-blocks:]
    height = w_refs[0].shape[0]
    part = doubled_gradient(bits, owners, a_ref, b_ref, w_refs)
    for block in range(blocks):
        piece = part[block * height : (block + 1) * height]
        new_refs[block][...] = piece if fresh else old_refs[block][...] + piece


def add_gradient(bits, owners, a, b, weights, sums, flops):
    blocks = len(weights)
    height, width = weights[0].shape
    vmem = pl.BlockSpec(memory_space=pltpu.VMEM)
    sums = list(sums)
    inputs = [a, b, *weights, *sums]
    first_sum = len(inputs) - len(sums)
    return pl.pallas_call(
        functools.partial(gradient_kernel, bits, owners, not sums),
        in_specs=[vmem] * len(inputs),
        out_specs=[vmem] * blocks,
        out_shape=[jax.ShapeDtypeStruct((height, width), jnp.float32)] * blocks,
        input_output_aliases={first_sum + i: i for i in range(len(sums))},
        compiler_params=pltpu.CompilerParams(vmem_limit_bytes=VMEM_LIMIT),
        cost_estimate=pl.CostEstimate(flops=flops, bytes_accessed=10**6, transcendentals=0),
        name="gradient",
    )(*inputs)


def finish_kernel(
    bits,
    a_ref,
    b_ref,
    cast_ref,
    sum_ref,
    other_ref,
    weights_ref,
    first_ref,
    second_ref,
    weights_hbm,
    first_hbm,
    second_hbm,
    weights_out,
    first_out,
    second_out,
    done,
):
    writes = []
    for i in range(sum_ref.shape[0] // PIECE):
        start = i * PIECE
        here = pl.ds(start, PIECE)
        if start % LANES == 0:
            part = doubled_gradient(bits, (0,), a_ref, b_ref, [cast_ref], [start // LANES])
        piece = part[start % LANES : start % LANES + PIECE]
        gradient = 0.5 * (sum_ref[here, :] + other_ref[here, :] + piece)
        new_weights, new_first, new_second = adam_step(
            weights_ref[here, :], first_ref[here, :], second_ref[here, :], gradient
        )
        for k, (value, out, hbm) in enumerate(
            (
                (new_first, first_out, first_hbm),
                (new_second, second_out, second_hbm),
                (new_weights, weights_out, weights_hbm),
            )
        ):
            out[here, :] = value
            write = pltpu.make_async_copy(out.at[here], hbm.at[here], done.at[i, k])
            write.start()
            writes.append(write)
    for write in writes:
        write.wait()


def finish(bits, a, b, cast, mine_sum, other_sum, weights, first_moment, second_moment):
    shape = jax.ShapeDtypeStruct(weights.shape, jnp.float32)
    return pl.pallas_call(
        functools.partial(finish_kernel, bits),
        in_specs=[pl.BlockSpec(memory_space=pltpu.VMEM)] * 8,
        out_specs=[pl.BlockSpec(memory_space=pltpu.HBM)] * 3,
        out_shape=[shape] * 3,
        scratch_shapes=[pltpu.VMEM(weights.shape, jnp.float32)] * 3
        + [pltpu.SemaphoreType.DMA((weights.shape[0] // PIECE, 3))],
        compiler_params=pltpu.CompilerParams(vmem_limit_bytes=VMEM_LIMIT),
        cost_estimate=pl.CostEstimate(flops=END_FLOPS, bytes_accessed=10**6, transcendentals=0),
        name="finish",
    )(a, b, cast, mine_sum, other_sum, weights, first_moment, second_moment)


def adam_step(weights, first_moment, second_moment, gradient):
    new_first = beta_one * first_moment + (1.0 - beta_one) * gradient
    new_second = beta_two * second_moment + (1.0 - beta_two) * gradient * gradient
    update = new_first / correct_one / (jnp.sqrt(new_second / correct_two) + adam_eps)
    new_weights = weights - learn_rate * (update + decay_rate * weights)
    return (new_weights, new_first, new_second)


def ring_of(blocks, across):
    path = list(range(0, blocks // 2, across))
    if across == 2:
        path += list(range(1, blocks // 2, 2))[::-1]
    steps = zip(path, path[1:] + path[:1])
    return [(2 * here + core, 2 * there + core) for here, there in steps for core in range(2)]


together = lax.optimization_barrier


def per_device(
    blocks,
    across,
    embeddings,
    pos_ids,
    pos_count,
    label_slot,
    weights,
    first_moment,
    second_moment,
):
    half_way = blocks // 4
    up = ring_of(blocks, across)
    down = [(there, here) for here, there in up]
    swap = [(i, i ^ 1) for i in range(blocks)]
    bits = (label_slot.shape[0] // LANES - 1).bit_length()
    head = embeddings.shape[0] // 2

    def send(value, pairs):
        return lax.ppermute(value, "blk", pairs)

    a, b, mine = prepare(label_slot, pos_ids, pos_count, embeddings, weights, head)
    coming = {"up_b": send(b, up), "down_a": send(a, down)}
    coming |= {"up_a": send(a, up), "down_b": send(b, down)}
    cast = [mine, send(mine, swap)]
    sums = ()
    waiting = [(a, b)]

    def work(flops):
        return add_gradient(bits, (0, 1), *waiting.pop(0), cast, sums, flops)

    for step in range(1, half_way):
        last = step == half_way - 1
        came = {}
        for message in ("up_b", "down_a", "up_a", "down_b"):
            came[message], waiting, sums = together((coming.pop(message), waiting, sums))
            if message in ("up_b", "down_a") or not last:
                coming[message] = send(came[message], up if message in ("up_a", "up_b") else down)
            if message in ("up_a", "down_b"):
                side = message.split("_")[0]
                waiting.append((came[side + "_a"], came[side + "_b"]))
            if waiting and (last or (step > 1 and message != "down_b")):
                sums = work(LATE_FLOPS if last else FLOPS)
    while waiting:
        sums = work(LATE_FLOPS)
    mine_sum, other_sum = sums
    got = send(other_sum, swap)
    last_b, mine_sum = together((coming["up_b"], mine_sum))
    beside_b = send(last_b, swap)
    last_a, mine_sum = together((coming["down_a"], mine_sum))
    beside_a = send(last_a, swap)
    (mine_sum,) = add_gradient(bits, (0,), last_a, last_b, [mine], [mine_sum], END_FLOPS)
    state = (weights, first_moment, second_moment)
    return finish(bits, beside_a, beside_b, mine, mine_sum, got, *state)


def solution(mesh):
    in_specs = (
        P(("groups", "blk"), None),
        P(("groups", "blk"), None),
        P(("groups", "blk")),
        P(),
        P("blk", None),
        P("blk", None),
        P("blk", None),
    )
    out_specs = (P(("groups", "blk"), None), P(("groups", "blk"), None), P(("groups", "blk"), None))
    return jax.shard_map(
        functools.partial(per_device, mesh.shape["blk"], 4 // mesh.shape["groups"]),
        mesh=mesh,
        in_specs=in_specs,
        out_specs=out_specs,
        check_vma=False,
    )
```

```python
import functools
import math

import jax
import jax.numpy as jnp
from jax import lax
from jax.experimental import pallas as pl
from jax.experimental.pallas import tpu as pltpu
from jax.sharding import PartitionSpec as P

learn_rate = 0.01
beta_one = 0.9
beta_two = 0.95
adam_eps = 1e-08
decay_rate = 0.1
correct_one = 1.0 - 0.9**10
correct_two = 1.0 - 0.95**10

WORD = 32
LANES = 128
PIECES = 4
VMEM_LIMIT = 32 * 1024 * 1024
FLOPS = 5 * 10**8
LATE_FLOPS = 10 * 10**8
END_FLOPS = 100 * 10**8


def power_of_two(exponent, bits, start, sign):
    value = start
    for bit in range(bits):
        factor = 2.0 ** (sign * (1 << bit))
        value = value * jnp.where(((exponent >> bit) & 1) == 1, factor, 1.0)
    return value


def prepare_kernel(
    bits,
    ids_hbm,
    count_hbm,
    table_hbm,
    docs_hbm,
    a_ref,
    b_ref,
    ids_ref,
    count_ref,
    table_ref,
    done,
):
    slots, docs = ids_ref.shape
    head = docs - b_ref.shape[0]
    fetches = [
        pltpu.make_async_copy(source, target, done.at[i])
        for i, (source, target) in enumerate(
            (
                (ids_hbm, ids_ref),
                (table_hbm, table_ref),
                (count_hbm, count_ref),
                (docs_hbm.at[pl.ds(0, head)], a_ref.at[pl.ds(0, head)]),
                (docs_hbm.at[pl.ds(head, docs - head)], b_ref),
            )
        )
    ]
    for fetch in fetches:
        fetch.start()
    for fetch in fetches[:3]:
        fetch.wait()
    pairs = table_ref.shape[0] // 2
    starts = range(0, docs, LANES)
    ids = [ids_ref[:, start : start + LANES] for start in starts]
    line_of = [(chunk >> 7) & (pairs - 1) for chunk in ids]
    lane_of = [chunk & (LANES - 1) for chunk in ids]

    def pick(t, found):
        both = table_ref[pl.ds(t, 1), :] | (table_ref[pl.ds(t + pairs, 1), :] << 16)
        line = jnp.broadcast_to(both, (slots, LANES))
        return tuple(
            jnp.where(line_of[i] == t, jnp.take_along_axis(line, lane_of[i], axis=1), found[i])
            for i in range(len(ids))
        )

    found = tuple(jnp.zeros((slots, LANES), jnp.int32) for _ in ids)
    if pairs <= 16:
        for t in range(pairs):
            found = pick(t, found)
    else:
        found = lax.fori_loop(0, pairs, pick, found, unroll=8)
    place = lax.broadcasted_iota(jnp.int32, (slots, LANES), 0)
    a_ref[head:, :] = jnp.zeros((slots // 2, a_ref.shape[1]), jnp.bfloat16)
    for i, start in enumerate(starts):
        row = jnp.where((ids[i] >> 7) < pairs, found[i], found[i] >> 16) & 0xFFFF
        low = (LANES + (row & (LANES - 1))).astype(jnp.float32)
        code = power_of_two(row >> 7, bits, low * 2.0**-64, 1)
        code = jnp.where(place < count_ref[:, start : start + LANES], code, 0.0)
        code = code.astype(jnp.bfloat16)
        a_ref[head:, start : start + LANES] = code[: slots // 2]
        a_ref[head:, docs + start : docs + start + LANES] = code[slots // 2 :]
    for fetch in fetches[3:]:
        fetch.wait()


def prepare(label_slot, pos_ids, pos_count, embeddings, head):
    docs, slots = pos_ids.shape
    width = embeddings.shape[1]
    lines = label_slot.shape[0] // LANES
    table = label_slot.reshape(lines, LANES)
    inputs = (pos_ids.T, pos_count.reshape(1, docs), table, embeddings)
    return pl.pallas_call(
        functools.partial(prepare_kernel, (lines - 1).bit_length()),
        in_specs=[pl.BlockSpec(memory_space=pltpu.HBM)] * 4,
        out_specs=[pl.BlockSpec(memory_space=pltpu.VMEM)] * 2,
        out_shape=[
            jax.ShapeDtypeStruct((head + slots // 2, width), jnp.bfloat16),
            jax.ShapeDtypeStruct((docs - head, width), jnp.bfloat16),
        ],
        scratch_shapes=[
            pltpu.VMEM((slots, docs), jnp.int32),
            pltpu.VMEM((1, docs), jnp.int32),
            pltpu.VMEM((lines, LANES), jnp.int32),
            pltpu.SemaphoreType.DMA((5,)),
        ],
        compiler_params=pltpu.CompilerParams(vmem_limit_bytes=VMEM_LIMIT),
        name="prepare",
    )(*(pltpu.with_memory_space_constraint(x, pltpu.HBM) for x in inputs))


def cast_kernel(weights_ref, cast_ref):
    cast_ref[...] = weights_ref[...].astype(jnp.bfloat16) * 0.5


def halved_cast(weights):
    return pl.pallas_call(
        cast_kernel,
        in_specs=[pl.BlockSpec(memory_space=pltpu.VMEM)],
        out_specs=pl.BlockSpec(memory_space=pltpu.VMEM),
        out_shape=jax.ShapeDtypeStruct(weights.shape, jnp.bfloat16),
        compiler_params=pltpu.CompilerParams(vmem_limit_bytes=VMEM_LIMIT),
        name="cast",
    )(weights)


def signs_of(codes, owner, bits, height):
    docs = codes.shape[1]
    scale = power_of_two(owner * (height // LANES), bits, jnp.float32(2.0**64), -1)
    scaled = codes * scale
    place = jnp.left_shift(
        jnp.ones((WORD, docs), jnp.int32), lax.broadcasted_iota(jnp.int32, (WORD, docs), 0)
    )
    spread = []
    for part in range(height // LANES):
        row = jnp.minimum(scaled * 2.0**-part, 512.0).astype(jnp.int32) - LANES
        word = row >> 5
        bit = jnp.left_shift(jnp.ones_like(row), row & (WORD - 1))
        for w in range(LANES // WORD):
            line = jnp.sum(jnp.where(word == w, bit, 0), axis=0, keepdims=True)
            line = jnp.broadcast_to(line, (WORD, docs))
            spread.append(jnp.where((line & place) != 0, -1.0, 1.0))
    return jnp.concatenate(spread, axis=0)


def doubled_gradient(bits, owners, a_ref, b_ref, w_refs):
    height = w_refs[0].shape[0]
    head = b_ref.shape[0]
    number = 2 * head
    docs = jnp.concatenate([a_ref[:head, :], b_ref[...]], axis=0)
    codes = jnp.concatenate([a_ref[head:, :number], a_ref[head:, number : 2 * number]], axis=0)
    codes = codes.astype(jnp.float32)
    weights = jnp.concatenate([ref[...] for ref in w_refs], axis=0)
    halved = lax.dot_general(
        weights, docs, (((1,), (1,)), ((), ())), preferred_element_type=jnp.float32
    )
    me = lax.axis_index("blk")
    signs = jnp.concatenate([signs_of(codes, me ^ owner, bits, height) for owner in owners], axis=0)
    signal = (jnp.tanh(halved) + signs).astype(jnp.bfloat16)
    return jnp.dot(signal, docs, preferred_element_type=jnp.float32)


def gradient_kernel(bits, owners, fresh, a_ref, b_ref, *refs):
    blocks = len(owners)
    w_refs, refs = refs[:blocks], refs[blocks:]
    old_refs, new_refs = refs[:-blocks], refs[-blocks:]
    height = w_refs[0].shape[0]
    part = doubled_gradient(bits, owners, a_ref, b_ref, w_refs)
    for block in range(blocks):
        piece = part[block * height : (block + 1) * height]
        new_refs[block][...] = piece if fresh else old_refs[block][...] + piece


def add_gradient(bits, owners, a, b, weights, sums, flops):
    blocks = len(weights)
    height, width = weights[0].shape
    vmem = pl.BlockSpec(memory_space=pltpu.VMEM)
    sums = list(sums)
    inputs = [a, b, *weights, *sums]
    first_sum = len(inputs) - len(sums)
    return pl.pallas_call(
        functools.partial(gradient_kernel, bits, owners, not sums),
        in_specs=[vmem] * len(inputs),
        out_specs=[vmem] * blocks,
        out_shape=[jax.ShapeDtypeStruct((height, width), jnp.float32)] * blocks,
        input_output_aliases={first_sum + i: i for i in range(len(sums))},
        compiler_params=pltpu.CompilerParams(vmem_limit_bytes=VMEM_LIMIT),
        cost_estimate=pl.CostEstimate(flops=flops, bytes_accessed=10**6, transcendentals=0),
        name="gradient",
    )(*inputs)


def finish_kernel(
    bits,
    a_ref,
    b_ref,
    cast_ref,
    sum_ref,
    other_ref,
    weights_ref,
    first_ref,
    second_ref,
    weights_hbm,
    first_hbm,
    second_hbm,
    weights_out,
    first_out,
    second_out,
    done,
):
    part = doubled_gradient(bits, (0,), a_ref, b_ref, [cast_ref])
    height = part.shape[0]
    size = height // PIECES
    writes = []
    for i in range(PIECES):
        here = pl.ds(i * size, size)
        doubled = sum_ref[here, :] + other_ref[here, :] + part[i * size : (i + 1) * size]
        new_weights, new_first, new_second = adam_step(
            weights_ref[here, :], first_ref[here, :], second_ref[here, :], doubled
        )
        for k, (value, out, hbm) in enumerate(
            (
                (new_first, first_out, first_hbm),
                (new_second, second_out, second_hbm),
                (new_weights, weights_out, weights_hbm),
            )
        ):
            out[here, :] = value
            write = pltpu.make_async_copy(out.at[here], hbm.at[here], done.at[i, k])
            write.start()
            writes.append(write)
    for write in writes:
        write.wait()


def finish(bits, a, b, cast, mine_sum, other_sum, weights, first_moment, second_moment):
    shape = jax.ShapeDtypeStruct(weights.shape, jnp.float32)
    return pl.pallas_call(
        functools.partial(finish_kernel, bits),
        in_specs=[pl.BlockSpec(memory_space=pltpu.VMEM)] * 8,
        out_specs=[pl.BlockSpec(memory_space=pltpu.HBM)] * 3,
        out_shape=[shape] * 3,
        scratch_shapes=[pltpu.VMEM(weights.shape, jnp.float32)] * 3
        + [pltpu.SemaphoreType.DMA((PIECES, 3))],
        compiler_params=pltpu.CompilerParams(vmem_limit_bytes=VMEM_LIMIT),
        cost_estimate=pl.CostEstimate(flops=END_FLOPS, bytes_accessed=10**6, transcendentals=0),
        name="finish",
    )(a, b, cast, mine_sum, other_sum, weights, first_moment, second_moment)


def adam_step(weights, first_moment, second_moment, doubled):
    new_first = beta_one * first_moment + ((1.0 - beta_one) * 0.5) * doubled
    new_second = beta_two * second_moment + ((1.0 - beta_two) * 0.25) * (doubled * doubled)
    steep = correct_one / (learn_rate * math.sqrt(correct_two))
    update = new_first / (jnp.sqrt(new_second) * steep + correct_one * adam_eps / learn_rate)
    new_weights = weights * (1.0 - learn_rate * decay_rate) - update
    return (new_weights, new_first, new_second)


def ring_of(blocks, across):
    path = list(range(0, blocks // 2, across))
    if across == 2:
        path += list(range(1, blocks // 2, 2))[::-1]
    steps = zip(path, path[1:] + path[:1])
    return [(2 * here + core, 2 * there + core) for here, there in steps for core in range(2)]


together = lax.optimization_barrier


def per_device(
    blocks,
    across,
    embeddings,
    pos_ids,
    pos_count,
    label_slot,
    weights,
    first_moment,
    second_moment,
):
    half_way = blocks // 4
    up = ring_of(blocks, across)
    down = [(there, here) for here, there in up]
    swap = [(i, i ^ 1) for i in range(blocks)]
    bits = (label_slot.shape[0] // LANES - 1).bit_length()
    head = embeddings.shape[0] // 2

    def send(value, pairs):
        return lax.ppermute(value, "blk", pairs)

    a, b = prepare(label_slot, pos_ids, pos_count, embeddings, head)
    coming = {"up_b": send(b, up), "down_a": send(a, down)}
    coming |= {"up_a": send(a, up), "down_b": send(b, down)}
    mine = halved_cast(weights)
    cast = [mine, send(mine, swap)]
    sums = ()
    waiting = [(a, b)]

    def work(flops):
        return add_gradient(bits, (0, 1), *waiting.pop(0), cast, sums, flops)

    for step in range(1, half_way):
        last = step == half_way - 1
        came = {}
        for message in ("up_b", "down_a", "up_a", "down_b"):
            came[message], waiting, sums = together((coming.pop(message), waiting, sums))
            if message in ("up_b", "down_a") or not last:
                coming[message] = send(came[message], up if message in ("up_a", "up_b") else down)
            if message in ("up_a", "down_b"):
                side = message.split("_")[0]
                waiting.append((came[side + "_a"], came[side + "_b"]))
            if waiting and (last or (step > 1 and message != "down_b")):
                sums = work(LATE_FLOPS if last else FLOPS)
    while waiting:
        sums = work(LATE_FLOPS)
    mine_sum, other_sum = sums
    got = send(other_sum, swap)
    last_b, mine_sum = together((coming["up_b"], mine_sum))
    beside_b = send(last_b, swap)
    last_a, mine_sum = together((coming["down_a"], mine_sum))
    beside_a = send(last_a, swap)
    (mine_sum,) = add_gradient(bits, (0,), last_a, last_b, [mine], [mine_sum], END_FLOPS)
    state = (weights, first_moment, second_moment)
    return finish(bits, beside_a, beside_b, mine, mine_sum, got, *state)


def solution(mesh):
    in_specs = (
        P(("groups", "blk"), None),
        P(("groups", "blk"), None),
        P(("groups", "blk")),
        P(),
        P("blk", None),
        P("blk", None),
        P("blk", None),
    )
    out_specs = (P(("groups", "blk"), None), P(("groups", "blk"), None), P(("groups", "blk"), None))
    return jax.shard_map(
        functools.partial(per_device, mesh.shape["blk"], 4 // mesh.shape["groups"]),
        mesh=mesh,
        in_specs=in_specs,
        out_specs=out_specs,
        check_vma=False,
    )
```

```python
import functools
import math

import jax
import jax.numpy as jnp
from jax import lax
from jax.experimental import pallas as pl
from jax.experimental.pallas import tpu as pltpu
from jax.sharding import PartitionSpec as P

learn_rate = 0.01
beta_one = 0.9
beta_two = 0.95
adam_eps = 1e-08
decay_rate = 0.1
correct_one = 1.0 - 0.9**10
correct_two = 1.0 - 0.95**10

WORD = 32
LANES = 128
PIECES = 4
VMEM_LIMIT = 32 * 1024 * 1024
FLOPS = 2 * 10**8
LATE_FLOPS = 10 * 10**8
END_FLOPS = 100 * 10**8


def power_of_two(exponent, bits, start, sign):
    value = start
    for bit in range(bits):
        factor = 2.0 ** (sign * (1 << bit))
        value = value * jnp.where(((exponent >> bit) & 1) == 1, factor, 1.0)
    return value


def prepare_kernel(
    bits,
    ids_hbm,
    count_hbm,
    table_hbm,
    docs_hbm,
    a_ref,
    b_ref,
    ids_ref,
    count_ref,
    table_ref,
    done,
):
    slots, docs = ids_ref.shape
    head = docs - b_ref.shape[0]
    tiles = [pl.ds(start, LANES) for start in range(0, b_ref.shape[1], LANES)]
    fetches = [
        pltpu.make_async_copy(source, target, done.at[i])
        for i, (source, target) in enumerate(
            (
                (ids_hbm, ids_ref),
                (table_hbm, table_ref),
                (count_hbm, count_ref),
                (docs_hbm.at[pl.ds(head, docs - head)], b_ref),
                *(
                    (docs_hbm.at[pl.ds(0, head), tile], a_ref.at[pl.ds(j * head, head)])
                    for j, tile in enumerate(tiles)
                ),
            )
        )
    ]
    for fetch in fetches:
        fetch.start()
    for fetch in fetches[:3]:
        fetch.wait()
    pairs = table_ref.shape[0] // 2
    starts = range(0, docs, LANES)
    ids = [ids_ref[:, start : start + LANES] for start in starts]
    line_of = [(chunk >> 7) & (pairs - 1) for chunk in ids]
    lane_of = [chunk & (LANES - 1) for chunk in ids]

    def pick(t, found):
        both = table_ref[pl.ds(t, 1), :] | (table_ref[pl.ds(t + pairs, 1), :] << 16)
        line = jnp.broadcast_to(both, (slots, LANES))
        return tuple(
            jnp.where(line_of[i] == t, jnp.take_along_axis(line, lane_of[i], axis=1), found[i])
            for i in range(len(ids))
        )

    found = tuple(jnp.zeros((slots, LANES), jnp.int32) for _ in ids)
    if pairs <= 16:
        for t in range(pairs):
            found = pick(t, found)
    else:
        found = lax.fori_loop(0, pairs, pick, found, unroll=8)
    place = lax.broadcasted_iota(jnp.int32, (slots, LANES), 0)
    for i, start in enumerate(starts):
        row = jnp.where((ids[i] >> 7) < pairs, found[i], found[i] >> 16) & 0xFFFF
        low = (LANES + (row & (LANES - 1))).astype(jnp.float32)
        code = power_of_two(row >> 7, bits, low * 2.0**-64, 1)
        code = jnp.where(place < count_ref[:, start : start + LANES], code, 0.0)
        first = len(tiles) * head + i * slots
        a_ref[first : first + slots, :] = code.astype(jnp.bfloat16)
    for fetch in fetches[3:]:
        fetch.wait()


def prepare(label_slot, pos_ids, pos_count, embeddings, head):
    docs, slots = pos_ids.shape
    width = embeddings.shape[1]
    tall = width // LANES * head + slots * (docs // LANES)
    lines = label_slot.shape[0] // LANES
    table = label_slot.reshape(lines, LANES)
    inputs = (pos_ids.T, pos_count.reshape(1, docs), table, embeddings)
    return pl.pallas_call(
        functools.partial(prepare_kernel, (lines - 1).bit_length()),
        in_specs=[pl.BlockSpec(memory_space=pltpu.HBM)] * 4,
        out_specs=[pl.BlockSpec(memory_space=pltpu.VMEM)] * 2,
        out_shape=[
            jax.ShapeDtypeStruct((tall, LANES), jnp.bfloat16),
            jax.ShapeDtypeStruct((docs - head, width), jnp.bfloat16),
        ],
        scratch_shapes=[
            pltpu.VMEM((slots, docs), jnp.int32),
            pltpu.VMEM((1, docs), jnp.int32),
            pltpu.VMEM((lines, LANES), jnp.int32),
            pltpu.SemaphoreType.DMA((4 + width // LANES,)),
        ],
        compiler_params=pltpu.CompilerParams(vmem_limit_bytes=VMEM_LIMIT),
        name="prepare",
    )(*(pltpu.with_memory_space_constraint(x, pltpu.HBM) for x in inputs))


def cast_kernel(weights_ref, cast_ref):
    cast_ref[...] = weights_ref[...].astype(jnp.bfloat16) * 0.5


def halved_cast(weights):
    return pl.pallas_call(
        cast_kernel,
        in_specs=[pl.BlockSpec(memory_space=pltpu.VMEM)],
        out_specs=pl.BlockSpec(memory_space=pltpu.VMEM),
        out_shape=jax.ShapeDtypeStruct(weights.shape, jnp.bfloat16),
        compiler_params=pltpu.CompilerParams(vmem_limit_bytes=VMEM_LIMIT),
        name="cast",
    )(weights)


def signs_of(codes, owner, bits, height):
    docs = codes.shape[1]
    scale = power_of_two(owner * (height // LANES), bits, jnp.float32(2.0**64), -1)
    scaled = codes * scale
    place = jnp.left_shift(
        jnp.ones((WORD, docs), jnp.int32), lax.broadcasted_iota(jnp.int32, (WORD, docs), 0)
    )
    spread = []
    for part in range(height // LANES):
        row = jnp.minimum(scaled * 2.0**-part, 512.0).astype(jnp.int32) - LANES
        word = row >> 5
        bit = jnp.left_shift(jnp.ones_like(row), row & (WORD - 1))
        for w in range(LANES // WORD):
            line = jnp.sum(jnp.where(word == w, bit, 0), axis=0, keepdims=True)
            line = jnp.broadcast_to(line, (WORD, docs))
            spread.append(jnp.where((line & place) != 0, -1.0, 1.0))
    return jnp.concatenate(spread, axis=0)


def doubled_gradient(bits, owners, a_ref, b_ref, w_refs):
    height = w_refs[0].shape[0]
    head, width = b_ref.shape
    tiles = width // LANES
    chunks = 2 * head // LANES
    slots = (a_ref.shape[0] - tiles * head) // chunks
    top = jnp.concatenate([a_ref[j * head : (j + 1) * head, :] for j in range(tiles)], axis=1)
    docs = jnp.concatenate([top, b_ref[...]], axis=0)
    starts = [tiles * head + i * slots for i in range(chunks)]
    codes = jnp.concatenate([a_ref[start : start + slots, :] for start in starts], axis=1)
    codes = codes.astype(jnp.float32)
    weights = jnp.concatenate([ref[...] for ref in w_refs], axis=0)
    halved = lax.dot_general(
        weights, docs, (((1,), (1,)), ((), ())), preferred_element_type=jnp.float32
    )
    me = lax.axis_index("blk")
    signs = jnp.concatenate([signs_of(codes, me ^ owner, bits, height) for owner in owners], axis=0)
    signal = (jnp.tanh(halved) + signs).astype(jnp.bfloat16)
    return jnp.dot(signal, docs, preferred_element_type=jnp.float32)


def gradient_kernel(bits, owners, fresh, a_ref, b_ref, *refs):
    blocks = len(owners)
    w_refs, refs = refs[:blocks], refs[blocks:]
    old_refs, new_refs = refs[:-blocks], refs[-blocks:]
    height = w_refs[0].shape[0]
    part = doubled_gradient(bits, owners, a_ref, b_ref, w_refs)
    for block in range(blocks):
        piece = part[block * height : (block + 1) * height]
        new_refs[block][...] = piece if fresh else old_refs[block][...] + piece


def add_gradient(bits, owners, a, b, weights, sums, flops):
    blocks = len(weights)
    height, width = weights[0].shape
    vmem = pl.BlockSpec(memory_space=pltpu.VMEM)
    sums = list(sums)
    inputs = [a, b, *weights, *sums]
    first_sum = len(inputs) - len(sums)
    return pl.pallas_call(
        functools.partial(gradient_kernel, bits, owners, not sums),
        in_specs=[vmem] * len(inputs),
        out_specs=[vmem] * blocks,
        out_shape=[jax.ShapeDtypeStruct((height, width), jnp.float32)] * blocks,
        input_output_aliases={first_sum + i: i for i in range(len(sums))},
        compiler_params=pltpu.CompilerParams(vmem_limit_bytes=VMEM_LIMIT),
        cost_estimate=pl.CostEstimate(flops=flops, bytes_accessed=10**6, transcendentals=0),
        name="gradient",
    )(*inputs)


def finish_kernel(
    bits,
    a_ref,
    b_ref,
    cast_ref,
    sum_ref,
    other_ref,
    weights_ref,
    first_ref,
    second_ref,
    weights_hbm,
    first_hbm,
    second_hbm,
    weights_out,
    first_out,
    second_out,
    done,
):
    part = doubled_gradient(bits, (0,), a_ref, b_ref, [cast_ref])
    height = part.shape[0]
    size = height // PIECES
    writes = []
    for i in range(PIECES):
        here = pl.ds(i * size, size)
        doubled = sum_ref[here, :] + other_ref[here, :] + part[i * size : (i + 1) * size]
        new_weights, new_first, new_second = adam_step(
            weights_ref[here, :], first_ref[here, :], second_ref[here, :], doubled
        )
        for k, (value, out, hbm) in enumerate(
            (
                (new_first, first_out, first_hbm),
                (new_second, second_out, second_hbm),
                (new_weights, weights_out, weights_hbm),
            )
        ):
            out[here, :] = value
            write = pltpu.make_async_copy(out.at[here], hbm.at[here], done.at[i, k])
            write.start()
            writes.append(write)
    for write in writes:
        write.wait()


def finish(bits, a, b, cast, mine_sum, other_sum, weights, first_moment, second_moment):
    shape = jax.ShapeDtypeStruct(weights.shape, jnp.float32)
    return pl.pallas_call(
        functools.partial(finish_kernel, bits),
        in_specs=[pl.BlockSpec(memory_space=pltpu.VMEM)] * 8,
        out_specs=[pl.BlockSpec(memory_space=pltpu.HBM)] * 3,
        out_shape=[shape] * 3,
        scratch_shapes=[pltpu.VMEM(weights.shape, jnp.float32)] * 3
        + [pltpu.SemaphoreType.DMA((PIECES, 3))],
        compiler_params=pltpu.CompilerParams(vmem_limit_bytes=VMEM_LIMIT),
        cost_estimate=pl.CostEstimate(flops=END_FLOPS, bytes_accessed=10**6, transcendentals=0),
        name="finish",
    )(a, b, cast, mine_sum, other_sum, weights, first_moment, second_moment)


def adam_step(weights, first_moment, second_moment, doubled):
    new_first = beta_one * first_moment + ((1.0 - beta_one) * 0.5) * doubled
    new_second = beta_two * second_moment + ((1.0 - beta_two) * 0.25) * (doubled * doubled)
    steep = correct_one / (learn_rate * math.sqrt(correct_two))
    update = new_first / (jnp.sqrt(new_second) * steep + correct_one * adam_eps / learn_rate)
    new_weights = weights * (1.0 - learn_rate * decay_rate) - update
    return (new_weights, new_first, new_second)


def ring_of(blocks, across):
    path = list(range(0, blocks // 2, across))
    if across == 2:
        path += list(range(1, blocks // 2, 2))[::-1]
    steps = zip(path, path[1:] + path[:1])
    return [(2 * here + core, 2 * there + core) for here, there in steps for core in range(2)]


together = lax.optimization_barrier


def per_device(
    blocks,
    across,
    embeddings,
    pos_ids,
    pos_count,
    label_slot,
    weights,
    first_moment,
    second_moment,
):
    half_way = blocks // 4
    up = ring_of(blocks, across)
    down = [(there, here) for here, there in up]
    swap = [(i, i ^ 1) for i in range(blocks)]
    bits = (label_slot.shape[0] // LANES - 1).bit_length()
    head = embeddings.shape[0] // 2

    def send(value, pairs):
        return lax.ppermute(value, "blk", pairs)

    a, b = prepare(label_slot, pos_ids, pos_count, embeddings, head)
    coming = {"up_b": send(b, up), "down_a": send(a, down)}
    coming |= {"up_a": send(a, up), "down_b": send(b, down)}
    mine = halved_cast(weights)
    cast = [mine, send(mine, swap)]
    sums = ()
    waiting = [(a, b)]

    def work(flops):
        return add_gradient(bits, (0, 1), *waiting.pop(0), cast, sums, flops)

    for step in range(1, half_way):
        last = step == half_way - 1
        came = {}
        for message in ("up_b", "down_a", "up_a", "down_b"):
            came[message], waiting, sums = together((coming.pop(message), waiting, sums))
            if message in ("up_b", "down_a") or not last:
                coming[message] = send(came[message], up if message in ("up_a", "up_b") else down)
            if message in ("up_a", "down_b"):
                side = message.split("_")[0]
                waiting.append((came[side + "_a"], came[side + "_b"]))
            if waiting and (last or (step > 1 and message != "up_b")):
                sums = work(LATE_FLOPS if last else FLOPS)
    while waiting:
        sums = work(LATE_FLOPS)
    mine_sum, other_sum = sums
    got = send(other_sum, swap)
    last_b, mine_sum = together((coming["up_b"], mine_sum))
    beside_b = send(last_b, swap)
    last_a, mine_sum = together((coming["down_a"], mine_sum))
    beside_a = send(last_a, swap)
    (mine_sum,) = add_gradient(bits, (0,), last_a, last_b, [mine], [mine_sum], END_FLOPS)
    state = (weights, first_moment, second_moment)
    return finish(bits, beside_a, beside_b, mine, mine_sum, got, *state)


def solution(mesh):
    in_specs = (
        P(("groups", "blk"), None),
        P(("groups", "blk"), None),
        P(("groups", "blk")),
        P(),
        P("blk", None),
        P("blk", None),
        P("blk", None),
    )
    out_specs = (P(("groups", "blk"), None), P(("groups", "blk"), None), P(("groups", "blk"), None))
    return jax.shard_map(
        functools.partial(per_device, mesh.shape["blk"], 4 // mesh.shape["groups"]),
        mesh=mesh,
        in_specs=in_specs,
        out_specs=out_specs,
        check_vma=False,
    )
```

```python
import functools
import math

import jax
import jax.numpy as jnp
from jax import lax
from jax.experimental import pallas as pl
from jax.experimental.pallas import tpu as pltpu
from jax.sharding import PartitionSpec as P

learn_rate = 0.01
beta_one = 0.9
beta_two = 0.95
adam_eps = 1e-08
decay_rate = 0.1
correct_one = 1.0 - 0.9**10
correct_two = 1.0 - 0.95**10

WORD = 32
LANES = 128
PIECES = 4
VMEM_LIMIT = 32 * 1024 * 1024
FLOPS = 5 * 10**8
LATE_FLOPS = 10 * 10**8
PLAN = {(1,"down_b"):1,(2,"up_b"):1,(2,"up_a"):1,(3,"up_b"):1,(3,"up_a"):1,("last","up_b"):1,("last","down_a"):1,("last","up_a"):1,("last","down_b"):1}
END_FLOPS = 100 * 10**8


def power_of_two(exponent, bits, start, sign):
    value = start
    for bit in range(bits):
        factor = 2.0 ** (sign * (1 << bit))
        value = value * jnp.where(((exponent >> bit) & 1) == 1, factor, 1.0)
    return value


def prepare_kernel(
    bits,
    ids_hbm,
    count_hbm,
    table_hbm,
    docs_hbm,
    weights_hbm,
    a_ref,
    b_ref,
    cast_ref,
    ids_ref,
    count_ref,
    table_ref,
    weights_ref,
    done,
):
    slots, docs = ids_ref.shape
    head = docs - b_ref.shape[0]
    tiles = [pl.ds(start, LANES) for start in range(0, b_ref.shape[1], LANES)]
    fetches = [
        pltpu.make_async_copy(source, target, done.at[i])
        for i, (source, target) in enumerate(
            (
                (ids_hbm, ids_ref),
                (table_hbm, table_ref),
                (count_hbm, count_ref),
                (docs_hbm.at[pl.ds(head, docs - head)], b_ref),
                *(
                    (docs_hbm.at[pl.ds(0, head), tile], a_ref.at[pl.ds(j * head, head)])
                    for j, tile in enumerate(tiles)
                ),
                (weights_hbm, weights_ref),
            )
        )
    ]
    for fetch in fetches:
        fetch.start()
    for fetch in fetches[:3]:
        fetch.wait()
    pairs = table_ref.shape[0] // 2
    starts = range(0, docs, LANES)
    ids = [ids_ref[:, start : start + LANES] for start in starts]
    line_of = [(chunk >> 7) & (pairs - 1) for chunk in ids]
    lane_of = [chunk & (LANES - 1) for chunk in ids]

    def pick(t, found):
        both = table_ref[pl.ds(t, 1), :] | (table_ref[pl.ds(t + pairs, 1), :] << 16)
        line = jnp.broadcast_to(both, (slots, LANES))
        return tuple(
            jnp.where(line_of[i] == t, jnp.take_along_axis(line, lane_of[i], axis=1), found[i])
            for i in range(len(ids))
        )

    found = tuple(jnp.zeros((slots, LANES), jnp.int32) for _ in ids)
    if pairs <= 16:
        for t in range(pairs):
            found = pick(t, found)
    else:
        found = lax.fori_loop(0, pairs, pick, found, unroll=8)
    place = lax.broadcasted_iota(jnp.int32, (slots, LANES), 0)
    for i, start in enumerate(starts):
        row = jnp.where((ids[i] >> 7) < pairs, found[i], found[i] >> 16) & 0xFFFF
        low = (LANES + (row & (LANES - 1))).astype(jnp.float32)
        code = power_of_two(row >> 7, bits, low * 2.0**-64, 1)
        code = jnp.where(place < count_ref[:, start : start + LANES], code, 0.0)
        first = len(tiles) * head + i * slots
        a_ref[first : first + slots, :] = code.astype(jnp.bfloat16)
    for fetch in fetches[3:]:
        fetch.wait()
    cast_ref[...] = weights_ref[...].astype(jnp.bfloat16) * 0.5


def prepare(label_slot, pos_ids, pos_count, embeddings, weights, head):
    docs, slots = pos_ids.shape
    width = embeddings.shape[1]
    tall = width // LANES * head + slots * (docs // LANES)
    lines = label_slot.shape[0] // LANES
    table = label_slot.reshape(lines, LANES)
    inputs = (pos_ids.T, pos_count.reshape(1, docs), table, embeddings, weights)
    return pl.pallas_call(
        functools.partial(prepare_kernel, (lines - 1).bit_length()),
        in_specs=[pl.BlockSpec(memory_space=pltpu.HBM)] * 5,
        out_specs=[pl.BlockSpec(memory_space=pltpu.VMEM)] * 3,
        out_shape=[
            jax.ShapeDtypeStruct((tall, LANES), jnp.bfloat16),
            jax.ShapeDtypeStruct((docs - head, width), jnp.bfloat16),
            jax.ShapeDtypeStruct(weights.shape, jnp.bfloat16),
        ],
        scratch_shapes=[
            pltpu.VMEM((slots, docs), jnp.int32),
            pltpu.VMEM((1, docs), jnp.int32),
            pltpu.VMEM((lines, LANES), jnp.int32),
            pltpu.VMEM(weights.shape, jnp.float32),
            pltpu.SemaphoreType.DMA((5 + width // LANES,)),
        ],
        compiler_params=pltpu.CompilerParams(vmem_limit_bytes=VMEM_LIMIT),
        name="prepare",
    )(*(pltpu.with_memory_space_constraint(x, pltpu.HBM) for x in inputs))


def signs_of(codes, owner, bits, height):
    docs = codes.shape[1]
    scale = power_of_two(owner * (height // LANES), bits, jnp.float32(2.0**64), -1)
    scaled = codes * scale
    place = jnp.left_shift(
        jnp.ones((WORD, docs), jnp.int32), lax.broadcasted_iota(jnp.int32, (WORD, docs), 0)
    )
    spread = []
    for part in range(height // LANES):
        row = jnp.minimum(scaled * 2.0**-part, 512.0).astype(jnp.int32) - LANES
        word = row >> 5
        bit = jnp.left_shift(jnp.ones_like(row), row & (WORD - 1))
        for w in range(LANES // WORD):
            line = jnp.sum(jnp.where(word == w, bit, 0), axis=0, keepdims=True)
            line = jnp.broadcast_to(line, (WORD, docs))
            spread.append(jnp.where((line & place) != 0, -1.0, 1.0))
    return jnp.concatenate(spread, axis=0)


def doubled_gradient(bits, owners, a_ref, b_ref, w_refs):
    height = w_refs[0].shape[0]
    head, width = b_ref.shape
    tiles = width // LANES
    chunks = 2 * head // LANES
    slots = (a_ref.shape[0] - tiles * head) // chunks
    top = jnp.concatenate([a_ref[j * head : (j + 1) * head, :] for j in range(tiles)], axis=1)
    docs = jnp.concatenate([top, b_ref[...]], axis=0)
    starts = [tiles * head + i * slots for i in range(chunks)]
    codes = jnp.concatenate([a_ref[start : start + slots, :] for start in starts], axis=1)
    codes = codes.astype(jnp.float32)
    weights = jnp.concatenate([ref[...] for ref in w_refs], axis=0)
    halved = lax.dot_general(
        weights, docs, (((1,), (1,)), ((), ())), preferred_element_type=jnp.float32
    )
    me = lax.axis_index("blk")
    signs = jnp.concatenate([signs_of(codes, me ^ owner, bits, height) for owner in owners], axis=0)
    signal = (jnp.tanh(halved) + signs).astype(jnp.bfloat16)
    return jnp.dot(signal, docs, preferred_element_type=jnp.float32)


def gradient_kernel(bits, owners, fresh, a_ref, b_ref, *refs):
    blocks = len(owners)
    w_refs, refs = refs[:blocks], refs[blocks:]
    old_refs, new_refs = refs[:-blocks], refs[-blocks:]
    height = w_refs[0].shape[0]
    part = doubled_gradient(bits, owners, a_ref, b_ref, w_refs)
    for block in range(blocks):
        piece = part[block * height : (block + 1) * height]
        new_refs[block][...] = piece if fresh else old_refs[block][...] + piece


def add_gradient(bits, owners, a, b, weights, sums, flops):
    blocks = len(weights)
    height, width = weights[0].shape
    vmem = pl.BlockSpec(memory_space=pltpu.VMEM)
    sums = list(sums)
    inputs = [a, b, *weights, *sums]
    first_sum = len(inputs) - len(sums)
    return pl.pallas_call(
        functools.partial(gradient_kernel, bits, owners, not sums),
        in_specs=[vmem] * len(inputs),
        out_specs=[vmem] * blocks,
        out_shape=[jax.ShapeDtypeStruct((height, width), jnp.float32)] * blocks,
        input_output_aliases={first_sum + i: i for i in range(len(sums))},
        compiler_params=pltpu.CompilerParams(vmem_limit_bytes=VMEM_LIMIT),
        cost_estimate=pl.CostEstimate(flops=flops, bytes_accessed=10**6, transcendentals=0),
        name="gradient",
    )(*inputs)


def finish_kernel(
    bits,
    a_ref,
    b_ref,
    cast_ref,
    sum_ref,
    other_ref,
    weights_ref,
    first_ref,
    second_ref,
    weights_hbm,
    first_hbm,
    second_hbm,
    weights_out,
    first_out,
    second_out,
    done,
):
    part = doubled_gradient(bits, (0,), a_ref, b_ref, [cast_ref])
    height = part.shape[0]
    size = height // PIECES
    writes = []
    for i in range(PIECES):
        here = pl.ds(i * size, size)
        doubled = sum_ref[here, :] + other_ref[here, :] + part[i * size : (i + 1) * size]
        new_weights, new_first, new_second = adam_step(
            weights_ref[here, :], first_ref[here, :], second_ref[here, :], doubled
        )
        for k, (value, out, hbm) in enumerate(
            (
                (new_first, first_out, first_hbm),
                (new_second, second_out, second_hbm),
                (new_weights, weights_out, weights_hbm),
            )
        ):
            out[here, :] = value
            write = pltpu.make_async_copy(out.at[here], hbm.at[here], done.at[i, k])
            write.start()
            writes.append(write)
    for write in writes:
        write.wait()


def finish(bits, a, b, cast, mine_sum, other_sum, weights, first_moment, second_moment):
    shape = jax.ShapeDtypeStruct(weights.shape, jnp.float32)
    return pl.pallas_call(
        functools.partial(finish_kernel, bits),
        in_specs=[pl.BlockSpec(memory_space=pltpu.VMEM)] * 8,
        out_specs=[pl.BlockSpec(memory_space=pltpu.HBM)] * 3,
        out_shape=[shape] * 3,
        scratch_shapes=[pltpu.VMEM(weights.shape, jnp.float32)] * 3
        + [pltpu.SemaphoreType.DMA((PIECES, 3))],
        compiler_params=pltpu.CompilerParams(vmem_limit_bytes=VMEM_LIMIT),
        cost_estimate=pl.CostEstimate(flops=END_FLOPS, bytes_accessed=10**6, transcendentals=0),
        name="finish",
    )(a, b, cast, mine_sum, other_sum, weights, first_moment, second_moment)


def adam_step(weights, first_moment, second_moment, doubled):
    new_first = beta_one * first_moment + ((1.0 - beta_one) * 0.5) * doubled
    new_second = beta_two * second_moment + ((1.0 - beta_two) * 0.25) * (doubled * doubled)
    steep = correct_one / (learn_rate * math.sqrt(correct_two))
    update = new_first / (jnp.sqrt(new_second) * steep + correct_one * adam_eps / learn_rate)
    new_weights = weights * (1.0 - learn_rate * decay_rate) - update
    return (new_weights, new_first, new_second)


def ring_of(blocks, across):
    path = list(range(0, blocks // 2, across))
    if across == 2:
        path += list(range(1, blocks // 2, 2))[::-1]
    steps = zip(path, path[1:] + path[:1])
    return [(2 * here + core, 2 * there + core) for here, there in steps for core in range(2)]


together = lax.optimization_barrier


def per_device(
    blocks,
    across,
    embeddings,
    pos_ids,
    pos_count,
    label_slot,
    weights,
    first_moment,
    second_moment,
):
    half_way = blocks // 4
    up = ring_of(blocks, across)
    down = [(there, here) for here, there in up]
    swap = [(i, i ^ 1) for i in range(blocks)]
    bits = (label_slot.shape[0] // LANES - 1).bit_length()
    head = embeddings.shape[0] // 2

    def send(value, pairs):
        return lax.ppermute(value, "blk", pairs)

    a, b, mine = prepare(label_slot, pos_ids, pos_count, embeddings, weights, head)
    coming = {"up_b": send(b, up), "down_a": send(a, down)}
    coming |= {"up_a": send(a, up), "down_b": send(b, down)}
    cast = [mine, send(mine, swap)]
    sums = ()
    waiting = [(a, b)]

    def work(flops):
        return add_gradient(bits, (0, 1), *waiting.pop(0), cast, sums, flops)

    for step in range(1, half_way):
        last = step == half_way - 1
        came = {}
        for message in ("up_b", "down_a", "up_a", "down_b"):
            came[message], waiting, sums = together((coming.pop(message), waiting, sums))
            if message in ("up_b", "down_a") or not last:
                coming[message] = send(came[message], up if message in ("up_a", "up_b") else down)
            if message in ("up_a", "down_b"):
                side = message.split("_")[0]
                waiting.append((came[side + "_a"], came[side + "_b"]))
            for _ in range(PLAN.get((min(step, 3) if not last else "last", message), 0)):
                if waiting:
                    sums = work(LATE_FLOPS if last else FLOPS)
    while waiting:
        sums = work(LATE_FLOPS)
    mine_sum, other_sum = sums
    got = send(other_sum, swap)
    last_b, mine_sum = together((coming["up_b"], mine_sum))
    beside_b = send(last_b, swap)
    last_a, mine_sum = together((coming["down_a"], mine_sum))
    beside_a = send(last_a, swap)
    (mine_sum,) = add_gradient(bits, (0,), last_a, last_b, [mine], [mine_sum], END_FLOPS)
    state = (weights, first_moment, second_moment)
    return finish(bits, beside_a, beside_b, mine, mine_sum, got, *state)


def solution(mesh):
    in_specs = (
        P(("groups", "blk"), None),
        P(("groups", "blk"), None),
        P(("groups", "blk")),
        P(),
        P("blk", None),
        P("blk", None),
        P("blk", None),
    )
    out_specs = (P(("groups", "blk"), None), P(("groups", "blk"), None), P(("groups", "blk"), None))
    return jax.shard_map(
        functools.partial(per_device, mesh.shape["blk"], 4 // mesh.shape["groups"]),
        mesh=mesh,
        in_specs=in_specs,
        out_specs=out_specs,
        check_vma=False,
    )
```

```python
import functools
import math

import jax
import jax.numpy as jnp
from jax import lax
from jax.experimental import pallas as pl
from jax.experimental.pallas import tpu as pltpu
from jax.sharding import PartitionSpec as P

learn_rate = 0.01
beta_one = 0.9
beta_two = 0.95
adam_eps = 1e-08
decay_rate = 0.1
correct_one = 1.0 - 0.9**10
correct_two = 1.0 - 0.95**10

WORD = 32
LANES = 128
PIECES = 4
VMEM_LIMIT = 32 * 1024 * 1024
FLOPS = 2 * 10**8
LATE_FLOPS = 10 * 10**8
END_FLOPS = 100 * 10**8


def power_of_two(exponent, bits, start, sign):
    value = start
    for bit in range(bits):
        factor = 2.0 ** (sign * (1 << bit))
        value = value * jnp.where(((exponent >> bit) & 1) == 1, factor, 1.0)
    return value


def prepare_kernel(
    bits,
    ids_hbm,
    count_hbm,
    table_hbm,
    docs_hbm,
    a_ref,
    b_ref,
    ids_ref,
    count_ref,
    table_ref,
    done,
):
    slots, docs = ids_ref.shape
    head = docs - b_ref.shape[0]
    tiles = [pl.ds(start, LANES) for start in range(0, b_ref.shape[1], LANES)]
    fetches = [
        pltpu.make_async_copy(source, target, done.at[i])
        for i, (source, target) in enumerate(
            (
                (ids_hbm, ids_ref),
                (table_hbm, table_ref),
                (count_hbm, count_ref),
                (docs_hbm.at[pl.ds(head, docs - head)], b_ref),
                *(
                    (docs_hbm.at[pl.ds(0, head), tile], a_ref.at[pl.ds(j * head, head)])
                    for j, tile in enumerate(tiles)
                ),
            )
        )
    ]
    for fetch in fetches:
        fetch.start()
    for fetch in fetches[:3]:
        fetch.wait()
    pairs = table_ref.shape[0] // 2
    starts = range(0, docs, LANES)
    ids = [ids_ref[:, start : start + LANES] for start in starts]
    line_of = [(chunk >> 7) & (pairs - 1) for chunk in ids]
    lane_of = [chunk & (LANES - 1) for chunk in ids]

    def pick(t, found):
        both = table_ref[pl.ds(t, 1), :] | (table_ref[pl.ds(t + pairs, 1), :] << 16)
        line = jnp.broadcast_to(both, (slots, LANES))
        return tuple(
            jnp.where(line_of[i] == t, jnp.take_along_axis(line, lane_of[i], axis=1), found[i])
            for i in range(len(ids))
        )

    found = tuple(jnp.zeros((slots, LANES), jnp.int32) for _ in ids)
    if pairs <= 16:
        for t in range(pairs):
            found = pick(t, found)
    else:
        found = lax.fori_loop(0, pairs, pick, found, unroll=8)
    place = lax.broadcasted_iota(jnp.int32, (slots, LANES), 0)
    for i, start in enumerate(starts):
        row = jnp.where((ids[i] >> 7) < pairs, found[i], found[i] >> 16) & 0xFFFF
        low = (LANES + (row & (LANES - 1))).astype(jnp.float32)
        code = power_of_two(row >> 7, bits, low * 2.0**-64, 1)
        code = jnp.where(place < count_ref[:, start : start + LANES], code, 0.0)
        first = len(tiles) * head + i * slots
        a_ref[first : first + slots, :] = code.astype(jnp.bfloat16)
    for fetch in fetches[3:]:
        fetch.wait()


def prepare(label_slot, pos_ids, pos_count, embeddings, head):
    docs, slots = pos_ids.shape
    width = embeddings.shape[1]
    tall = width // LANES * head + slots * (docs // LANES)
    lines = label_slot.shape[0] // LANES
    table = label_slot.reshape(lines, LANES)
    inputs = (pos_ids.T, pos_count.reshape(1, docs), table, embeddings)
    return pl.pallas_call(
        functools.partial(prepare_kernel, (lines - 1).bit_length()),
        in_specs=[pl.BlockSpec(memory_space=pltpu.HBM)] * 4,
        out_specs=[pl.BlockSpec(memory_space=pltpu.VMEM)] * 2,
        out_shape=[
            jax.ShapeDtypeStruct((tall, LANES), jnp.bfloat16),
            jax.ShapeDtypeStruct((docs - head, width), jnp.bfloat16),
        ],
        scratch_shapes=[
            pltpu.VMEM((slots, docs), jnp.int32),
            pltpu.VMEM((1, docs), jnp.int32),
            pltpu.VMEM((lines, LANES), jnp.int32),
            pltpu.SemaphoreType.DMA((4 + width // LANES,)),
        ],
        compiler_params=pltpu.CompilerParams(vmem_limit_bytes=VMEM_LIMIT),
        name="prepare",
    )(*(pltpu.with_memory_space_constraint(x, pltpu.HBM) for x in inputs))


def cast_kernel(weights_ref, cast_ref):
    cast_ref[...] = weights_ref[...].astype(jnp.bfloat16) * 0.5


def halved_cast(weights):
    return pl.pallas_call(
        cast_kernel,
        in_specs=[pl.BlockSpec(memory_space=pltpu.VMEM)],
        out_specs=pl.BlockSpec(memory_space=pltpu.VMEM),
        out_shape=jax.ShapeDtypeStruct(weights.shape, jnp.bfloat16),
        compiler_params=pltpu.CompilerParams(vmem_limit_bytes=VMEM_LIMIT),
        name="cast",
    )(weights)


def signs_of(codes, owner, bits, height):
    docs = codes.shape[1]
    scale = power_of_two(owner * (height // LANES), bits, jnp.float32(2.0**64), -1)
    scaled = codes * scale
    place = jnp.left_shift(
        jnp.ones((WORD, docs), jnp.int32), lax.broadcasted_iota(jnp.int32, (WORD, docs), 0)
    )
    spread = []
    for part in range(height // LANES):
        row = jnp.minimum(scaled * 2.0**-part, 512.0).astype(jnp.int32) - LANES
        word = row >> 5
        bit = jnp.left_shift(jnp.ones_like(row), row & (WORD - 1))
        for w in range(LANES // WORD):
            line = jnp.sum(jnp.where(word == w, bit, 0), axis=0, keepdims=True)
            line = jnp.broadcast_to(line, (WORD, docs))
            spread.append(jnp.where((line & place) != 0, -1.0, 1.0))
    return jnp.concatenate(spread, axis=0)


def doubled_gradient(bits, owners, a_ref, b_ref, w_refs):
    height = w_refs[0].shape[0]
    head, width = b_ref.shape
    tiles = width // LANES
    chunks = 2 * head // LANES
    slots = (a_ref.shape[0] - tiles * head) // chunks
    top = jnp.concatenate([a_ref[j * head : (j + 1) * head, :] for j in range(tiles)], axis=1)
    docs = jnp.concatenate([top, b_ref[...]], axis=0)
    starts = [tiles * head + i * slots for i in range(chunks)]
    codes = jnp.concatenate([a_ref[start : start + slots, :] for start in starts], axis=1)
    codes = codes.astype(jnp.float32)
    weights = jnp.concatenate([ref[...] for ref in w_refs], axis=0)
    halved = lax.dot_general(
        weights, docs, (((1,), (1,)), ((), ())), preferred_element_type=jnp.float32
    )
    me = lax.axis_index("blk")
    signs = jnp.concatenate([signs_of(codes, me ^ owner, bits, height) for owner in owners], axis=0)
    signal = (jnp.tanh(halved) + signs).astype(jnp.bfloat16)
    return jnp.dot(signal, docs, preferred_element_type=jnp.float32)


def gradient_kernel(bits, owners, fresh, a_ref, b_ref, *refs):
    blocks = len(owners)
    w_refs, refs = refs[:blocks], refs[blocks:]
    old_refs, new_refs = refs[:-blocks], refs[-blocks:]
    height = w_refs[0].shape[0]
    part = doubled_gradient(bits, owners, a_ref, b_ref, w_refs)
    for block in range(blocks):
        piece = part[block * height : (block + 1) * height]
        new_refs[block][...] = piece if fresh else old_refs[block][...] + piece


def add_gradient(bits, owners, a, b, weights, sums, flops):
    blocks = len(weights)
    height, width = weights[0].shape
    vmem = pl.BlockSpec(memory_space=pltpu.VMEM)
    sums = list(sums)
    inputs = [a, b, *weights, *sums]
    first_sum = len(inputs) - len(sums)
    return pl.pallas_call(
        functools.partial(gradient_kernel, bits, owners, not sums),
        in_specs=[vmem] * len(inputs),
        out_specs=[vmem] * blocks,
        out_shape=[jax.ShapeDtypeStruct((height, width), jnp.float32)] * blocks,
        input_output_aliases={first_sum + i: i for i in range(len(sums))},
        compiler_params=pltpu.CompilerParams(vmem_limit_bytes=VMEM_LIMIT),
        cost_estimate=pl.CostEstimate(flops=flops, bytes_accessed=10**6, transcendentals=0),
        name="gradient",
    )(*inputs)


def finish_kernel(
    bits,
    a_ref,
    b_ref,
    cast_ref,
    sum_ref,
    other_ref,
    weights_ref,
    first_ref,
    second_ref,
    weights_hbm,
    first_hbm,
    second_hbm,
    weights_out,
    first_out,
    second_out,
    done,
):
    part = doubled_gradient(bits, (0,), a_ref, b_ref, [cast_ref])
    height = part.shape[0]
    size = height // PIECES
    writes = []
    for i in range(PIECES):
        here = pl.ds(i * size, size)
        doubled = sum_ref[here, :] + other_ref[here, :] + part[i * size : (i + 1) * size]
        new_weights, new_first, new_second = adam_step(
            weights_ref[here, :], first_ref[here, :], second_ref[here, :], doubled
        )
        for k, (value, out, hbm) in enumerate(
            (
                (new_first, first_out, first_hbm),
                (new_second, second_out, second_hbm),
                (new_weights, weights_out, weights_hbm),
            )
        ):
            out[here, :] = value
            write = pltpu.make_async_copy(out.at[here], hbm.at[here], done.at[i, k])
            write.start()
            writes.append(write)
    for write in writes:
        write.wait()


def finish(bits, a, b, cast, mine_sum, other_sum, weights, first_moment, second_moment):
    shape = jax.ShapeDtypeStruct(weights.shape, jnp.float32)
    return pl.pallas_call(
        functools.partial(finish_kernel, bits),
        in_specs=[pl.BlockSpec(memory_space=pltpu.VMEM)] * 8,
        out_specs=[pl.BlockSpec(memory_space=pltpu.HBM)] * 3,
        out_shape=[shape] * 3,
        scratch_shapes=[pltpu.VMEM(weights.shape, jnp.float32)] * 3
        + [pltpu.SemaphoreType.DMA((PIECES, 3))],
        compiler_params=pltpu.CompilerParams(vmem_limit_bytes=VMEM_LIMIT),
        cost_estimate=pl.CostEstimate(flops=END_FLOPS, bytes_accessed=10**6, transcendentals=0),
        name="finish",
    )(a, b, cast, mine_sum, other_sum, weights, first_moment, second_moment)


def adam_step(weights, first_moment, second_moment, doubled):
    new_first = beta_one * first_moment + ((1.0 - beta_one) * 0.5) * doubled
    new_second = beta_two * second_moment + ((1.0 - beta_two) * 0.25) * (doubled * doubled)
    steep = correct_one / (learn_rate * math.sqrt(correct_two))
    update = new_first / (jnp.sqrt(new_second) * steep + correct_one * adam_eps / learn_rate)
    new_weights = weights * (1.0 - learn_rate * decay_rate) - update
    return (new_weights, new_first, new_second)


def ring_of(blocks, across):
    path = list(range(0, blocks // 2, across))
    if across == 2:
        path += list(range(1, blocks // 2, 2))[::-1]
    pairs = []
    for here, there in zip(path, path[1:] + path[:1]):
        pairs += [(2 * here, 2 * there), (2 * there + 1, 2 * here + 1)]
    return pairs


together = lax.optimization_barrier


def per_device(
    blocks,
    across,
    embeddings,
    pos_ids,
    pos_count,
    label_slot,
    weights,
    first_moment,
    second_moment,
):
    half_way = blocks // 4
    up = ring_of(blocks, across)
    down = [(there, here) for here, there in up]
    swap = [(i, i ^ 1) for i in range(blocks)]
    bits = (label_slot.shape[0] // LANES - 1).bit_length()
    head = embeddings.shape[0] // 2

    def send(value, pairs):
        return lax.ppermute(value, "blk", pairs)

    a, b = prepare(label_slot, pos_ids, pos_count, embeddings, head)
    coming = {"up_b": send(b, up), "down_a": send(a, down)}
    coming |= {"up_a": send(a, up), "down_b": send(b, down)}
    mine = halved_cast(weights)
    cast = [mine, send(mine, swap)]
    sums = ()
    waiting = [(a, b)]

    def work(flops):
        return add_gradient(bits, (0, 1), *waiting.pop(0), cast, sums, flops)

    for step in range(1, half_way):
        last = step == half_way - 1
        came = {}
        for message in ("up_b", "down_a", "up_a", "down_b"):
            came[message], waiting, sums = together((coming.pop(message), waiting, sums))
            if message in ("up_b", "down_a") or not last:
                coming[message] = send(came[message], up if message in ("up_a", "up_b") else down)
            if message in ("up_a", "down_b"):
                side = message.split("_")[0]
                waiting.append((came[side + "_a"], came[side + "_b"]))
            if waiting and (last or (step > 1 and message != "up_b")):
                sums = work(LATE_FLOPS if last else FLOPS)
    while waiting:
        sums = work(LATE_FLOPS)
    mine_sum, other_sum = sums
    got = send(other_sum, swap)
    last_b, mine_sum = together((coming["up_b"], mine_sum))
    beside_b = send(last_b, swap)
    last_a, mine_sum = together((coming["down_a"], mine_sum))
    beside_a = send(last_a, swap)
    (mine_sum,) = add_gradient(bits, (0,), last_a, last_b, [mine], [mine_sum], END_FLOPS)
    state = (weights, first_moment, second_moment)
    return finish(bits, beside_a, beside_b, mine, mine_sum, got, *state)


def solution(mesh):
    in_specs = (
        P(("groups", "blk"), None),
        P(("groups", "blk"), None),
        P(("groups", "blk")),
        P(),
        P("blk", None),
        P("blk", None),
        P("blk", None),
    )
    out_specs = (P(("groups", "blk"), None), P(("groups", "blk"), None), P(("groups", "blk"), None))
    return jax.shard_map(
        functools.partial(per_device, mesh.shape["blk"], 4 // mesh.shape["groups"]),
        mesh=mesh,
        in_specs=in_specs,
        out_specs=out_specs,
        check_vma=False,
    )
```

```python
import functools
import math

import jax
import jax.numpy as jnp
from jax import lax
from jax.experimental import pallas as pl
from jax.experimental.pallas import tpu as pltpu
from jax.sharding import PartitionSpec as P

learn_rate = 0.01
beta_one = 0.9
beta_two = 0.95
adam_eps = 1e-08
decay_rate = 0.1
correct_one = 1.0 - 0.9**10
correct_two = 1.0 - 0.95**10

WORD = 32
LANES = 128
PIECES = 4
VMEM_LIMIT = 32 * 1024 * 1024
FLOPS = 2 * 10**8
LATE_FLOPS = 10 * 10**8
END_FLOPS = 100 * 10**8


def power_of_two(exponent, bits, start, sign):
    value = start
    for bit in range(bits):
        factor = 2.0 ** (sign * (1 << bit))
        value = value * jnp.where(((exponent >> bit) & 1) == 1, factor, 1.0)
    return value


def prepare_kernel(
    bits,
    ids_hbm,
    count_hbm,
    table_hbm,
    docs_hbm,
    a_ref,
    b_ref,
    ids_ref,
    count_ref,
    table_ref,
    done,
):
    slots, docs = ids_ref.shape
    head = docs - b_ref.shape[0]
    tiles = [pl.ds(start, LANES) for start in range(0, b_ref.shape[1], LANES)]
    fetches = [
        pltpu.make_async_copy(source, target, done.at[i])
        for i, (source, target) in enumerate(
            (
                (ids_hbm, ids_ref),
                (table_hbm, table_ref),
                (count_hbm, count_ref),
                (docs_hbm.at[pl.ds(head, docs - head)], b_ref),
                *(
                    (docs_hbm.at[pl.ds(0, head), tile], a_ref.at[pl.ds(j * head, head)])
                    for j, tile in enumerate(tiles)
                ),
            )
        )
    ]
    for fetch in fetches:
        fetch.start()
    for fetch in fetches[:3]:
        fetch.wait()
    pairs = table_ref.shape[0] // 2
    starts = range(0, docs, LANES)
    ids = [ids_ref[:, start : start + LANES] for start in starts]
    line_of = [(chunk >> 7) & (pairs - 1) for chunk in ids]
    lane_of = [chunk & (LANES - 1) for chunk in ids]

    def pick(t, found):
        both = table_ref[pl.ds(t, 1), :] | (table_ref[pl.ds(t + pairs, 1), :] << 16)
        line = jnp.broadcast_to(both, (slots, LANES))
        return tuple(
            jnp.where(line_of[i] == t, jnp.take_along_axis(line, lane_of[i], axis=1), found[i])
            for i in range(len(ids))
        )

    found = tuple(jnp.zeros((slots, LANES), jnp.int32) for _ in ids)
    if pairs <= 16:
        for t in range(pairs):
            found = pick(t, found)
    else:
        found = lax.fori_loop(0, pairs, pick, found, unroll=8)
    place = lax.broadcasted_iota(jnp.int32, (slots, LANES), 0)
    for i, start in enumerate(starts):
        row = jnp.where((ids[i] >> 7) < pairs, found[i], found[i] >> 16) & 0xFFFF
        low = (LANES + (row & (LANES - 1))).astype(jnp.float32)
        code = power_of_two(row >> 7, bits, low * 2.0**-64, 1)
        code = jnp.where(place < count_ref[:, start : start + LANES], code, 0.0)
        first = len(tiles) * head + i * slots
        a_ref[first : first + slots, :] = code.astype(jnp.bfloat16)
    for fetch in fetches[3:]:
        fetch.wait()


def prepare(label_slot, pos_ids, pos_count, embeddings, head):
    docs, slots = pos_ids.shape
    width = embeddings.shape[1]
    tall = width // LANES * head + slots * (docs // LANES)
    lines = label_slot.shape[0] // LANES
    table = label_slot.reshape(lines, LANES)
    inputs = (pos_ids.T, pos_count.reshape(1, docs), table, embeddings)
    return pl.pallas_call(
        functools.partial(prepare_kernel, (lines - 1).bit_length()),
        in_specs=[pl.BlockSpec(memory_space=pltpu.HBM)] * 4,
        out_specs=[pl.BlockSpec(memory_space=pltpu.VMEM)] * 2,
        out_shape=[
            jax.ShapeDtypeStruct((tall, LANES), jnp.bfloat16),
            jax.ShapeDtypeStruct((docs - head, width), jnp.bfloat16),
        ],
        scratch_shapes=[
            pltpu.VMEM((slots, docs), jnp.int32),
            pltpu.VMEM((1, docs), jnp.int32),
            pltpu.VMEM((lines, LANES), jnp.int32),
            pltpu.SemaphoreType.DMA((4 + width // LANES,)),
        ],
        compiler_params=pltpu.CompilerParams(vmem_limit_bytes=VMEM_LIMIT),
        name="prepare",
    )(*(pltpu.with_memory_space_constraint(x, pltpu.HBM) for x in inputs))


def cast_kernel(weights_ref, cast_ref):
    cast_ref[...] = weights_ref[...].astype(jnp.bfloat16) * 0.5


def halved_cast(weights):
    return pl.pallas_call(
        cast_kernel,
        in_specs=[pl.BlockSpec(memory_space=pltpu.VMEM)],
        out_specs=pl.BlockSpec(memory_space=pltpu.VMEM),
        out_shape=jax.ShapeDtypeStruct(weights.shape, jnp.bfloat16),
        compiler_params=pltpu.CompilerParams(vmem_limit_bytes=VMEM_LIMIT),
        name="cast",
    )(weights)


def signs_of(codes, owner, bits, height):
    docs = codes.shape[1]
    scale = power_of_two(owner * (height // LANES), bits, jnp.float32(2.0**64), -1)
    scaled = codes * scale
    place = jnp.left_shift(
        jnp.ones((WORD, docs), jnp.int32), lax.broadcasted_iota(jnp.int32, (WORD, docs), 0)
    )
    spread = []
    for part in range(height // LANES):
        row = jnp.minimum(scaled * 2.0**-part, 512.0).astype(jnp.int32) - LANES
        word = row >> 5
        bit = jnp.left_shift(jnp.ones_like(row), row & (WORD - 1))
        for w in range(LANES // WORD):
            line = jnp.sum(jnp.where(word == w, bit, 0), axis=0, keepdims=True)
            line = jnp.broadcast_to(line, (WORD, docs))
            spread.append(jnp.where((line & place) != 0, -1.0, 1.0))
    return jnp.concatenate(spread, axis=0)


def doubled_gradient(bits, owners, a_ref, b_ref, w_refs):
    height = w_refs[0].shape[0]
    head, width = b_ref.shape
    tiles = width // LANES
    chunks = 2 * head // LANES
    slots = (a_ref.shape[0] - tiles * head) // chunks
    top = jnp.concatenate([a_ref[j * head : (j + 1) * head, :] for j in range(tiles)], axis=1)
    docs = jnp.concatenate([top, b_ref[...]], axis=0)
    starts = [tiles * head + i * slots for i in range(chunks)]
    codes = jnp.concatenate([a_ref[start : start + slots, :] for start in starts], axis=1)
    codes = codes.astype(jnp.float32)
    weights = jnp.concatenate([ref[...] for ref in w_refs], axis=0)
    halved = lax.dot_general(
        weights, docs, (((1,), (1,)), ((), ())), preferred_element_type=jnp.float32
    )
    me = lax.axis_index("blk")
    signs = jnp.concatenate([signs_of(codes, me ^ owner, bits, height) for owner in owners], axis=0)
    signal = (jnp.tanh(halved) + signs).astype(jnp.bfloat16)
    return jnp.dot(signal, docs, preferred_element_type=jnp.float32)


def gradient_kernel(bits, owners, fresh, a_ref, b_ref, *refs):
    blocks = len(owners)
    w_refs, refs = refs[:blocks], refs[blocks:]
    old_refs, new_refs = refs[:-blocks], refs[-blocks:]
    height = w_refs[0].shape[0]
    part = doubled_gradient(bits, owners, a_ref, b_ref, w_refs)
    for block in range(blocks):
        piece = part[block * height : (block + 1) * height]
        new_refs[block][...] = piece if fresh else old_refs[block][...] + piece


def add_gradient(bits, owners, a, b, weights, sums, flops):
    blocks = len(weights)
    height, width = weights[0].shape
    vmem = pl.BlockSpec(memory_space=pltpu.VMEM)
    sums = list(sums)
    inputs = [a, b, *weights, *sums]
    first_sum = len(inputs) - len(sums)
    return pl.pallas_call(
        functools.partial(gradient_kernel, bits, owners, not sums),
        in_specs=[vmem] * len(inputs),
        out_specs=[vmem] * blocks,
        out_shape=[jax.ShapeDtypeStruct((height, width), jnp.float32)] * blocks,
        input_output_aliases={first_sum + i: i for i in range(len(sums))},
        compiler_params=pltpu.CompilerParams(vmem_limit_bytes=VMEM_LIMIT),
        cost_estimate=pl.CostEstimate(flops=flops, bytes_accessed=10**6, transcendentals=0),
        name="gradient",
    )(*inputs)


def finish_kernel(
    bits,
    a_ref,
    b_ref,
    cast_ref,
    sum_ref,
    other_ref,
    weights_ref,
    first_ref,
    second_ref,
    weights_hbm,
    first_hbm,
    second_hbm,
    weights_out,
    first_out,
    second_out,
    done,
):
    part = doubled_gradient(bits, (0,), a_ref, b_ref, [cast_ref])
    height = part.shape[0]
    size = height // PIECES
    writes = []
    for i in range(PIECES):
        here = pl.ds(i * size, size)
        doubled = sum_ref[here, :] + other_ref[here, :] + part[i * size : (i + 1) * size]
        new_weights, new_first, new_second = adam_step(
            weights_ref[here, :], first_ref[here, :], second_ref[here, :], doubled
        )
        for k, (value, out, hbm) in enumerate(
            (
                (new_first, first_out, first_hbm),
                (new_second, second_out, second_hbm),
                (new_weights, weights_out, weights_hbm),
            )
        ):
            out[here, :] = value
            write = pltpu.make_async_copy(out.at[here], hbm.at[here], done.at[i, k])
            write.start()
            writes.append(write)
    for write in writes:
        write.wait()


def finish(bits, a, b, cast, mine_sum, other_sum, weights, first_moment, second_moment):
    shape = jax.ShapeDtypeStruct(weights.shape, jnp.float32)
    return pl.pallas_call(
        functools.partial(finish_kernel, bits),
        in_specs=[pl.BlockSpec(memory_space=pltpu.VMEM)] * 8,
        out_specs=[pl.BlockSpec(memory_space=pltpu.HBM)] * 3,
        out_shape=[shape] * 3,
        scratch_shapes=[pltpu.VMEM(weights.shape, jnp.float32)] * 3
        + [pltpu.SemaphoreType.DMA((PIECES, 3))],
        compiler_params=pltpu.CompilerParams(vmem_limit_bytes=VMEM_LIMIT),
        cost_estimate=pl.CostEstimate(flops=END_FLOPS, bytes_accessed=10**6, transcendentals=0),
        name="finish",
    )(a, b, cast, mine_sum, other_sum, weights, first_moment, second_moment)


def adam_step(weights, first_moment, second_moment, doubled):
    new_first = beta_one * first_moment + ((1.0 - beta_one) * 0.5) * doubled
    new_second = beta_two * second_moment + ((1.0 - beta_two) * 0.25) * (doubled * doubled)
    steep = correct_one / (learn_rate * math.sqrt(correct_two))
    update = new_first / (jnp.sqrt(new_second) * steep + correct_one * adam_eps / learn_rate)
    new_weights = weights * (1.0 - learn_rate * decay_rate) - update
    return (new_weights, new_first, new_second)


def ring_of(blocks, across):
    path = list(range(0, blocks // 2, across))
    if across == 2:
        path += list(range(1, blocks // 2, 2))[::-1]
    pairs = []
    for here, there in zip(path, path[1:] + path[:1]):
        pairs += [(2 * here, 2 * there), (2 * there + 1, 2 * here + 1)]
    return pairs


together = lax.optimization_barrier


def per_device(
    blocks,
    across,
    embeddings,
    pos_ids,
    pos_count,
    label_slot,
    weights,
    first_moment,
    second_moment,
):
    half_way = blocks // 4
    up = ring_of(blocks, across)
    down = [(there, here) for here, there in up]
    swap = [(i, i ^ 1) for i in range(blocks)]
    bits = (label_slot.shape[0] // LANES - 1).bit_length()
    head = embeddings.shape[0] // 2

    def send(value, pairs):
        return lax.ppermute(value, "blk", pairs)

    a, b = prepare(label_slot, pos_ids, pos_count, embeddings, head)
    coming = {"up_b": send(b, up), "down_a": send(a, down)}
    coming |= {"up_a": send(a, up), "down_b": send(b, down)}
    mine = halved_cast(weights)
    cast = [mine, send(mine, swap)]
    sums = ()
    waiting = [(a, b)]

    def work(flops):
        return add_gradient(bits, (0, 1), *waiting.pop(0), cast, sums, flops)

    for step in range(1, half_way):
        last = step == half_way - 1
        came = {}
        for message in ("up_b", "down_a", "up_a", "down_b"):
            came[message], waiting, sums = together((coming.pop(message), waiting, sums))
            if message in ("up_b", "down_a") or not last:
                coming[message] = send(came[message], up if message in ("up_a", "up_b") else down)
            if message in ("up_a", "down_b"):
                side = message.split("_")[0]
                waiting.append((came[side + "_a"], came[side + "_b"]))
            if last:
                number = 2 if message == "down_a" else 1
            else:
                number = 1 if step > 1 and message in ("down_a", "up_a") else 0
            for _ in range(min(number, len(waiting))):
                sums = work(LATE_FLOPS if last else FLOPS)
    while waiting:
        sums = work(LATE_FLOPS)
    mine_sum, other_sum = sums
    got = send(other_sum, swap)
    last_b, mine_sum = together((coming["up_b"], mine_sum))
    beside_b = send(last_b, swap)
    last_a, mine_sum = together((coming["down_a"], mine_sum))
    beside_a = send(last_a, swap)
    (mine_sum,) = add_gradient(bits, (0,), last_a, last_b, [mine], [mine_sum], END_FLOPS)
    state = (weights, first_moment, second_moment)
    return finish(bits, beside_a, beside_b, mine, mine_sum, got, *state)


def solution(mesh):
    in_specs = (
        P(("groups", "blk"), None),
        P(("groups", "blk"), None),
        P(("groups", "blk")),
        P(),
        P("blk", None),
        P("blk", None),
        P("blk", None),
    )
    out_specs = (P(("groups", "blk"), None), P(("groups", "blk"), None), P(("groups", "blk"), None))
    return jax.shard_map(
        functools.partial(per_device, mesh.shape["blk"], 4 // mesh.shape["groups"]),
        mesh=mesh,
        in_specs=in_specs,
        out_specs=out_specs,
        check_vma=False,
    )
```

```python
import functools
import math

import jax
import jax.numpy as jnp
from jax import lax
from jax.experimental import pallas as pl
from jax.experimental.pallas import tpu as pltpu
from jax.sharding import PartitionSpec as P

learn_rate = 0.01
beta_one = 0.9
beta_two = 0.95
adam_eps = 1e-08
decay_rate = 0.1
correct_one = 1.0 - 0.9**10
correct_two = 1.0 - 0.95**10

WORD = 32
LANES = 128
PIECES = 4
VMEM_LIMIT = 32 * 1024 * 1024
FLOPS = 2 * 10**8
LATE_FLOPS = 10 * 10**8
END_FLOPS = 100 * 10**8


def power_of_two(exponent, bits, start, sign):
    value = start
    for bit in range(bits):
        factor = 2.0 ** (sign * (1 << bit))
        value = value * jnp.where(((exponent >> bit) & 1) == 1, factor, 1.0)
    return value


def prepare_kernel(
    bits,
    ids_hbm,
    count_hbm,
    table_hbm,
    docs_hbm,
    _,
    a_ref,
    ids_ref,
    count_ref,
    table_ref,
    done,
):
    slots, docs = ids_ref.shape
    tiles = [pl.ds(start, LANES) for start in range(0, docs_hbm.shape[1], LANES)]
    head = (a_ref.shape[0] - slots * (docs // LANES)) // len(tiles)
    fetches = [
        pltpu.make_async_copy(source, target, done.at[i])
        for i, (source, target) in enumerate(
            (
                (ids_hbm, ids_ref),
                (table_hbm, table_ref),
                (count_hbm, count_ref),
                *(
                    (docs_hbm.at[pl.ds(0, head), tile], a_ref.at[pl.ds(j * head, head)])
                    for j, tile in enumerate(tiles)
                ),
            )
        )
    ]
    for fetch in fetches:
        fetch.start()
    for fetch in fetches[:3]:
        fetch.wait()
    pairs = table_ref.shape[0] // 2
    starts = range(0, docs, LANES)
    ids = [ids_ref[:, start : start + LANES] for start in starts]
    line_of = [(chunk >> 7) & (pairs - 1) for chunk in ids]
    lane_of = [chunk & (LANES - 1) for chunk in ids]

    def pick(t, found):
        both = table_ref[pl.ds(t, 1), :] | (table_ref[pl.ds(t + pairs, 1), :] << 16)
        line = jnp.broadcast_to(both, (slots, LANES))
        return tuple(
            jnp.where(line_of[i] == t, jnp.take_along_axis(line, lane_of[i], axis=1), found[i])
            for i in range(len(ids))
        )

    found = tuple(jnp.zeros((slots, LANES), jnp.int32) for _ in ids)
    if pairs <= 16:
        for t in range(pairs):
            found = pick(t, found)
    else:
        found = lax.fori_loop(0, pairs, pick, found, unroll=8)
    place = lax.broadcasted_iota(jnp.int32, (slots, LANES), 0)
    for i, start in enumerate(starts):
        row = jnp.where((ids[i] >> 7) < pairs, found[i], found[i] >> 16) & 0xFFFF
        low = (LANES + (row & (LANES - 1))).astype(jnp.float32)
        code = power_of_two(row >> 7, bits, low * 2.0**-64, 1)
        code = jnp.where(place < count_ref[:, start : start + LANES], code, 0.0)
        first = len(tiles) * head + i * slots
        a_ref[first : first + slots, :] = code.astype(jnp.bfloat16)
    for fetch in fetches[3:]:
        fetch.wait()


def fetch_kernel(head, docs_hbm, b_ref, done):
    fetch = pltpu.make_async_copy(docs_hbm.at[pl.ds(head, b_ref.shape[0])], b_ref, done)
    fetch.start()
    fetch.wait()


def fetch_later(embeddings, head):
    docs, width = embeddings.shape
    return pl.pallas_call(
        functools.partial(fetch_kernel, head),
        in_specs=[pl.BlockSpec(memory_space=pltpu.HBM)],
        out_specs=pl.BlockSpec(memory_space=pltpu.VMEM),
        out_shape=jax.ShapeDtypeStruct((docs - head, width), jnp.bfloat16),
        scratch_shapes=[pltpu.SemaphoreType.DMA],
        compiler_params=pltpu.CompilerParams(vmem_limit_bytes=VMEM_LIMIT),
        name="fetch",
    )(pltpu.with_memory_space_constraint(embeddings, pltpu.HBM))


def prepare(label_slot, pos_ids, pos_count, embeddings, b, head):
    docs, slots = pos_ids.shape
    width = embeddings.shape[1]
    tall = width // LANES * head + slots * (docs // LANES)
    lines = label_slot.shape[0] // LANES
    table = label_slot.reshape(lines, LANES)
    inputs = (pos_ids.T, pos_count.reshape(1, docs), table, embeddings)
    return pl.pallas_call(
        functools.partial(prepare_kernel, (lines - 1).bit_length()),
        in_specs=[pl.BlockSpec(memory_space=pltpu.HBM)] * 4 + [pl.BlockSpec(memory_space=pl.ANY)],
        out_specs=pl.BlockSpec(memory_space=pltpu.VMEM),
        out_shape=jax.ShapeDtypeStruct((tall, LANES), jnp.bfloat16),
        scratch_shapes=[
            pltpu.VMEM((slots, docs), jnp.int32),
            pltpu.VMEM((1, docs), jnp.int32),
            pltpu.VMEM((lines, LANES), jnp.int32),
            pltpu.SemaphoreType.DMA((3 + width // LANES,)),
        ],
        compiler_params=pltpu.CompilerParams(vmem_limit_bytes=VMEM_LIMIT),
        name="prepare",
    )(*(pltpu.with_memory_space_constraint(x, pltpu.HBM) for x in inputs), b)


def cast_kernel(weights_ref, cast_ref):
    cast_ref[...] = weights_ref[...].astype(jnp.bfloat16) * 0.5


def halved_cast(weights):
    return pl.pallas_call(
        cast_kernel,
        in_specs=[pl.BlockSpec(memory_space=pltpu.VMEM)],
        out_specs=pl.BlockSpec(memory_space=pltpu.VMEM),
        out_shape=jax.ShapeDtypeStruct(weights.shape, jnp.bfloat16),
        compiler_params=pltpu.CompilerParams(vmem_limit_bytes=VMEM_LIMIT),
        name="cast",
    )(weights)


def signs_of(codes, owner, bits, height):
    docs = codes.shape[1]
    scale = power_of_two(owner * (height // LANES), bits, jnp.float32(2.0**64), -1)
    scaled = codes * scale
    place = jnp.left_shift(
        jnp.ones((WORD, docs), jnp.int32), lax.broadcasted_iota(jnp.int32, (WORD, docs), 0)
    )
    spread = []
    for part in range(height // LANES):
        row = jnp.minimum(scaled * 2.0**-part, 512.0).astype(jnp.int32) - LANES
        word = row >> 5
        bit = jnp.left_shift(jnp.ones_like(row), row & (WORD - 1))
        for w in range(LANES // WORD):
            line = jnp.sum(jnp.where(word == w, bit, 0), axis=0, keepdims=True)
            line = jnp.broadcast_to(line, (WORD, docs))
            spread.append(jnp.where((line & place) != 0, -1.0, 1.0))
    return jnp.concatenate(spread, axis=0)


def doubled_gradient(bits, owners, a_ref, b_ref, w_refs):
    height = w_refs[0].shape[0]
    head, width = b_ref.shape
    tiles = width // LANES
    chunks = 2 * head // LANES
    slots = (a_ref.shape[0] - tiles * head) // chunks
    top = jnp.concatenate([a_ref[j * head : (j + 1) * head, :] for j in range(tiles)], axis=1)
    docs = jnp.concatenate([top, b_ref[...]], axis=0)
    starts = [tiles * head + i * slots for i in range(chunks)]
    codes = jnp.concatenate([a_ref[start : start + slots, :] for start in starts], axis=1)
    codes = codes.astype(jnp.float32)
    weights = jnp.concatenate([ref[...] for ref in w_refs], axis=0)
    halved = lax.dot_general(
        weights, docs, (((1,), (1,)), ((), ())), preferred_element_type=jnp.float32
    )
    me = lax.axis_index("blk")
    signs = jnp.concatenate([signs_of(codes, me ^ owner, bits, height) for owner in owners], axis=0)
    signal = (jnp.tanh(halved) + signs).astype(jnp.bfloat16)
    return jnp.dot(signal, docs, preferred_element_type=jnp.float32)


def gradient_kernel(bits, owners, fresh, a_ref, b_ref, *refs):
    blocks = len(owners)
    w_refs, refs = refs[:blocks], refs[blocks:]
    old_refs, new_refs = refs[:-blocks], refs[-blocks:]
    height = w_refs[0].shape[0]
    part = doubled_gradient(bits, owners, a_ref, b_ref, w_refs)
    for block in range(blocks):
        piece = part[block * height : (block + 1) * height]
        new_refs[block][...] = piece if fresh else old_refs[block][...] + piece


def add_gradient(bits, owners, a, b, weights, sums, flops):
    blocks = len(weights)
    height, width = weights[0].shape
    vmem = pl.BlockSpec(memory_space=pltpu.VMEM)
    sums = list(sums)
    inputs = [a, b, *weights, *sums]
    first_sum = len(inputs) - len(sums)
    return pl.pallas_call(
        functools.partial(gradient_kernel, bits, owners, not sums),
        in_specs=[vmem] * len(inputs),
        out_specs=[vmem] * blocks,
        out_shape=[jax.ShapeDtypeStruct((height, width), jnp.float32)] * blocks,
        input_output_aliases={first_sum + i: i for i in range(len(sums))},
        compiler_params=pltpu.CompilerParams(vmem_limit_bytes=VMEM_LIMIT),
        cost_estimate=pl.CostEstimate(flops=flops, bytes_accessed=10**6, transcendentals=0),
        name="gradient",
    )(*inputs)


def finish_kernel(
    bits,
    a_ref,
    b_ref,
    cast_ref,
    sum_ref,
    other_ref,
    weights_ref,
    first_ref,
    second_ref,
    weights_hbm,
    first_hbm,
    second_hbm,
    weights_out,
    first_out,
    second_out,
    done,
):
    part = doubled_gradient(bits, (0,), a_ref, b_ref, [cast_ref])
    height = part.shape[0]
    size = height // PIECES
    writes = []
    for i in range(PIECES):
        here = pl.ds(i * size, size)
        doubled = sum_ref[here, :] + other_ref[here, :] + part[i * size : (i + 1) * size]
        new_weights, new_first, new_second = adam_step(
            weights_ref[here, :], first_ref[here, :], second_ref[here, :], doubled
        )
        for k, (value, out, hbm) in enumerate(
            (
                (new_first, first_out, first_hbm),
                (new_second, second_out, second_hbm),
                (new_weights, weights_out, weights_hbm),
            )
        ):
            out[here, :] = value
            write = pltpu.make_async_copy(out.at[here], hbm.at[here], done.at[i, k])
            write.start()
            writes.append(write)
    for write in writes:
        write.wait()


def finish(bits, a, b, cast, mine_sum, other_sum, weights, first_moment, second_moment):
    shape = jax.ShapeDtypeStruct(weights.shape, jnp.float32)
    return pl.pallas_call(
        functools.partial(finish_kernel, bits),
        in_specs=[pl.BlockSpec(memory_space=pltpu.VMEM)] * 8,
        out_specs=[pl.BlockSpec(memory_space=pltpu.HBM)] * 3,
        out_shape=[shape] * 3,
        scratch_shapes=[pltpu.VMEM(weights.shape, jnp.float32)] * 3
        + [pltpu.SemaphoreType.DMA((PIECES, 3))],
        compiler_params=pltpu.CompilerParams(vmem_limit_bytes=VMEM_LIMIT),
        cost_estimate=pl.CostEstimate(flops=END_FLOPS, bytes_accessed=10**6, transcendentals=0),
        name="finish",
    )(a, b, cast, mine_sum, other_sum, weights, first_moment, second_moment)


def adam_step(weights, first_moment, second_moment, doubled):
    new_first = beta_one * first_moment + ((1.0 - beta_one) * 0.5) * doubled
    new_second = beta_two * second_moment + ((1.0 - beta_two) * 0.25) * (doubled * doubled)
    steep = correct_one / (learn_rate * math.sqrt(correct_two))
    update = new_first / (jnp.sqrt(new_second) * steep + correct_one * adam_eps / learn_rate)
    new_weights = weights * (1.0 - learn_rate * decay_rate) - update
    return (new_weights, new_first, new_second)


def ring_of(blocks, across):
    path = list(range(0, blocks // 2, across))
    if across == 2:
        path += list(range(1, blocks // 2, 2))[::-1]
    pairs = []
    for here, there in zip(path, path[1:] + path[:1]):
        pairs += [(2 * here, 2 * there), (2 * there + 1, 2 * here + 1)]
    return pairs


together = lax.optimization_barrier


def per_device(
    blocks,
    across,
    embeddings,
    pos_ids,
    pos_count,
    label_slot,
    weights,
    first_moment,
    second_moment,
):
    half_way = blocks // 4
    up = ring_of(blocks, across)
    down = [(there, here) for here, there in up]
    swap = [(i, i ^ 1) for i in range(blocks)]
    bits = (label_slot.shape[0] // LANES - 1).bit_length()
    head = embeddings.shape[0] // 2

    def send(value, pairs):
        return lax.ppermute(value, "blk", pairs)

    b = fetch_later(embeddings, head)
    coming = {"up_b": send(b, up)}
    a = prepare(label_slot, pos_ids, pos_count, embeddings, b, head)
    coming["down_a"] = send(a, down)
    coming |= {"up_a": send(a, up), "down_b": send(b, down)}
    mine = halved_cast(weights)
    cast = [mine, send(mine, swap)]
    sums = ()
    waiting = [(a, b)]

    def work(flops):
        return add_gradient(bits, (0, 1), *waiting.pop(0), cast, sums, flops)

    for step in range(1, half_way):
        last = step == half_way - 1
        came = {}
        for message in ("up_b", "down_a", "up_a", "down_b"):
            came[message], waiting, sums = together((coming.pop(message), waiting, sums))
            if message in ("up_b", "down_a") or not last:
                coming[message] = send(came[message], up if message in ("up_a", "up_b") else down)
            if message in ("up_a", "down_b"):
                side = message.split("_")[0]
                waiting.append((came[side + "_a"], came[side + "_b"]))
            if last:
                number = 2 if message == "down_a" else 1
            else:
                number = 1 if step > 1 and message in ("down_a", "up_a") else 0
            for _ in range(min(number, len(waiting))):
                sums = work(LATE_FLOPS if last else FLOPS)
    while waiting:
        sums = work(LATE_FLOPS)
    mine_sum, other_sum = sums
    got = send(other_sum, swap)
    last_b, mine_sum = together((coming["up_b"], mine_sum))
    beside_b = send(last_b, swap)
    last_a, mine_sum = together((coming["down_a"], mine_sum))
    beside_a = send(last_a, swap)
    (mine_sum,) = add_gradient(bits, (0,), last_a, last_b, [mine], [mine_sum], END_FLOPS)
    state = (weights, first_moment, second_moment)
    return finish(bits, beside_a, beside_b, mine, mine_sum, got, *state)


def solution(mesh):
    in_specs = (
        P(("groups", "blk"), None),
        P(("groups", "blk"), None),
        P(("groups", "blk")),
        P(),
        P("blk", None),
        P("blk", None),
        P("blk", None),
    )
    out_specs = (P(("groups", "blk"), None), P(("groups", "blk"), None), P(("groups", "blk"), None))
    return jax.shard_map(
        functools.partial(per_device, mesh.shape["blk"], 4 // mesh.shape["groups"]),
        mesh=mesh,
        in_specs=in_specs,
        out_specs=out_specs,
        check_vma=False,
    )
```

```python
import functools
import math

import jax
import jax.numpy as jnp
from jax import lax
from jax.experimental import pallas as pl
from jax.experimental.pallas import tpu as pltpu
from jax.sharding import PartitionSpec as P

learn_rate = 0.01
beta_one = 0.9
beta_two = 0.95
adam_eps = 1e-08
decay_rate = 0.1
correct_one = 1.0 - 0.9**10
correct_two = 1.0 - 0.95**10

WORD = 32
LANES = 128
PIECES = 4
VMEM_LIMIT = 32 * 1024 * 1024
FLOPS = 2 * 10**8
LATE_FLOPS = 10 * 10**8
END_FLOPS = 100 * 10**8


def power_of_two(exponent, bits, start, sign):
    value = start
    for bit in range(bits):
        factor = 2.0 ** (sign * (1 << bit))
        value = value * jnp.where(((exponent >> bit) & 1) == 1, factor, 1.0)
    return value


def fetch_kernel(
    ids_hbm,
    count_hbm,
    table_hbm,
    docs_hbm,
    b_ref,
    top_ref,
    ids_ref,
    count_ref,
    table_ref,
    done,
):
    docs, width = docs_hbm.shape
    head = docs - b_ref.shape[0]
    pairs = [
        (docs_hbm.at[pl.ds(head, docs - head)], b_ref),
        (ids_hbm, ids_ref),
        (table_hbm, table_ref),
        (count_hbm, count_ref),
    ]
    for j in range(width // LANES):
        tile = docs_hbm.at[pl.ds(0, head), pl.ds(j * LANES, LANES)]
        pairs.append((tile, top_ref.at[pl.ds(j * head, head)]))
    fetches = [pltpu.make_async_copy(*pair, done.at[k]) for k, pair in enumerate(pairs)]
    for fetch in fetches:
        fetch.start()
    for fetch in fetches:
        fetch.wait()


def fetch(label_slot, pos_ids, pos_count, embeddings, head):
    docs, slots = pos_ids.shape
    width = embeddings.shape[1]
    lines = label_slot.shape[0] // LANES
    table = label_slot.reshape(lines, LANES)
    inputs = (pos_ids.T, pos_count.reshape(1, docs), table, embeddings)
    return pl.pallas_call(
        fetch_kernel,
        in_specs=[pl.BlockSpec(memory_space=pltpu.HBM)] * 4,
        out_specs=[pl.BlockSpec(memory_space=pltpu.VMEM)] * 5,
        out_shape=[
            jax.ShapeDtypeStruct((docs - head, width), jnp.bfloat16),
            jax.ShapeDtypeStruct((width // LANES * head, LANES), jnp.bfloat16),
            jax.ShapeDtypeStruct((slots, docs), jnp.int32),
            jax.ShapeDtypeStruct((1, docs), jnp.int32),
            jax.ShapeDtypeStruct((lines, LANES), jnp.int32),
        ],
        scratch_shapes=[pltpu.SemaphoreType.DMA((4 + width // LANES,))],
        compiler_params=pltpu.CompilerParams(vmem_limit_bytes=VMEM_LIMIT),
        name="fetch",
    )(*(pltpu.with_memory_space_constraint(x, pltpu.HBM) for x in inputs))


def prepare_kernel(bits, top_ref, ids_ref, count_ref, table_ref, a_ref):
    slots, docs = ids_ref.shape
    top = top_ref.shape[0]
    a_ref[:top, :] = top_ref[...]
    pairs = table_ref.shape[0] // 2
    starts = range(0, docs, LANES)
    ids = [ids_ref[:, start : start + LANES] for start in starts]
    line_of = [(chunk >> 7) & (pairs - 1) for chunk in ids]
    lane_of = [chunk & (LANES - 1) for chunk in ids]

    def pick(t, found):
        both = table_ref[pl.ds(t, 1), :] | (table_ref[pl.ds(t + pairs, 1), :] << 16)
        line = jnp.broadcast_to(both, (slots, LANES))
        return tuple(
            jnp.where(line_of[i] == t, jnp.take_along_axis(line, lane_of[i], axis=1), found[i])
            for i in range(len(ids))
        )

    found = tuple(jnp.zeros((slots, LANES), jnp.int32) for _ in ids)
    if pairs <= 16:
        for t in range(pairs):
            found = pick(t, found)
    else:
        found = lax.fori_loop(0, pairs, pick, found, unroll=8)
    place = lax.broadcasted_iota(jnp.int32, (slots, LANES), 0)
    for i, start in enumerate(starts):
        row = jnp.where((ids[i] >> 7) < pairs, found[i], found[i] >> 16) & 0xFFFF
        low = (LANES + (row & (LANES - 1))).astype(jnp.float32)
        code = power_of_two(row >> 7, bits, low * 2.0**-64, 1)
        code = jnp.where(place < count_ref[:, start : start + LANES], code, 0.0)
        first = top + i * slots
        a_ref[first : first + slots, :] = code.astype(jnp.bfloat16)


def prepare(top, ids, count, table):
    slots, docs = ids.shape
    vmem = pl.BlockSpec(memory_space=pltpu.VMEM)
    return pl.pallas_call(
        functools.partial(prepare_kernel, (table.shape[0] - 1).bit_length()),
        in_specs=[vmem] * 4,
        out_specs=vmem,
        out_shape=jax.ShapeDtypeStruct((top.shape[0] + slots * docs // LANES, LANES), jnp.bfloat16),
        compiler_params=pltpu.CompilerParams(vmem_limit_bytes=VMEM_LIMIT),
        name="prepare",
    )(top, ids, count, table)


def cast_kernel(weights_ref, cast_ref):
    cast_ref[...] = weights_ref[...].astype(jnp.bfloat16) * 0.5


def halved_cast(weights):
    return pl.pallas_call(
        cast_kernel,
        in_specs=[pl.BlockSpec(memory_space=pltpu.VMEM)],
        out_specs=pl.BlockSpec(memory_space=pltpu.VMEM),
        out_shape=jax.ShapeDtypeStruct(weights.shape, jnp.bfloat16),
        compiler_params=pltpu.CompilerParams(vmem_limit_bytes=VMEM_LIMIT),
        name="cast",
    )(weights)


def signs_of(codes, owner, bits, height):
    docs = codes.shape[1]
    scale = power_of_two(owner * (height // LANES), bits, jnp.float32(2.0**64), -1)
    scaled = codes * scale
    place = jnp.left_shift(
        jnp.ones((WORD, docs), jnp.int32), lax.broadcasted_iota(jnp.int32, (WORD, docs), 0)
    )
    spread = []
    for part in range(height // LANES):
        row = jnp.minimum(scaled * 2.0**-part, 512.0).astype(jnp.int32) - LANES
        word = row >> 5
        bit = jnp.left_shift(jnp.ones_like(row), row & (WORD - 1))
        for w in range(LANES // WORD):
            line = jnp.sum(jnp.where(word == w, bit, 0), axis=0, keepdims=True)
            line = jnp.broadcast_to(line, (WORD, docs))
            spread.append(jnp.where((line & place) != 0, -1.0, 1.0))
    return jnp.concatenate(spread, axis=0)


def doubled_gradient(bits, owners, a_ref, b_ref, w_refs):
    height = w_refs[0].shape[0]
    head, width = b_ref.shape
    tiles = width // LANES
    chunks = 2 * head // LANES
    slots = (a_ref.shape[0] - tiles * head) // chunks
    top = jnp.concatenate([a_ref[j * head : (j + 1) * head, :] for j in range(tiles)], axis=1)
    docs = jnp.concatenate([top, b_ref[...]], axis=0)
    starts = [tiles * head + i * slots for i in range(chunks)]
    codes = jnp.concatenate([a_ref[start : start + slots, :] for start in starts], axis=1)
    codes = codes.astype(jnp.float32)
    weights = jnp.concatenate([ref[...] for ref in w_refs], axis=0)
    halved = lax.dot_general(
        weights, docs, (((1,), (1,)), ((), ())), preferred_element_type=jnp.float32
    )
    me = lax.axis_index("blk")
    signs = jnp.concatenate([signs_of(codes, me ^ owner, bits, height) for owner in owners], axis=0)
    signal = (jnp.tanh(halved) + signs).astype(jnp.bfloat16)
    return jnp.dot(signal, docs, preferred_element_type=jnp.float32)


def gradient_kernel(bits, owners, fresh, a_ref, b_ref, *refs):
    blocks = len(owners)
    w_refs, refs = refs[:blocks], refs[blocks:]
    old_refs, new_refs = refs[:-blocks], refs[-blocks:]
    height = w_refs[0].shape[0]
    part = doubled_gradient(bits, owners, a_ref, b_ref, w_refs)
    for block in range(blocks):
        piece = part[block * height : (block + 1) * height]
        new_refs[block][...] = piece if fresh else old_refs[block][...] + piece


def add_gradient(bits, owners, a, b, weights, sums, flops):
    blocks = len(weights)
    height, width = weights[0].shape
    vmem = pl.BlockSpec(memory_space=pltpu.VMEM)
    sums = list(sums)
    inputs = [a, b, *weights, *sums]
    first_sum = len(inputs) - len(sums)
    return pl.pallas_call(
        functools.partial(gradient_kernel, bits, owners, not sums),
        in_specs=[vmem] * len(inputs),
        out_specs=[vmem] * blocks,
        out_shape=[jax.ShapeDtypeStruct((height, width), jnp.float32)] * blocks,
        input_output_aliases={first_sum + i: i for i in range(len(sums))},
        compiler_params=pltpu.CompilerParams(vmem_limit_bytes=VMEM_LIMIT),
        cost_estimate=pl.CostEstimate(flops=flops, bytes_accessed=10**6, transcendentals=0),
        name="gradient",
    )(*inputs)


def finish_kernel(
    bits,
    a_ref,
    b_ref,
    cast_ref,
    sum_ref,
    other_ref,
    weights_ref,
    first_ref,
    second_ref,
    weights_hbm,
    first_hbm,
    second_hbm,
    weights_out,
    first_out,
    second_out,
    done,
):
    part = doubled_gradient(bits, (0,), a_ref, b_ref, [cast_ref])
    height = part.shape[0]
    size = height // PIECES
    writes = []
    for i in range(PIECES):
        here = pl.ds(i * size, size)
        doubled = sum_ref[here, :] + other_ref[here, :] + part[i * size : (i + 1) * size]
        new_weights, new_first, new_second = adam_step(
            weights_ref[here, :], first_ref[here, :], second_ref[here, :], doubled
        )
        for k, (value, out, hbm) in enumerate(
            (
                (new_first, first_out, first_hbm),
                (new_second, second_out, second_hbm),
                (new_weights, weights_out, weights_hbm),
            )
        ):
            out[here, :] = value
            write = pltpu.make_async_copy(out.at[here], hbm.at[here], done.at[i, k])
            write.start()
            writes.append(write)
    for write in writes:
        write.wait()


def finish(bits, a, b, cast, mine_sum, other_sum, weights, first_moment, second_moment):
    shape = jax.ShapeDtypeStruct(weights.shape, jnp.float32)
    return pl.pallas_call(
        functools.partial(finish_kernel, bits),
        in_specs=[pl.BlockSpec(memory_space=pltpu.VMEM)] * 8,
        out_specs=[pl.BlockSpec(memory_space=pltpu.HBM)] * 3,
        out_shape=[shape] * 3,
        scratch_shapes=[pltpu.VMEM(weights.shape, jnp.float32)] * 3
        + [pltpu.SemaphoreType.DMA((PIECES, 3))],
        compiler_params=pltpu.CompilerParams(vmem_limit_bytes=VMEM_LIMIT),
        cost_estimate=pl.CostEstimate(flops=END_FLOPS, bytes_accessed=10**6, transcendentals=0),
        name="finish",
    )(a, b, cast, mine_sum, other_sum, weights, first_moment, second_moment)


def adam_step(weights, first_moment, second_moment, doubled):
    new_first = beta_one * first_moment + ((1.0 - beta_one) * 0.5) * doubled
    new_second = beta_two * second_moment + ((1.0 - beta_two) * 0.25) * (doubled * doubled)
    steep = correct_one / (learn_rate * math.sqrt(correct_two))
    update = new_first / (jnp.sqrt(new_second) * steep + correct_one * adam_eps / learn_rate)
    new_weights = weights * (1.0 - learn_rate * decay_rate) - update
    return (new_weights, new_first, new_second)


def ring_of(blocks, across):
    path = list(range(0, blocks // 2, across))
    if across == 2:
        path += list(range(1, blocks // 2, 2))[::-1]
    pairs = []
    for here, there in zip(path, path[1:] + path[:1]):
        pairs += [(2 * here, 2 * there), (2 * there + 1, 2 * here + 1)]
    return pairs


together = lax.optimization_barrier


def per_device(
    blocks,
    across,
    embeddings,
    pos_ids,
    pos_count,
    label_slot,
    weights,
    first_moment,
    second_moment,
):
    half_way = blocks // 4
    up = ring_of(blocks, across)
    down = [(there, here) for here, there in up]
    swap = [(i, i ^ 1) for i in range(blocks)]
    bits = (label_slot.shape[0] // LANES - 1).bit_length()
    head = embeddings.shape[0] // 2

    def send(value, pairs):
        return lax.ppermute(value, "blk", pairs)

    b, *rest = fetch(label_slot, pos_ids, pos_count, embeddings, head)
    coming = {"up_b": send(b, up)}
    a = prepare(*rest)
    coming["down_a"] = send(a, down)
    coming |= {"up_a": send(a, up), "down_b": send(b, down)}
    mine = halved_cast(weights)
    cast = [mine, send(mine, swap)]
    sums = ()
    waiting = [(a, b)]

    def work(flops):
        return add_gradient(bits, (0, 1), *waiting.pop(0), cast, sums, flops)

    for step in range(1, half_way):
        last = step == half_way - 1
        came = {}
        for message in ("up_b", "down_a", "up_a", "down_b"):
            came[message], waiting, sums = together((coming.pop(message), waiting, sums))
            if message in ("up_b", "down_a") or not last:
                coming[message] = send(came[message], up if message in ("up_a", "up_b") else down)
            if message in ("up_a", "down_b"):
                side = message.split("_")[0]
                waiting.append((came[side + "_a"], came[side + "_b"]))
            if last:
                number = 2 if message == "down_a" else 1
            else:
                number = 1 if step > 1 and message in ("down_a", "up_a") else 0
            for _ in range(min(number, len(waiting))):
                sums = work(LATE_FLOPS if last else FLOPS)
    while waiting:
        sums = work(LATE_FLOPS)
    mine_sum, other_sum = sums
    got = send(other_sum, swap)
    last_b, mine_sum = together((coming["up_b"], mine_sum))
    beside_b = send(last_b, swap)
    last_a, mine_sum = together((coming["down_a"], mine_sum))
    beside_a = send(last_a, swap)
    (mine_sum,) = add_gradient(bits, (0,), last_a, last_b, [mine], [mine_sum], END_FLOPS)
    state = (weights, first_moment, second_moment)
    return finish(bits, beside_a, beside_b, mine, mine_sum, got, *state)


def solution(mesh):
    in_specs = (
        P(("groups", "blk"), None),
        P(("groups", "blk"), None),
        P(("groups", "blk")),
        P(),
        P("blk", None),
        P("blk", None),
        P("blk", None),
    )
    out_specs = (P(("groups", "blk"), None), P(("groups", "blk"), None), P(("groups", "blk"), None))
    return jax.shard_map(
        functools.partial(per_device, mesh.shape["blk"], 4 // mesh.shape["groups"]),
        mesh=mesh,
        in_specs=in_specs,
        out_specs=out_specs,
        check_vma=False,
    )
```

```python
import functools
import math

import jax
import jax.numpy as jnp
from jax import lax
from jax.experimental import pallas as pl
from jax.experimental.pallas import tpu as pltpu
from jax.sharding import PartitionSpec as P

learn_rate = 0.01
beta_one = 0.9
beta_two = 0.95
adam_eps = 1e-08
decay_rate = 0.1
correct_one = 1.0 - 0.9**10
correct_two = 1.0 - 0.95**10

WORD = 32
LANES = 128
PIECES = 2
VMEM_LIMIT = 32 * 1024 * 1024
FLOPS = 2 * 10**8
LATE_FLOPS = 10 * 10**8
END_FLOPS = 100 * 10**8


def power_of_two(exponent, bits, start, sign):
    value = start
    for bit in range(bits):
        factor = 2.0 ** (sign * (1 << bit))
        value = value * jnp.where(((exponent >> bit) & 1) == 1, factor, 1.0)
    return value


def fetch_kernel(
    ids_hbm,
    count_hbm,
    table_hbm,
    docs_hbm,
    b_ref,
    top_ref,
    ids_ref,
    count_ref,
    table_ref,
    done,
):
    docs = docs_hbm.shape[0]
    head = docs - b_ref.shape[0]
    pairs = [
        (docs_hbm.at[pl.ds(head, docs - head)], b_ref),
        (docs_hbm.at[pl.ds(0, head)], top_ref),
        (ids_hbm, ids_ref),
        (table_hbm, table_ref),
        (count_hbm, count_ref),
    ]
    fetches = [pltpu.make_async_copy(*pair, done.at[k]) for k, pair in enumerate(pairs)]
    for fetch in fetches:
        fetch.start()
    for fetch in fetches:
        fetch.wait()


def fetch(label_slot, pos_ids, pos_count, embeddings, head):
    docs, slots = pos_ids.shape
    width = embeddings.shape[1]
    lines = label_slot.shape[0] // LANES
    table = label_slot.reshape(lines, LANES)
    inputs = (pos_ids.T, pos_count.reshape(1, docs), table, embeddings)
    return pl.pallas_call(
        fetch_kernel,
        in_specs=[pl.BlockSpec(memory_space=pltpu.HBM)] * 4,
        out_specs=[pl.BlockSpec(memory_space=pltpu.VMEM)] * 5,
        out_shape=[
            jax.ShapeDtypeStruct((docs - head, width), jnp.bfloat16),
            jax.ShapeDtypeStruct((head, width), jnp.bfloat16),
            jax.ShapeDtypeStruct((slots, docs), jnp.int32),
            jax.ShapeDtypeStruct((1, docs), jnp.int32),
            jax.ShapeDtypeStruct((lines, LANES), jnp.int32),
        ],
        scratch_shapes=[pltpu.SemaphoreType.DMA((5,))],
        compiler_params=pltpu.CompilerParams(vmem_limit_bytes=VMEM_LIMIT),
        name="fetch",
    )(*(pltpu.with_memory_space_constraint(x, pltpu.HBM) for x in inputs))


def prepare_kernel(bits, top_ref, ids_ref, count_ref, table_ref, a_ref):
    slots, docs = ids_ref.shape
    head, width = top_ref.shape
    top = width // LANES * head
    for j in range(width // LANES):
        a_ref[j * head : (j + 1) * head, :] = top_ref[:, j * LANES : (j + 1) * LANES]
    pairs = table_ref.shape[0] // 2
    starts = range(0, docs, LANES)
    ids = [ids_ref[:, start : start + LANES] for start in starts]
    line_of = [(chunk >> 7) & (pairs - 1) for chunk in ids]
    lane_of = [chunk & (LANES - 1) for chunk in ids]

    def pick(t, found):
        both = table_ref[pl.ds(t, 1), :] | (table_ref[pl.ds(t + pairs, 1), :] << 16)
        line = jnp.broadcast_to(both, (slots, LANES))
        return tuple(
            jnp.where(line_of[i] == t, jnp.take_along_axis(line, lane_of[i], axis=1), found[i])
            for i in range(len(ids))
        )

    found = tuple(jnp.zeros((slots, LANES), jnp.int32) for _ in ids)
    if pairs <= 16:
        for t in range(pairs):
            found = pick(t, found)
    else:
        found = lax.fori_loop(0, pairs, pick, found, unroll=8)
    place = lax.broadcasted_iota(jnp.int32, (slots, LANES), 0)
    for i, start in enumerate(starts):
        row = jnp.where((ids[i] >> 7) < pairs, found[i], found[i] >> 16) & 0xFFFF
        low = (LANES + (row & (LANES - 1))).astype(jnp.float32)
        code = power_of_two(row >> 7, bits, low * 2.0**-64, 1)
        code = jnp.where(place < count_ref[:, start : start + LANES], code, 0.0)
        first = top + i * slots
        a_ref[first : first + slots, :] = code.astype(jnp.bfloat16)


def prepare(top, ids, count, table):
    slots, docs = ids.shape
    vmem = pl.BlockSpec(memory_space=pltpu.VMEM)
    return pl.pallas_call(
        functools.partial(prepare_kernel, (table.shape[0] - 1).bit_length()),
        in_specs=[vmem] * 4,
        out_specs=vmem,
        out_shape=jax.ShapeDtypeStruct(((top.size + slots * docs) // LANES, LANES), jnp.bfloat16),
        compiler_params=pltpu.CompilerParams(vmem_limit_bytes=VMEM_LIMIT),
        name="prepare",
    )(top, ids, count, table)


def cast_kernel(weights_ref, cast_ref):
    cast_ref[...] = weights_ref[...].astype(jnp.bfloat16) * 0.5


def halved_cast(weights):
    return pl.pallas_call(
        cast_kernel,
        in_specs=[pl.BlockSpec(memory_space=pltpu.VMEM)],
        out_specs=pl.BlockSpec(memory_space=pltpu.VMEM),
        out_shape=jax.ShapeDtypeStruct(weights.shape, jnp.bfloat16),
        compiler_params=pltpu.CompilerParams(vmem_limit_bytes=VMEM_LIMIT),
        name="cast",
    )(weights)


def signs_of(codes, owner, bits, height):
    docs = codes.shape[1]
    scale = power_of_two(owner * (height // LANES), bits, jnp.float32(2.0**64), -1)
    scaled = codes * scale
    place = jnp.left_shift(
        jnp.ones((WORD, docs), jnp.int32), lax.broadcasted_iota(jnp.int32, (WORD, docs), 0)
    )
    spread = []
    for part in range(height // LANES):
        row = jnp.minimum(scaled * 2.0**-part, 512.0).astype(jnp.int32) - LANES
        word = row >> 5
        bit = jnp.left_shift(jnp.ones_like(row), row & (WORD - 1))
        for w in range(LANES // WORD):
            line = jnp.sum(jnp.where(word == w, bit, 0), axis=0, keepdims=True)
            line = jnp.broadcast_to(line, (WORD, docs))
            spread.append(jnp.where((line & place) != 0, -1.0, 1.0))
    return jnp.concatenate(spread, axis=0)


def doubled_gradient(bits, owners, a_ref, b_ref, w_refs):
    height = w_refs[0].shape[0]
    head, width = b_ref.shape
    tiles = width // LANES
    chunks = 2 * head // LANES
    slots = (a_ref.shape[0] - tiles * head) // chunks
    top = jnp.concatenate([a_ref[j * head : (j + 1) * head, :] for j in range(tiles)], axis=1)
    docs = jnp.concatenate([top, b_ref[...]], axis=0)
    starts = [tiles * head + i * slots for i in range(chunks)]
    codes = jnp.concatenate([a_ref[start : start + slots, :] for start in starts], axis=1)
    codes = codes.astype(jnp.float32)
    weights = jnp.concatenate([ref[...] for ref in w_refs], axis=0)
    halved = lax.dot_general(
        weights, docs, (((1,), (1,)), ((), ())), preferred_element_type=jnp.float32
    )
    me = lax.axis_index("blk")
    signs = jnp.concatenate([signs_of(codes, me ^ owner, bits, height) for owner in owners], axis=0)
    signal = (jnp.tanh(halved) + signs).astype(jnp.bfloat16)
    return jnp.dot(signal, docs, preferred_element_type=jnp.float32)


def gradient_kernel(bits, owners, fresh, a_ref, b_ref, *refs):
    blocks = len(owners)
    w_refs, refs = refs[:blocks], refs[blocks:]
    old_refs, new_refs = refs[:-blocks], refs[-blocks:]
    height = w_refs[0].shape[0]
    part = doubled_gradient(bits, owners, a_ref, b_ref, w_refs)
    for block in range(blocks):
        piece = part[block * height : (block + 1) * height]
        new_refs[block][...] = piece if fresh else old_refs[block][...] + piece


def add_gradient(bits, owners, a, b, weights, sums, flops):
    blocks = len(weights)
    height, width = weights[0].shape
    vmem = pl.BlockSpec(memory_space=pltpu.VMEM)
    sums = list(sums)
    inputs = [a, b, *weights, *sums]
    first_sum = len(inputs) - len(sums)
    return pl.pallas_call(
        functools.partial(gradient_kernel, bits, owners, not sums),
        in_specs=[vmem] * len(inputs),
        out_specs=[vmem] * blocks,
        out_shape=[jax.ShapeDtypeStruct((height, width), jnp.float32)] * blocks,
        input_output_aliases={first_sum + i: i for i in range(len(sums))},
        compiler_params=pltpu.CompilerParams(vmem_limit_bytes=VMEM_LIMIT),
        cost_estimate=pl.CostEstimate(flops=flops, bytes_accessed=10**6, transcendentals=0),
        name="gradient",
    )(*inputs)


def finish_kernel(
    bits,
    a_ref,
    b_ref,
    cast_ref,
    sum_ref,
    other_ref,
    weights_ref,
    first_ref,
    second_ref,
    weights_hbm,
    first_hbm,
    second_hbm,
    weights_out,
    first_out,
    second_out,
    done,
):
    part = doubled_gradient(bits, (0,), a_ref, b_ref, [cast_ref])
    height = part.shape[0]
    size = height // PIECES
    writes = []
    for i in range(PIECES):
        here = pl.ds(i * size, size)
        doubled = sum_ref[here, :] + other_ref[here, :] + part[i * size : (i + 1) * size]
        new_weights, new_first, new_second = adam_step(
            weights_ref[here, :], first_ref[here, :], second_ref[here, :], doubled
        )
        for k, (value, out, hbm) in enumerate(
            (
                (new_first, first_out, first_hbm),
                (new_second, second_out, second_hbm),
                (new_weights, weights_out, weights_hbm),
            )
        ):
            out[here, :] = value
            write = pltpu.make_async_copy(out.at[here], hbm.at[here], done.at[i, k])
            write.start()
            writes.append(write)
    for write in writes:
        write.wait()


def finish(bits, a, b, cast, mine_sum, other_sum, weights, first_moment, second_moment):
    shape = jax.ShapeDtypeStruct(weights.shape, jnp.float32)
    return pl.pallas_call(
        functools.partial(finish_kernel, bits),
        in_specs=[pl.BlockSpec(memory_space=pltpu.VMEM)] * 8,
        out_specs=[pl.BlockSpec(memory_space=pltpu.HBM)] * 3,
        out_shape=[shape] * 3,
        scratch_shapes=[pltpu.VMEM(weights.shape, jnp.float32)] * 3
        + [pltpu.SemaphoreType.DMA((PIECES, 3))],
        compiler_params=pltpu.CompilerParams(vmem_limit_bytes=VMEM_LIMIT),
        cost_estimate=pl.CostEstimate(flops=END_FLOPS, bytes_accessed=10**6, transcendentals=0),
        name="finish",
    )(a, b, cast, mine_sum, other_sum, weights, first_moment, second_moment)


def adam_step(weights, first_moment, second_moment, doubled):
    new_first = beta_one * first_moment + ((1.0 - beta_one) * 0.5) * doubled
    new_second = beta_two * second_moment + ((1.0 - beta_two) * 0.25) * (doubled * doubled)
    steep = correct_one / (learn_rate * math.sqrt(correct_two))
    update = new_first / (jnp.sqrt(new_second) * steep + correct_one * adam_eps / learn_rate)
    new_weights = weights * (1.0 - learn_rate * decay_rate) - update
    return (new_weights, new_first, new_second)


def ring_of(blocks, across):
    path = list(range(0, blocks // 2, across))
    if across == 2:
        path += list(range(1, blocks // 2, 2))[::-1]
    pairs = []
    for here, there in zip(path, path[1:] + path[:1]):
        pairs += [(2 * here, 2 * there), (2 * there + 1, 2 * here + 1)]
    return pairs


together = lax.optimization_barrier


def per_device(
    blocks,
    across,
    embeddings,
    pos_ids,
    pos_count,
    label_slot,
    weights,
    first_moment,
    second_moment,
):
    half_way = blocks // 4
    up = ring_of(blocks, across)
    down = [(there, here) for here, there in up]
    swap = [(i, i ^ 1) for i in range(blocks)]
    bits = (label_slot.shape[0] // LANES - 1).bit_length()
    head = embeddings.shape[0] // 2

    def send(value, pairs):
        return lax.ppermute(value, "blk", pairs)

    b, *rest = fetch(label_slot, pos_ids, pos_count, embeddings, head)
    coming = {"up_b": send(b, up)}
    a = prepare(*rest)
    coming["down_a"] = send(a, down)
    coming |= {"up_a": send(a, up), "down_b": send(b, down)}
    mine = halved_cast(weights)
    cast = [mine, send(mine, swap)]
    sums = ()
    waiting = [(a, b)]

    def work(flops):
        return add_gradient(bits, (0, 1), *waiting.pop(0), cast, sums, flops)

    for step in range(1, half_way):
        last = step == half_way - 1
        came = {}
        for message in ("up_b", "down_a", "up_a", "down_b"):
            came[message], waiting, sums = together((coming.pop(message), waiting, sums))
            if message in ("up_b", "down_a") or not last:
                coming[message] = send(came[message], up if message in ("up_a", "up_b") else down)
            if message in ("up_a", "down_b"):
                side = message.split("_")[0]
                waiting.append((came[side + "_a"], came[side + "_b"]))
            if last:
                number = 2 if message == "down_a" else 1
            else:
                number = 1 if step > 1 and message in ("down_a", "up_a") else 0
            for _ in range(min(number, len(waiting))):
                sums = work(LATE_FLOPS if last else FLOPS)
    while waiting:
        sums = work(LATE_FLOPS)
    mine_sum, other_sum = sums
    got = send(other_sum, swap)
    last_b, mine_sum = together((coming["up_b"], mine_sum))
    beside_b = send(last_b, swap)
    last_a, mine_sum = together((coming["down_a"], mine_sum))
    beside_a = send(last_a, swap)
    (mine_sum,) = add_gradient(bits, (0,), last_a, last_b, [mine], [mine_sum], END_FLOPS)
    state = (weights, first_moment, second_moment)
    return finish(bits, beside_a, beside_b, mine, mine_sum, got, *state)


def solution(mesh):
    in_specs = (
        P(("groups", "blk"), None),
        P(("groups", "blk"), None),
        P(("groups", "blk")),
        P(),
        P("blk", None),
        P("blk", None),
        P("blk", None),
    )
    out_specs = (P(("groups", "blk"), None), P(("groups", "blk"), None), P(("groups", "blk"), None))
    return jax.shard_map(
        functools.partial(per_device, mesh.shape["blk"], 4 // mesh.shape["groups"]),
        mesh=mesh,
        in_specs=in_specs,
        out_specs=out_specs,
        check_vma=False,
    )
```

```python
import functools
import math

import jax
import jax.numpy as jnp
from jax import lax
from jax.experimental import pallas as pl
from jax.experimental.pallas import tpu as pltpu
from jax.sharding import PartitionSpec as P

learn_rate = 0.01
beta_one = 0.9
beta_two = 0.95
adam_eps = 1e-08
decay_rate = 0.1
correct_one = 1.0 - 0.9**10
correct_two = 1.0 - 0.95**10

WORD = 32
LANES = 128
PIECES = 2
VMEM_LIMIT = 32 * 1024 * 1024
FLOPS = 8 * 10**8
LATE_FLOPS = 10 * 10**8
END_FLOPS = 100 * 10**8


def power_of_two(exponent, bits, start, sign):
    value = start
    for bit in range(bits):
        factor = 2.0 ** (sign * (1 << bit))
        value = value * jnp.where(((exponent >> bit) & 1) == 1, factor, 1.0)
    return value


def fetch_kernel(
    ids_hbm,
    count_hbm,
    table_hbm,
    docs_hbm,
    b_ref,
    top_ref,
    ids_ref,
    count_ref,
    table_ref,
    done,
):
    docs = docs_hbm.shape[0]
    head = docs - b_ref.shape[0]
    pairs = [
        (docs_hbm.at[pl.ds(head, docs - head)], b_ref),
        (docs_hbm.at[pl.ds(0, head)], top_ref),
        (ids_hbm, ids_ref),
        (table_hbm, table_ref),
        (count_hbm, count_ref),
    ]
    fetches = [pltpu.make_async_copy(*pair, done.at[k]) for k, pair in enumerate(pairs)]
    for fetch in fetches:
        fetch.start()
    for fetch in fetches:
        fetch.wait()


def fetch(label_slot, pos_ids, pos_count, embeddings, head):
    docs, slots = pos_ids.shape
    width = embeddings.shape[1]
    lines = label_slot.shape[0] // LANES
    table = label_slot.reshape(lines, LANES)
    inputs = (pos_ids.T, pos_count.reshape(1, docs), table, embeddings)
    return pl.pallas_call(
        fetch_kernel,
        in_specs=[pl.BlockSpec(memory_space=pltpu.HBM)] * 4,
        out_specs=[pl.BlockSpec(memory_space=pltpu.VMEM)] * 5,
        out_shape=[
            jax.ShapeDtypeStruct((docs - head, width), jnp.bfloat16),
            jax.ShapeDtypeStruct((head, width), jnp.bfloat16),
            jax.ShapeDtypeStruct((slots, docs), jnp.int32),
            jax.ShapeDtypeStruct((1, docs), jnp.int32),
            jax.ShapeDtypeStruct((lines, LANES), jnp.int32),
        ],
        scratch_shapes=[pltpu.SemaphoreType.DMA((5,))],
        compiler_params=pltpu.CompilerParams(vmem_limit_bytes=VMEM_LIMIT),
        name="fetch",
    )(*(pltpu.with_memory_space_constraint(x, pltpu.HBM) for x in inputs))


def prepare_kernel(bits, top_ref, ids_ref, count_ref, table_ref, a_ref):
    slots, docs = ids_ref.shape
    head, width = top_ref.shape
    top = width // LANES * head
    for j in range(width // LANES):
        a_ref[j * head : (j + 1) * head, :] = top_ref[:, j * LANES : (j + 1) * LANES]
    pairs = table_ref.shape[0] // 2
    starts = range(0, docs, LANES)
    ids = [ids_ref[:, start : start + LANES] for start in starts]
    line_of = [(chunk >> 7) & (pairs - 1) for chunk in ids]
    lane_of = [chunk & (LANES - 1) for chunk in ids]

    def pick(t, found):
        both = table_ref[pl.ds(t, 1), :] | (table_ref[pl.ds(t + pairs, 1), :] << 16)
        line = jnp.broadcast_to(both, (slots, LANES))
        return tuple(
            jnp.where(line_of[i] == t, jnp.take_along_axis(line, lane_of[i], axis=1), found[i])
            for i in range(len(ids))
        )

    found = tuple(jnp.zeros((slots, LANES), jnp.int32) for _ in ids)
    if pairs <= 16:
        for t in range(pairs):
            found = pick(t, found)
    else:
        found = lax.fori_loop(0, pairs, pick, found, unroll=8)
    place = lax.broadcasted_iota(jnp.int32, (slots, LANES), 0)
    for i, start in enumerate(starts):
        row = jnp.where((ids[i] >> 7) < pairs, found[i], found[i] >> 16) & 0xFFFF
        low = (LANES + (row & (LANES - 1))).astype(jnp.float32)
        code = power_of_two(row >> 7, bits, low * 2.0**-64, 1)
        code = jnp.where(place < count_ref[:, start : start + LANES], code, 0.0)
        first = top + i * slots
        a_ref[first : first + slots, :] = code.astype(jnp.bfloat16)


def prepare(top, ids, count, table):
    slots, docs = ids.shape
    vmem = pl.BlockSpec(memory_space=pltpu.VMEM)
    return pl.pallas_call(
        functools.partial(prepare_kernel, (table.shape[0] - 1).bit_length()),
        in_specs=[vmem] * 4,
        out_specs=vmem,
        out_shape=jax.ShapeDtypeStruct(((top.size + slots * docs) // LANES, LANES), jnp.bfloat16),
        compiler_params=pltpu.CompilerParams(vmem_limit_bytes=VMEM_LIMIT),
        name="prepare",
    )(top, ids, count, table)


def cast_kernel(weights_ref, cast_ref):
    cast_ref[...] = weights_ref[...].astype(jnp.bfloat16) * 0.5


def halved_cast(weights):
    return pl.pallas_call(
        cast_kernel,
        in_specs=[pl.BlockSpec(memory_space=pltpu.VMEM)],
        out_specs=pl.BlockSpec(memory_space=pltpu.VMEM),
        out_shape=jax.ShapeDtypeStruct(weights.shape, jnp.bfloat16),
        compiler_params=pltpu.CompilerParams(vmem_limit_bytes=VMEM_LIMIT),
        name="cast",
    )(weights)


def signs_of(codes, owner, bits, height):
    docs = codes.shape[1]
    scale = power_of_two(owner * (height // LANES), bits, jnp.float32(2.0**64), -1)
    scaled = codes * scale
    place = jnp.left_shift(
        jnp.ones((WORD, docs), jnp.int32), lax.broadcasted_iota(jnp.int32, (WORD, docs), 0)
    )
    spread = []
    for part in range(height // LANES):
        row = jnp.minimum(scaled * 2.0**-part, 512.0).astype(jnp.int32) - LANES
        word = row >> 5
        bit = jnp.left_shift(jnp.ones_like(row), row & (WORD - 1))
        for w in range(LANES // WORD):
            line = jnp.sum(jnp.where(word == w, bit, 0), axis=0, keepdims=True)
            line = jnp.broadcast_to(line, (WORD, docs))
            spread.append(jnp.where((line & place) != 0, -1.0, 1.0))
    return jnp.concatenate(spread, axis=0)


def doubled_gradient(bits, owners, a_ref, b_ref, w_refs):
    height = w_refs[0].shape[0]
    bits, head = bits
    later, width = b_ref.shape
    tiles = width // LANES
    chunks = (head + later) // LANES
    slots = (a_ref.shape[0] - tiles * head) // chunks
    top = jnp.concatenate([a_ref[j * head : (j + 1) * head, :] for j in range(tiles)], axis=1)
    docs = jnp.concatenate([top, b_ref[...]], axis=0)
    starts = [tiles * head + i * slots for i in range(chunks)]
    codes = jnp.concatenate([a_ref[start : start + slots, :] for start in starts], axis=1)
    codes = codes.astype(jnp.float32)
    weights = jnp.concatenate([ref[...] for ref in w_refs], axis=0)
    halved = lax.dot_general(
        weights, docs, (((1,), (1,)), ((), ())), preferred_element_type=jnp.float32
    )
    me = lax.axis_index("blk")
    signs = jnp.concatenate([signs_of(codes, me ^ owner, bits, height) for owner in owners], axis=0)
    signal = (jnp.tanh(halved) + signs).astype(jnp.bfloat16)
    return jnp.dot(signal, docs, preferred_element_type=jnp.float32)


def gradient_kernel(bits, owners, fresh, a_ref, b_ref, *refs):
    blocks = len(owners)
    w_refs, refs = refs[:blocks], refs[blocks:]
    old_refs, new_refs = refs[:-blocks], refs[-blocks:]
    height = w_refs[0].shape[0]
    part = doubled_gradient(bits, owners, a_ref, b_ref, w_refs)
    for block in range(blocks):
        piece = part[block * height : (block + 1) * height]
        new_refs[block][...] = piece if fresh else old_refs[block][...] + piece


def add_gradient(bits, owners, a, b, weights, sums, flops):
    blocks = len(weights)
    height, width = weights[0].shape
    vmem = pl.BlockSpec(memory_space=pltpu.VMEM)
    sums = list(sums)
    inputs = [a, b, *weights, *sums]
    first_sum = len(inputs) - len(sums)
    return pl.pallas_call(
        functools.partial(gradient_kernel, bits, owners, not sums),
        in_specs=[vmem] * len(inputs),
        out_specs=[vmem] * blocks,
        out_shape=[jax.ShapeDtypeStruct((height, width), jnp.float32)] * blocks,
        input_output_aliases={first_sum + i: i for i in range(len(sums))},
        compiler_params=pltpu.CompilerParams(vmem_limit_bytes=VMEM_LIMIT),
        cost_estimate=pl.CostEstimate(flops=flops, bytes_accessed=10**6, transcendentals=0),
        name="gradient",
    )(*inputs)


def finish_kernel(
    bits,
    a_ref,
    b_ref,
    cast_ref,
    sum_ref,
    other_ref,
    weights_ref,
    first_ref,
    second_ref,
    weights_hbm,
    first_hbm,
    second_hbm,
    weights_out,
    first_out,
    second_out,
    done,
):
    part = doubled_gradient(bits, (0,), a_ref, b_ref, [cast_ref])
    height = part.shape[0]
    size = height // PIECES
    writes = []
    for i in range(PIECES):
        here = pl.ds(i * size, size)
        doubled = sum_ref[here, :] + other_ref[here, :] + part[i * size : (i + 1) * size]
        new_weights, new_first, new_second = adam_step(
            weights_ref[here, :], first_ref[here, :], second_ref[here, :], doubled
        )
        for k, (value, out, hbm) in enumerate(
            (
                (new_first, first_out, first_hbm),
                (new_second, second_out, second_hbm),
                (new_weights, weights_out, weights_hbm),
            )
        ):
            out[here, :] = value
            write = pltpu.make_async_copy(out.at[here], hbm.at[here], done.at[i, k])
            write.start()
            writes.append(write)
    for write in writes:
        write.wait()


def finish(bits, a, b, cast, mine_sum, other_sum, weights, first_moment, second_moment):
    shape = jax.ShapeDtypeStruct(weights.shape, jnp.float32)
    return pl.pallas_call(
        functools.partial(finish_kernel, bits),
        in_specs=[pl.BlockSpec(memory_space=pltpu.VMEM)] * 8,
        out_specs=[pl.BlockSpec(memory_space=pltpu.HBM)] * 3,
        out_shape=[shape] * 3,
        scratch_shapes=[pltpu.VMEM(weights.shape, jnp.float32)] * 3
        + [pltpu.SemaphoreType.DMA((PIECES, 3))],
        compiler_params=pltpu.CompilerParams(vmem_limit_bytes=VMEM_LIMIT),
        cost_estimate=pl.CostEstimate(flops=END_FLOPS, bytes_accessed=10**6, transcendentals=0),
        name="finish",
    )(a, b, cast, mine_sum, other_sum, weights, first_moment, second_moment)


def adam_step(weights, first_moment, second_moment, doubled):
    new_first = beta_one * first_moment + ((1.0 - beta_one) * 0.5) * doubled
    new_second = beta_two * second_moment + ((1.0 - beta_two) * 0.25) * (doubled * doubled)
    steep = correct_one / (learn_rate * math.sqrt(correct_two))
    update = new_first / (jnp.sqrt(new_second) * steep + correct_one * adam_eps / learn_rate)
    new_weights = weights * (1.0 - learn_rate * decay_rate) - update
    return (new_weights, new_first, new_second)


def ring_of(blocks, across):
    path = list(range(0, blocks // 2, across))
    if across == 2:
        path += list(range(1, blocks // 2, 2))[::-1]
    pairs = []
    for here, there in zip(path, path[1:] + path[:1]):
        pairs += [(2 * here, 2 * there), (2 * there + 1, 2 * here + 1)]
    return pairs


together = lax.optimization_barrier


def per_device(
    blocks,
    across,
    embeddings,
    pos_ids,
    pos_count,
    label_slot,
    weights,
    first_moment,
    second_moment,
):
    half_way = blocks // 4
    up = ring_of(blocks, across)
    down = [(there, here) for here, there in up]
    swap = [(i, i ^ 1) for i in range(blocks)]
    bits = (label_slot.shape[0] // LANES - 1).bit_length()
    head = embeddings.shape[0] * 7 // 16
    layout = (bits, head)

    def send(value, pairs):
        return lax.ppermute(value, "blk", pairs)

    b, *rest = fetch(label_slot, pos_ids, pos_count, embeddings, head)
    coming = {"up_b": send(b, up)}
    a = prepare(*rest)
    coming["down_a"] = send(a, down)
    coming |= {"up_a": send(a, up), "down_b": send(b, down)}
    mine = halved_cast(weights)
    cast = [mine, send(mine, swap)]
    sums = ()
    waiting = [(a, b)]

    def work(flops):
        return add_gradient(layout, (0, 1), *waiting.pop(0), cast, sums, flops)

    for step in range(1, half_way):
        last = step == half_way - 1
        came = {}
        for message in ("up_b", "down_a", "up_a", "down_b"):
            came[message], waiting, sums = together((coming.pop(message), waiting, sums))
            if message in ("up_b", "down_a") or not last:
                coming[message] = send(came[message], up if message in ("up_a", "up_b") else down)
            if message in ("up_a", "down_b"):
                side = message.split("_")[0]
                waiting.append((came[side + "_a"], came[side + "_b"]))
            if last:
                number = 2 if message == "down_a" else 1
            else:
                number = 1 if step > 1 and message in ("down_a", "up_a") else 0
            for _ in range(min(number, len(waiting))):
                sums = work(LATE_FLOPS if last else FLOPS)
    while waiting:
        sums = work(LATE_FLOPS)
    mine_sum, other_sum = sums
    got = send(other_sum, swap)
    last_b, mine_sum = together((coming["up_b"], mine_sum))
    beside_b = send(last_b, swap)
    last_a, mine_sum = together((coming["down_a"], mine_sum))
    beside_a = send(last_a, swap)
    (mine_sum,) = add_gradient(layout, (0,), last_a, last_b, [mine], [mine_sum], END_FLOPS)
    state = (weights, first_moment, second_moment)
    return finish(layout, beside_a, beside_b, mine, mine_sum, got, *state)


def solution(mesh):
    in_specs = (
        P(("groups", "blk"), None),
        P(("groups", "blk"), None),
        P(("groups", "blk")),
        P(),
        P("blk", None),
        P("blk", None),
        P("blk", None),
    )
    out_specs = (P(("groups", "blk"), None), P(("groups", "blk"), None), P(("groups", "blk"), None))
    return jax.shard_map(
        functools.partial(per_device, mesh.shape["blk"], 4 // mesh.shape["groups"]),
        mesh=mesh,
        in_specs=in_specs,
        out_specs=out_specs,
        check_vma=False,
    )
```

```python
import functools
import math

import jax
import jax.numpy as jnp
from jax import lax
from jax.experimental import pallas as pl
from jax.experimental.pallas import tpu as pltpu
from jax.sharding import PartitionSpec as P

learn_rate = 0.01
beta_one = 0.9
beta_two = 0.95
adam_eps = 1e-08
decay_rate = 0.1
correct_one = 1.0 - 0.9**10
correct_two = 1.0 - 0.95**10

WORD = 32
LANES = 128
PIECES = 2
VMEM_LIMIT = 32 * 1024 * 1024
FLOPS = 2 * 10**8
LATE_FLOPS = 5 * 10**8
END_FLOPS = 100 * 10**8


def power_of_two(exponent, bits, start, sign):
    value = start
    for bit in range(bits):
        factor = 2.0 ** (sign * (1 << bit))
        value = value * jnp.where(((exponent >> bit) & 1) == 1, factor, 1.0)
    return value


def fetch_kernel(
    ids_hbm,
    count_hbm,
    table_hbm,
    docs_hbm,
    b_ref,
    top_ref,
    ids_ref,
    count_ref,
    table_ref,
    done,
):
    docs = docs_hbm.shape[0]
    head = docs - b_ref.shape[0]
    pairs = [
        (docs_hbm.at[pl.ds(head, docs - head)], b_ref),
        (docs_hbm.at[pl.ds(0, head)], top_ref),
        (ids_hbm, ids_ref),
        (table_hbm, table_ref),
        (count_hbm, count_ref),
    ]
    fetches = [pltpu.make_async_copy(*pair, done.at[k]) for k, pair in enumerate(pairs)]
    for fetch in fetches:
        fetch.start()
    for fetch in fetches:
        fetch.wait()


def fetch(label_slot, pos_ids, pos_count, embeddings, head):
    docs, slots = pos_ids.shape
    width = embeddings.shape[1]
    lines = label_slot.shape[0] // LANES
    table = label_slot.reshape(lines, LANES)
    inputs = (pos_ids.T, pos_count.reshape(1, docs), table, embeddings)
    return pl.pallas_call(
        fetch_kernel,
        in_specs=[pl.BlockSpec(memory_space=pltpu.HBM)] * 4,
        out_specs=[pl.BlockSpec(memory_space=pltpu.VMEM)] * 5,
        out_shape=[
            jax.ShapeDtypeStruct((docs - head, width), jnp.bfloat16),
            jax.ShapeDtypeStruct((head, width), jnp.bfloat16),
            jax.ShapeDtypeStruct((slots, docs), jnp.int32),
            jax.ShapeDtypeStruct((1, docs), jnp.int32),
            jax.ShapeDtypeStruct((lines, LANES), jnp.int32),
        ],
        scratch_shapes=[pltpu.SemaphoreType.DMA((5,))],
        compiler_params=pltpu.CompilerParams(vmem_limit_bytes=VMEM_LIMIT),
        name="fetch",
    )(*(pltpu.with_memory_space_constraint(x, pltpu.HBM) for x in inputs))


def prepare_kernel(bits, top_ref, ids_ref, count_ref, table_ref, a_ref):
    slots, docs = ids_ref.shape
    head, width = top_ref.shape
    top = width // LANES * head
    for j in range(width // LANES):
        a_ref[j * head : (j + 1) * head, :] = top_ref[:, j * LANES : (j + 1) * LANES]
    pairs = table_ref.shape[0] // 2
    starts = range(0, docs, LANES)
    ids = [ids_ref[:, start : start + LANES] for start in starts]
    line_of = [(chunk >> 7) & (pairs - 1) for chunk in ids]
    lane_of = [chunk & (LANES - 1) for chunk in ids]

    def pick(t, found):
        both = table_ref[pl.ds(t, 1), :] | (table_ref[pl.ds(t + pairs, 1), :] << 16)
        line = jnp.broadcast_to(both, (slots, LANES))
        return tuple(
            jnp.where(line_of[i] == t, jnp.take_along_axis(line, lane_of[i], axis=1), found[i])
            for i in range(len(ids))
        )

    found = tuple(jnp.zeros((slots, LANES), jnp.int32) for _ in ids)
    if pairs <= 16:
        for t in range(pairs):
            found = pick(t, found)
    else:
        found = lax.fori_loop(0, pairs, pick, found, unroll=8)
    place = lax.broadcasted_iota(jnp.int32, (slots, LANES), 0)
    for i, start in enumerate(starts):
        row = jnp.where((ids[i] >> 7) < pairs, found[i], found[i] >> 16) & 0xFFFF
        low = (LANES + (row & (LANES - 1))).astype(jnp.float32)
        code = power_of_two(row >> 7, bits, low * 2.0**-64, 1)
        code = jnp.where(place < count_ref[:, start : start + LANES], code, 0.0)
        first = top + i * slots
        a_ref[first : first + slots, :] = code.astype(jnp.bfloat16)


def prepare(top, ids, count, table):
    slots, docs = ids.shape
    vmem = pl.BlockSpec(memory_space=pltpu.VMEM)
    return pl.pallas_call(
        functools.partial(prepare_kernel, (table.shape[0] - 1).bit_length()),
        in_specs=[vmem] * 4,
        out_specs=vmem,
        out_shape=jax.ShapeDtypeStruct(((top.size + slots * docs) // LANES, LANES), jnp.bfloat16),
        compiler_params=pltpu.CompilerParams(vmem_limit_bytes=VMEM_LIMIT),
        name="prepare",
    )(top, ids, count, table)


def cast_kernel(weights_ref, cast_ref):
    cast_ref[...] = weights_ref[...].astype(jnp.bfloat16) * 0.5


def halved_cast(weights):
    return pl.pallas_call(
        cast_kernel,
        in_specs=[pl.BlockSpec(memory_space=pltpu.VMEM)],
        out_specs=pl.BlockSpec(memory_space=pltpu.VMEM),
        out_shape=jax.ShapeDtypeStruct(weights.shape, jnp.bfloat16),
        compiler_params=pltpu.CompilerParams(vmem_limit_bytes=VMEM_LIMIT),
        name="cast",
    )(weights)


def signs_of(codes, owner, bits, height):
    docs = codes.shape[1]
    scale = power_of_two(owner * (height // LANES), bits, jnp.float32(2.0**64), -1)
    scaled = codes * scale
    place = jnp.left_shift(
        jnp.ones((WORD, docs), jnp.int32), lax.broadcasted_iota(jnp.int32, (WORD, docs), 0)
    )
    spread = []
    for part in range(height // LANES):
        row = jnp.minimum(scaled * 2.0**-part, 512.0).astype(jnp.int32) - LANES
        word = row >> 5
        bit = jnp.left_shift(jnp.ones_like(row), row & (WORD - 1))
        for w in range(LANES // WORD):
            line = jnp.sum(jnp.where(word == w, bit, 0), axis=0, keepdims=True)
            line = jnp.broadcast_to(line, (WORD, docs))
            spread.append(jnp.where((line & place) != 0, -1.0, 1.0))
    return jnp.concatenate(spread, axis=0)


def doubled_gradient(bits, owners, a_ref, b_ref, w_refs):
    height = w_refs[0].shape[0]
    head, width = b_ref.shape
    tiles = width // LANES
    chunks = 2 * head // LANES
    slots = (a_ref.shape[0] - tiles * head) // chunks
    top = jnp.concatenate([a_ref[j * head : (j + 1) * head, :] for j in range(tiles)], axis=1)
    docs = jnp.concatenate([top, b_ref[...]], axis=0)
    starts = [tiles * head + i * slots for i in range(chunks)]
    codes = jnp.concatenate([a_ref[start : start + slots, :] for start in starts], axis=1)
    codes = codes.astype(jnp.float32)
    weights = jnp.concatenate([ref[...] for ref in w_refs], axis=0)
    halved = lax.dot_general(
        weights, docs, (((1,), (1,)), ((), ())), preferred_element_type=jnp.float32
    )
    me = lax.axis_index("blk")
    signs = jnp.concatenate([signs_of(codes, me ^ owner, bits, height) for owner in owners], axis=0)
    signal = (jnp.tanh(halved) + signs).astype(jnp.bfloat16)
    return jnp.dot(signal, docs, preferred_element_type=jnp.float32)


def gradient_kernel(bits, owners, fresh, a_ref, b_ref, *refs):
    blocks = len(owners)
    w_refs, refs = refs[:blocks], refs[blocks:]
    old_refs, new_refs = refs[:-blocks], refs[-blocks:]
    height = w_refs[0].shape[0]
    part = doubled_gradient(bits, owners, a_ref, b_ref, w_refs)
    for block in range(blocks):
        piece = part[block * height : (block + 1) * height]
        new_refs[block][...] = piece if fresh else old_refs[block][...] + piece


def add_gradient(bits, owners, a, b, weights, sums, flops):
    blocks = len(weights)
    height, width = weights[0].shape
    vmem = pl.BlockSpec(memory_space=pltpu.VMEM)
    sums = list(sums)
    inputs = [a, b, *weights, *sums]
    first_sum = len(inputs) - len(sums)
    return pl.pallas_call(
        functools.partial(gradient_kernel, bits, owners, not sums),
        in_specs=[vmem] * len(inputs),
        out_specs=[vmem] * blocks,
        out_shape=[jax.ShapeDtypeStruct((height, width), jnp.float32)] * blocks,
        input_output_aliases={first_sum + i: i for i in range(len(sums))},
        compiler_params=pltpu.CompilerParams(vmem_limit_bytes=VMEM_LIMIT),
        cost_estimate=pl.CostEstimate(flops=flops, bytes_accessed=10**6, transcendentals=0),
        name="gradient",
    )(*inputs)


def finish_kernel(
    bits,
    a_ref,
    b_ref,
    cast_ref,
    sum_ref,
    other_ref,
    weights_ref,
    first_ref,
    second_ref,
    weights_hbm,
    first_hbm,
    second_hbm,
    weights_out,
    first_out,
    second_out,
    done,
):
    part = doubled_gradient(bits, (0,), a_ref, b_ref, [cast_ref])
    height = part.shape[0]
    size = height // PIECES
    writes = []
    for i in range(PIECES):
        here = pl.ds(i * size, size)
        doubled = sum_ref[here, :] + other_ref[here, :] + part[i * size : (i + 1) * size]
        new_weights, new_first, new_second = adam_step(
            weights_ref[here, :], first_ref[here, :], second_ref[here, :], doubled
        )
        for k, (value, out, hbm) in enumerate(
            (
                (new_first, first_out, first_hbm),
                (new_second, second_out, second_hbm),
                (new_weights, weights_out, weights_hbm),
            )
        ):
            out[here, :] = value
            write = pltpu.make_async_copy(out.at[here], hbm.at[here], done.at[i, k])
            write.start()
            writes.append(write)
    for write in writes:
        write.wait()


def finish(bits, a, b, cast, mine_sum, other_sum, weights, first_moment, second_moment):
    shape = jax.ShapeDtypeStruct(weights.shape, jnp.float32)
    return pl.pallas_call(
        functools.partial(finish_kernel, bits),
        in_specs=[pl.BlockSpec(memory_space=pltpu.VMEM)] * 8,
        out_specs=[pl.BlockSpec(memory_space=pltpu.HBM)] * 3,
        out_shape=[shape] * 3,
        scratch_shapes=[pltpu.VMEM(weights.shape, jnp.float32)] * 3
        + [pltpu.SemaphoreType.DMA((PIECES, 3))],
        compiler_params=pltpu.CompilerParams(vmem_limit_bytes=VMEM_LIMIT),
        cost_estimate=pl.CostEstimate(flops=END_FLOPS, bytes_accessed=10**6, transcendentals=0),
        name="finish",
    )(a, b, cast, mine_sum, other_sum, weights, first_moment, second_moment)


def adam_step(weights, first_moment, second_moment, doubled):
    new_first = beta_one * first_moment + ((1.0 - beta_one) * 0.5) * doubled
    new_second = beta_two * second_moment + ((1.0 - beta_two) * 0.25) * (doubled * doubled)
    steep = correct_one / (learn_rate * math.sqrt(correct_two))
    update = new_first / (jnp.sqrt(new_second) * steep + correct_one * adam_eps / learn_rate)
    new_weights = weights * (1.0 - learn_rate * decay_rate) - update
    return (new_weights, new_first, new_second)


def ring_of(blocks, across):
    path = list(range(0, blocks // 2, across))
    if across == 2:
        path += list(range(1, blocks // 2, 2))[::-1]
    pairs = []
    for here, there in zip(path, path[1:] + path[:1]):
        pairs += [(2 * here, 2 * there), (2 * there + 1, 2 * here + 1)]
    return pairs


together = lax.optimization_barrier


def per_device(
    blocks,
    across,
    embeddings,
    pos_ids,
    pos_count,
    label_slot,
    weights,
    first_moment,
    second_moment,
):
    half_way = blocks // 4
    up = ring_of(blocks, across)
    down = [(there, here) for here, there in up]
    swap = [(i, i ^ 1) for i in range(blocks)]
    bits = (label_slot.shape[0] // LANES - 1).bit_length()
    head = embeddings.shape[0] // 2

    def send(value, pairs):
        return lax.ppermute(value, "blk", pairs)

    b, *rest = fetch(label_slot, pos_ids, pos_count, embeddings, head)
    coming = {"up_b": send(b, up)}
    a = prepare(*rest)
    coming["down_a"] = send(a, down)
    coming |= {"up_a": send(a, up), "down_b": send(b, down)}
    mine = halved_cast(weights)
    cast = [mine, send(mine, swap)]
    sums = ()
    waiting = [(a, b)]

    def work(flops):
        return add_gradient(bits, (0, 1), *waiting.pop(0), cast, sums, flops)

    for step in range(1, half_way):
        last = step == half_way - 1
        came = {}
        for message in ("up_b", "down_a", "up_a", "down_b"):
            came[message], waiting, sums = together((coming.pop(message), waiting, sums))
            if message in ("up_b", "down_a") or not last:
                coming[message] = send(came[message], up if message in ("up_a", "up_b") else down)
            if message in ("up_a", "down_b"):
                side = message.split("_")[0]
                waiting.append((came[side + "_a"], came[side + "_b"]))
            if last:
                number = {"down_a": 2, "down_b": 0}.get(message, 1)
            else:
                number = 1 if step > 1 and message in ("down_a", "up_a") else 0
            for _ in range(min(number, len(waiting))):
                sums = work(LATE_FLOPS if last else FLOPS)
    while len(waiting) > 1:
        sums = work(LATE_FLOPS)
    docs = waiting.pop()
    (other_sum,) = add_gradient(bits, (1,), *docs, cast[1:], sums[1:], LATE_FLOPS)
    got = send(other_sum, swap)
    (mine_sum,) = add_gradient(bits, (0,), *docs, cast[:1], sums[:1], LATE_FLOPS)
    last_a, mine_sum = together((coming["down_a"], mine_sum))
    beside_a = send(last_a, swap)
    last_b, mine_sum = together((coming["up_b"], mine_sum))
    beside_b = send(last_b, swap)
    (mine_sum,) = add_gradient(bits, (0,), last_a, last_b, [mine], [mine_sum], END_FLOPS)
    state = (weights, first_moment, second_moment)
    return finish(bits, beside_a, beside_b, mine, mine_sum, got, *state)


def solution(mesh):
    in_specs = (
        P(("groups", "blk"), None),
        P(("groups", "blk"), None),
        P(("groups", "blk")),
        P(),
        P("blk", None),
        P("blk", None),
        P("blk", None),
    )
    out_specs = (P(("groups", "blk"), None), P(("groups", "blk"), None), P(("groups", "blk"), None))
    return jax.shard_map(
        functools.partial(per_device, mesh.shape["blk"], 4 // mesh.shape["groups"]),
        mesh=mesh,
        in_specs=in_specs,
        out_specs=out_specs,
        check_vma=False,
    )
```
